32 devices in a mesh: row: 8 (over y, x, core), col: 4 (over z).
Axes of the slice: x: 2, y: 2, z: 4, core: 2. Of those that a mesh axis runs over, the one named last changes fastest.
Arguments:
- atom_types: int32 [32, 256], P(('row', 'col')), may hold values from 0 to 3
- neighbor_ids: int32 [32, 32, 256], P(('row', 'col')), may hold values from 0 to 255
- switching: float32 [32, 32, 256], P(('row', 'col')), may hold values from 0.1 to 1
- environment: float32 [32, 256, 64], P(('row', 'col')), may hold values from -6 to 6
- force_weights: float32 [32, 256], P(('row', 'col')), may hold values from -1 to 1
- targets: float32 [32], P(('row', 'col')), may hold values from -6 to 6
- type_embed: float32 [4, 64], replicated, may hold values from -8 to 8, as said below
- layer_weight: float32 [64, 128], replicated, may hold values from -1 to 1
- out_weight: float32 [128], replicated, may hold values from -0.5 to 0.5
- covariance: float32 [8192, 8192], P('row', 'col'), as said below
Outputs:
- new_weight: float32 [8192], P(('row', 'col'))
- new_cov: float32 [8192, 8192], P('row', 'col')
The draws below stay inside these ranges and needn't reach their ends.
Inputs may be any that keep to these rules, and one draw needn't show every extreme that they name: `neighbor_ids`: indices of atoms of the same configuration. `covariance`: symmetric positive definite. `type_embed`: each feature sums to zero over the 4 types.
All inputs are finite; a program needn't handle non-finite values. Where the reference program divides by a largest or mean magnitude, that divisor is 1e-20 or more.
Results may differ from the reference program's by a relative error of at most 0.0003.
Values sent between devices are 32-bit elements; how exact they have to be, the bound alone decides.
No kernel may reach another device: no remote copies, remote signals or barrier semaphores. Data moves between devices by JAX's collectives and lax.ppermute only.
A program may use at most 64 MiB of HBM per device.

```python
import math
import jax
import jax.numpy as jnp
from jax import lax

H = 128
HIN = 64
TYPES = 4
NBR = 32
NEWTON = 4
ATOMS = 256
NPARAM = 8192
STREAMS = 32


def draw_covariance(key, part):
    keys = jax.random.split(jax.random.fold_in(key, 11), 5)
    noise = jax.random.normal(keys[0], (NPARAM, NPARAM), jnp.float32)
    symmetric = (noise + noise.T) * (0.3 / math.sqrt(NPARAM))
    diagonal = jax.random.uniform(keys[1], (NPARAM,), jnp.float32, 1.0, 2.0)
    input_factor = jax.random.normal(keys[3], (HIN, HIN), jnp.float32)
    output_factor = jax.random.normal(keys[4], (H, H), jnp.float32)
    input_corr = jnp.dot(input_factor, input_factor.T, precision=jax.lax.Precision.HIGHEST) / HIN
    output_corr = jnp.dot(output_factor, output_factor.T, precision=jax.lax.Precision.HIGHEST) / H
    coupled = (input_corr[:, None, :, None] * output_corr[None, :, None, :]).reshape(NPARAM, NPARAM)
    matrix = symmetric + jnp.diag(diagonal) + coupled
    return matrix


def draw_environment(key, part):
    inner = jax.random.fold_in(key, 23)
    values = jnp.clip(jax.random.normal(inner, (STREAMS, ATOMS, HIN), jnp.float32), -6.0, 6.0)
    return values


def draw_force_weights(key, part):
    inner = jax.random.fold_in(key, 37)
    values = jax.random.uniform(inner, (STREAMS, ATOMS), jnp.float32, -1.0, 1.0)
    return values


def draw_type_embed(key, part):
    inner = jax.random.fold_in(key, 41)
    values = jnp.clip(jax.random.normal(inner, (TYPES, HIN), jnp.float32), -4.0, 4.0)
    return values - jnp.mean(values, axis=0, keepdims=True)


def draw_layer_weight(key, part):
    inner = jax.random.fold_in(key, 53)
    spread = 3.0 / math.sqrt(HIN)
    values = jax.random.normal(inner, (HIN, H), jnp.float32) * spread
    return jnp.clip(values, -1.0, 1.0)


def with_ends(result, key, low, high):
    spot = [jax.random.randint(jax.random.fold_in(key, axis), (), 0, length) for axis, length in enumerate(result.shape)]
    widest = result.shape.index(max(result.shape))
    neighbour = spot[:widest] + [(spot[widest] + 1) % result.shape[widest]] + spot[widest + 1:]
    return result.at[tuple(spot)].set(low).at[tuple(neighbour)].set(high)


def level_of(own_key, shape, pieces, low, largest):
    factor_of, own = 1.0, jax.random.fold_in(own_key, 6)
    for axis_at, parts in pieces:
        draws = jnp.exp(jax.random.uniform(jax.random.fold_in(own, axis_at), (parts,), jnp.float32, low / len(pieces), largest / len(pieces)))
        factor_of = factor_of * jnp.repeat(draws, shape[axis_at] // parts).reshape([-1 if axis == axis_at else 1 for axis in range(len(shape))])
    return factor_of


def scatter_about(stream_key, shape, scale, limit, cuts=(), kind=jnp.bfloat16):
    level = level_of(stream_key, shape, cuts, -0.22, 0.18) if cuts else 1.0
    result = jax.random.normal(stream_key, shape, jnp.float32) * scale * level
    return jnp.minimum(jnp.maximum(result, -limit), limit).astype(kind)


def setup_inputs(seed: int = 0) -> dict:
    seeds = jax.random.split(jax.random.key(seed), 11)
    atom_types = with_ends(jax.random.randint(seeds[0], (STREAMS, ATOMS), 0, TYPES), jax.random.fold_in(seeds[0], 1), 0, TYPES - 1).astype(jnp.int32)
    neighbor_ids = with_ends(jax.random.randint(seeds[1], (STREAMS, NBR, ATOMS), 0, ATOMS), jax.random.fold_in(seeds[1], 1), 0, ATOMS - 1).astype(jnp.int32)
    switching = jnp.clip(0.1 + 0.9 * jax.random.uniform(seeds[2], (STREAMS, NBR, ATOMS), jnp.float32) ** level_of(seeds[2], (STREAMS, NBR, ATOMS), ((0, 32),), -0.2, 0.2), 0.1, 1.0)
    environment = draw_environment(jax.random.fold_in(seeds[10], 71), 0)
    force_weights = draw_force_weights(jax.random.fold_in(seeds[10], 71), 0)
    targets = scatter_about(seeds[5], (STREAMS,), 1.0, 6.0, ((0, 32),), jnp.float32)
    type_embed = draw_type_embed(jax.random.fold_in(seeds[10], 71), 0)
    layer_weight = draw_layer_weight(jax.random.fold_in(seeds[10], 71), 0)
    out_weight = scatter_about(seeds[8], (H,), H ** -0.5, 0.5, (), jnp.float32)
    covariance = draw_covariance(jax.random.fold_in(seeds[10], 71), 0)
    return dict(atom_types=atom_types, neighbor_ids=neighbor_ids, switching=switching, environment=environment, force_weights=force_weights, targets=targets, type_embed=type_embed, layer_weight=layer_weight, out_weight=out_weight, covariance=covariance)


forget = 0.98
highest = lax.Precision.HIGHEST

def network(atom_types, neighbor_ids, switching, environment, force_weights, type_embed, layer_weight, out_weight):
    type_ids = jnp.arange(type_embed.shape[0], dtype=jnp.int32)
    onehot = (atom_types[:, None] == type_ids[None, :]).astype(jnp.float32)
    mixed = environment + jnp.dot(onehot, type_embed, precision=highest)
    nearby = jnp.take(mixed, neighbor_ids, axis=0)
    descriptor = lax.optimization_barrier(jnp.sum(switching[:, :, None] * nearby, axis=0)) / math.sqrt(neighbor_ids.shape[0])
    hidden = jnp.tanh(descriptor)
    activity = jnp.tanh(jnp.dot(hidden, layer_weight, precision=highest))
    energy = jnp.dot(activity, out_weight, precision=highest)
    atom_scale = 1.0 / math.sqrt(energy.shape[0])
    predicted = jnp.sum(force_weights * energy) * atom_scale
    slopes = out_weight[None, :] * (1.0 - activity * activity)
    jacobian = jnp.dot((force_weights[:, None] * hidden).T, slopes, precision=highest) * atom_scale
    return (predicted, jacobian.reshape(-1))

def first_inverse(innovation):
    identity = jnp.eye(innovation.shape[0], dtype=jnp.float32)
    row_bound = jnp.max(lax.optimization_barrier(jnp.sum(jnp.abs(innovation), axis=1)))
    return identity * (2.0 / row_bound) - innovation / (row_bound * row_bound)

def reference(atom_types, neighbor_ids, switching, environment, force_weights, targets, type_embed, layer_weight, out_weight, covariance):

    def single(inputs):
        return network(inputs[0], inputs[1], inputs[2], inputs[3], inputs[4], type_embed, layer_weight, out_weight)
    predicted, jacobian = lax.map(single, (atom_types, neighbor_ids, switching, environment, force_weights))
    errors = targets - predicted
    cross = jnp.dot(covariance, jacobian.T, precision=highest)
    identity = jnp.eye(jacobian.shape[0], dtype=jnp.float32)
    innovation = jnp.dot(jacobian, cross, precision=highest) + forget * identity
    inverse = first_inverse(innovation)
    for repeat in range(NEWTON - 1):
        inverse = 2.0 * inverse - jnp.dot(jnp.dot(inverse, innovation, precision=highest), inverse, precision=highest)
    gain = jnp.dot(cross, inverse, precision=highest)
    new_weight = layer_weight.reshape(-1) + jnp.dot(gain, errors, precision=highest)
    new_cov = (covariance - jnp.dot(gain, cross.T, precision=highest)) / forget
    return (new_weight, new_cov)
```

```python
import functools
import math

import jax
import jax.numpy as jnp
from jax import lax
from jax.experimental import pallas as pl
from jax.experimental.pallas import tpu as pltpu
from jax.sharding import PartitionSpec as P

NEWTON = 4
LANES = 128
SUBLANES = 8


forget = 0.98
highest = lax.Precision.HIGHEST
f32 = jnp.float32
bf16 = jnp.bfloat16


def dot(left, right, contract, precision=None):
    return lax.dot_general(
        left, right, (contract, ((), ())), precision=precision, preferred_element_type=f32
    )


def split3(x):
    hi = x.astype(bf16)
    rest = x - hi.astype(f32)
    mid = rest.astype(bf16)
    lo = (rest - mid.astype(f32)).astype(bf16)
    return hi, mid, lo


def split2(x):
    hi = x.astype(bf16)
    return hi, (x - hi.astype(f32)).astype(bf16)


def network_kernel(
    types_ref,
    ids_ref,
    switch_ref,
    env_ref,
    force_ref,
    target_ref,
    embed_ref,
    weight_ref,
    out_weight_ref,
    payload_ref,
    mix_ref,
):
    neighbours, atoms = ids_ref.shape
    hin, _ = weight_ref.shape
    n_types = embed_ref.shape[0]
    height = min(64, atoms)
    for start in range(0, atoms, height):
        atom_at = lax.broadcasted_iota(jnp.int32, (height, atoms), 0) + start
        total = jnp.zeros((height, atoms), f32)
        for k in range(neighbours):
            total = total + jnp.where(ids_ref[k : k + 1, :] == atom_at, switch_ref[k : k + 1, :], 0.0)
        mix_ref[start : start + height, :] = total
    mix = mix_ref[...]
    type_at = lax.broadcasted_iota(jnp.int32, (n_types, atoms), 0)
    onehot = (types_ref[...] == type_at).astype(f32)
    mixed = env_ref[...] + dot(onehot, embed_ref[...], ((0,), (0,)), highest)
    descriptor = dot(mixed, mix, ((0,), (0,)), highest) * (1.0 / math.sqrt(neighbours))
    hidden = jnp.tanh(descriptor)
    activity = jnp.tanh(dot(hidden, weight_ref[...], ((0,), (0,)), highest))
    out_weight = out_weight_ref[...]
    scale = 1.0 / math.sqrt(atoms)
    force = force_ref[...]
    weighted = dot(force, activity, ((1,), (0,)), highest)
    predicted = jnp.sum(weighted * out_weight, axis=1, keepdims=True) * scale
    slopes = out_weight * (1.0 - activity * activity)
    jacobian = dot(hidden * force, slopes, ((1,), (0,)), highest) * scale
    payload_ref[0:hin, :] = jacobian
    error = target_ref[...] - predicted
    payload_ref[hin:, :] = jnp.broadcast_to(error, (SUBLANES, jacobian.shape[1]))


def network(atom_types, neighbor_ids, switching, environment, force_weights, targets, type_embed, layer_weight, out_weight):
    per_dev, neighbours, atoms = neighbor_ids.shape
    hin, width = layer_weight.shape

    def per_stream(*shape):
        return pl.BlockSpec((None,) + shape, lambda s: (s,) + (0,) * len(shape))

    def shared(shape):
        return pl.BlockSpec(shape, lambda s: (0,) * len(shape))

    return pl.pallas_call(
        network_kernel,
        grid=(per_dev,),
        in_specs=[
            per_stream(1, atoms),
            per_stream(neighbours, atoms),
            per_stream(neighbours, atoms),
            per_stream(atoms, hin),
            per_stream(1, atoms),
            per_stream(1, 1),
            shared(type_embed.shape),
            shared(layer_weight.shape),
            shared((1, width)),
        ],
        out_specs=per_stream(hin + SUBLANES, width),
        out_shape=jax.ShapeDtypeStruct((per_dev, hin + SUBLANES, width), f32),
        scratch_shapes=[pltpu.VMEM((atoms, atoms), f32)],
        name="network",
    )(
        atom_types.reshape(per_dev, 1, atoms),
        neighbor_ids,
        switching,
        environment,
        force_weights.reshape(per_dev, 1, atoms),
        targets.reshape(per_dev, 1, 1),
        type_embed,
        layer_weight,
        out_weight.reshape(1, width),
    )


def cross_kernel(at_ref, jac_ref, cov_ref, cross_ref, parts_ref):
    streams, rows, lanes = jac_ref.shape

    @pl.when(pl.program_id(0) == 0)
    def _():
        flat = jac_ref.reshape(streams * rows, lanes)
        for i in range(rows):
            parts = split3(flat[pl.ds(i, streams, stride=rows), :])
            for n, part in enumerate(parts):
                parts_ref[n * streams : (n + 1) * streams, i * lanes : (i + 1) * lanes] = part

    hi, lo = split2(cov_ref[...])
    by_hi = dot(parts_ref[...], hi, ((1,), (1,)))
    by_lo = dot(parts_ref[0 : 2 * streams, :], lo, ((1,), (1,)))
    cross_ref[...] = by_hi[0:streams] + (
        by_hi[streams : 2 * streams]
        + by_lo[0:streams]
        + (by_hi[2 * streams :] + by_lo[streams:])
    )


def cross_partial(at, jac_all, covariance, slab):
    streams = jac_all.shape[0]
    tile_rows, tile_cols = covariance.shape
    jac_rows = tile_cols // LANES
    slabs = tile_rows // slab
    return pl.pallas_call(
        cross_kernel,
        grid_spec=pltpu.PrefetchScalarGridSpec(
            num_scalar_prefetch=1,
            grid=(slabs,),
            in_specs=[
                pl.BlockSpec((streams, jac_rows, LANES), lambda n, at: (0, at[1], 0)),
                pl.BlockSpec((slab, tile_cols), lambda n, at: (n, 0)),
            ],
            out_specs=pl.BlockSpec((None, streams, slab), lambda n, at: (n, 0, 0)),
            scratch_shapes=[pltpu.VMEM((3 * streams, tile_cols), bf16)],
        ),
        out_shape=jax.ShapeDtypeStruct((slabs, streams, slab), f32),
        compiler_params=pltpu.CompilerParams(vmem_limit_bytes=40 << 20),
        name="cross",
    )(at, jac_all, covariance)


def slab_kernel(at_ref, pieces_ref, jac_ref, out_ref, *, cols_n):
    pieces, streams, slab = pieces_ref.shape
    _, group, lanes = jac_ref.shape
    cross = pieces_ref[0]
    for n in range(1, pieces):
        cross = cross + pieces_ref[n]
    out_ref[:, 0:slab] = cross
    rows = slab // lanes
    first = ((at_ref[0] * cols_n + at_ref[1]) * rows) % group
    flat = jac_ref.reshape(streams * group, lanes)
    term = jnp.zeros((streams, streams), f32)
    for i in range(rows):
        own = flat[pl.ds(first + i, streams, stride=group), :]
        term = term + dot(own, cross[:, i * lanes : (i + 1) * lanes], ((1,), (1,)), highest)
    out_ref[:, slab:] = jnp.concatenate(
        [term, jnp.zeros((streams, out_ref.shape[1] - slab - streams), f32)], axis=1
    )


def slab_sum(at, pieces, jac_all, cols_n):
    count, streams, slab = pieces.shape
    rows = slab // LANES
    group = SUBLANES
    padded = slab + pl.cdiv(streams, LANES) * LANES
    return pl.pallas_call(
        functools.partial(slab_kernel, cols_n=cols_n),
        grid_spec=pltpu.PrefetchScalarGridSpec(
            num_scalar_prefetch=1,
            grid=(1,),
            in_specs=[
                pl.BlockSpec(pieces.shape, lambda n, at: (0, 0, 0)),
                pl.BlockSpec(
                    (streams, group, LANES),
                    lambda n, at: (0, (at[0] * cols_n + at[1]) * rows // group, 0),
                ),
            ],
            out_specs=pl.BlockSpec((streams, padded), lambda n, at: (0, 0)),
        ),
        out_shape=jax.ShapeDtypeStruct((streams, padded), f32),
        name="slab",
    )(at, pieces, jac_all)


def invert(innovation):
    streams = innovation.shape[0]
    row = lax.broadcasted_iota(jnp.int32, (streams, streams), 0)
    col = lax.broadcasted_iota(jnp.int32, (streams, streams), 1)
    identity = (row == col).astype(f32)
    innovation = innovation + forget * identity
    sums = jnp.sum(jnp.abs(innovation), axis=1, keepdims=True)
    bound = jnp.max(sums, axis=0, keepdims=True)
    inverse = identity * (2.0 / bound) - innovation / (bound * bound)
    for repeat in range(NEWTON - 1):
        step = dot(inverse, innovation, ((1,), (0,)), highest)
        inverse = 2.0 * inverse - dot(step, inverse, ((1,), (0,)), highest)
    return inverse


def update_kernel(
    at_ref, terms_ref, rows_ref, cols_ref, error_ref, weight_ref, cov_ref, new_weight_ref, new_cov_ref, gain_ref, right_ref
):
    devices, streams, _ = terms_ref.shape
    slabs, _, _ = rows_ref.shape
    slab = cov_ref.shape[0]
    step = pl.program_id(0)

    @pl.when(step == 0)
    def _():
        innovation = terms_ref[0, :, 0:streams]
        for n in range(1, devices):
            innovation = innovation + terms_ref[n, :, 0:streams]
        inverse = invert(innovation)
        for n in range(slabs):
            gain_ref[n] = dot(inverse, rows_ref[n, :, 0:slab], ((0,), (0,)), highest)
        for n in range(cols_ref.shape[0]):
            hi, mid, lo = split3(cols_ref[n, :, 0:slab])
            for m, part in enumerate((hi, mid, lo, hi, mid, hi)):
                right_ref[m * streams : (m + 1) * streams, n * slab : (n + 1) * slab] = part

    gain = gain_ref[step]
    hi, mid, lo = split3(gain)
    left = jnp.concatenate([hi, hi, hi, mid, mid, lo], axis=0)
    update = dot(left, right_ref[...], ((0,), (0,)))
    new_cov_ref[...] = (cov_ref[...] - update) * (1.0 / forget)

    @pl.when(step == at_ref[1])
    def _():
        group = error_ref.shape[1]
        lanes = error_ref.shape[2]
        errors = error_ref.reshape(streams * group, lanes)[pl.ds(0, streams, stride=group), :]
        for i in range(slab // lanes):
            moved = jnp.sum(gain[:, i * lanes : (i + 1) * lanes] * errors, axis=0, keepdims=True)
            own = weight_ref[pl.ds((at_ref[0] * slabs + at_ref[1]) * (slab // lanes) + i, 1), :]
            new_weight_ref[i : i + 1, :] = own + moved


def update(at, gathered, jac_all, layer_weight, covariance, slab):
    devices, streams, padded = gathered.shape
    tile_rows, tile_cols = covariance.shape
    hin, width = layer_weight.shape
    slabs = tile_rows // slab
    return pl.pallas_call(
        update_kernel,
        grid_spec=pltpu.PrefetchScalarGridSpec(
            num_scalar_prefetch=1,
            grid=(slabs,),
            in_specs=[
                pl.BlockSpec((devices, streams, LANES), lambda n, at: (0, 0, slab // LANES)),
                pl.BlockSpec((slabs, streams, padded), lambda n, at: (at[0], 0, 0)),
                pl.BlockSpec((tile_cols // slab, streams, padded), lambda n, at: (at[1], 0, 0)),
                pl.BlockSpec((streams, SUBLANES, width), lambda n, at: (0, hin // SUBLANES, 0)),
                pl.BlockSpec((hin, width), lambda n, at: (0, 0)),
                pl.BlockSpec((slab, tile_cols), lambda n, at: (n, 0)),
            ],
            out_specs=[
                pl.BlockSpec((slab // width, width), lambda n, at: (0, 0)),
                pl.BlockSpec((slab, tile_cols), lambda n, at: (n, 0)),
            ],
            scratch_shapes=[
                pltpu.VMEM((slabs, streams, slab), f32),
                pltpu.VMEM((6 * streams, tile_cols), bf16),
            ],
        ),
        out_shape=[
            jax.ShapeDtypeStruct((slab // width, width), f32),
            jax.ShapeDtypeStruct((tile_rows, tile_cols), f32),
        ],
        compiler_params=pltpu.CompilerParams(vmem_limit_bytes=48 << 20),
        name="update",
    )(at, gathered, gathered, gathered, jac_all, layer_weight, covariance)


def plain_steps(at, jac_all, layer_weight, covariance, slab, cols_n):
    streams = jac_all.shape[0]
    hin, width = layer_weight.shape
    tile_rows, tile_cols = covariance.shape
    first = (at[0] * cols_n + at[1]) * slab
    jacobian = jac_all[:, 0:hin, :].reshape(streams, hin * width)
    errors = jac_all[:, hin, 0]
    jac_cols = lax.dynamic_slice_in_dim(jacobian, at[1] * tile_cols, tile_cols, 1)
    partial = dot(jac_cols, covariance, ((1,), (1,)), highest)
    cross_own = lax.psum_scatter(partial, "col", scatter_dimension=1, tiled=True)
    cross = lax.all_gather(cross_own, ("row", "col"), axis=1, tiled=True)
    inverse = invert(dot(jacobian, cross, ((1,), (1,)), highest))
    gain = dot(inverse, lax.dynamic_slice_in_dim(cross, at[0] * tile_rows, tile_rows, 1), ((0,), (0,)), highest)
    across = lax.dynamic_slice_in_dim(cross, at[1] * tile_cols, tile_cols, 1)
    new_cov = (covariance - dot(gain, across, ((0,), (0,)), highest)) / forget
    own_gain = lax.dynamic_slice_in_dim(gain, at[1] * slab, slab, 1)
    own_weight = lax.dynamic_slice_in_dim(layer_weight.reshape(-1), first, slab, 0)
    new_weight = own_weight + dot(errors, own_gain, ((0,), (0,)), highest)
    return new_weight, new_cov


def on_device(
    atom_types,
    neighbor_ids,
    switching,
    environment,
    force_weights,
    targets,
    type_embed,
    layer_weight,
    out_weight,
    covariance,
):
    rows_n = lax.axis_size("row")
    cols_n = lax.axis_size("col")
    at = jnp.stack([lax.axis_index("row"), lax.axis_index("col")]).astype(jnp.int32)
    tile_rows, tile_cols = covariance.shape
    slab = tile_rows // cols_n
    payload = network(
        atom_types,
        neighbor_ids,
        switching,
        environment,
        force_weights,
        targets,
        type_embed,
        layer_weight,
        out_weight,
    )
    jac_all = lax.all_gather(payload, ("row", "col"), axis=0, tiled=True)
    slab_rows = slab // LANES
    if slab % LANES or SUBLANES % slab_rows or layer_weight.shape[1] != LANES or tile_cols % (SUBLANES * LANES):
        return plain_steps(at, jac_all, layer_weight, covariance, slab, cols_n)
    partial = cross_partial(at, jac_all, covariance, slab)
    pieces = lax.all_to_all(partial, "col", split_axis=0, concat_axis=0, tiled=True)
    own = slab_sum(at, pieces, jac_all, cols_n)
    gathered = lax.all_gather(own, ("row", "col"), axis=0, tiled=False)
    new_weight, new_cov = update(at, gathered, jac_all, layer_weight, covariance, slab)
    return new_weight.reshape(-1), new_cov


def solution(mesh):
    in_specs = (
        P(("row", "col"), None),
        P(("row", "col"), None, None),
        P(("row", "col"), None, None),
        P(("row", "col"), None, None),
        P(("row", "col"), None),
        P(("row", "col")),
        P(),
        P(),
        P(),
        P("row", "col"),
    )
    out_specs = (P(("row", "col")), P("row", "col"))
    return jax.shard_map(
        on_device, mesh=mesh, in_specs=in_specs, out_specs=out_specs, check_vma=False
    )
```

```python
import functools
import math

import jax
import jax.numpy as jnp
from jax import lax
from jax.experimental import pallas as pl
from jax.experimental.pallas import tpu as pltpu
from jax.sharding import PartitionSpec as P

NEWTON = 4
LANES = 128
SUBLANES = 8


forget = 0.98
highest = lax.Precision.HIGHEST
f32 = jnp.float32
bf16 = jnp.bfloat16


def dot(left, right, contract, precision=None):
    return lax.dot_general(
        left, right, (contract, ((), ())), precision=precision, preferred_element_type=f32
    )


def split3(x):
    hi = x.astype(bf16)
    rest = x - hi.astype(f32)
    mid = rest.astype(bf16)
    lo = (rest - mid.astype(f32)).astype(bf16)
    return hi, mid, lo


def split2(x):
    hi = x.astype(bf16)
    return hi, (x - hi.astype(f32)).astype(bf16)


def network_kernel(
    types_ref,
    ids_ref,
    switch_ref,
    env_ref,
    force_ref,
    target_ref,
    embed_ref,
    weight_ref,
    out_weight_ref,
    payload_ref,
    mix_ref,
    *,
    plan,
):
    neighbours, atoms = ids_ref.shape
    n_types = embed_ref.shape[0]
    height = min(64, atoms)
    for start in range(0, atoms, height):
        atom_at = lax.broadcasted_iota(jnp.int32, (height, atoms), 0) + start
        total = jnp.zeros((height, atoms), f32)
        for k in range(neighbours):
            total = total + jnp.where(ids_ref[k : k + 1, :] == atom_at, switch_ref[k : k + 1, :], 0.0)
        mix_ref[start : start + height, :] = total
    mix = mix_ref[...]
    type_at = lax.broadcasted_iota(jnp.int32, (n_types, atoms), 0)
    onehot = (types_ref[...] == type_at).astype(f32)
    mixed = env_ref[...] + dot(embed_ref[...], onehot, ((0,), (0,)), highest)
    descriptor = dot(mixed, mix, ((1,), (0,)), highest) * (1.0 / math.sqrt(neighbours))
    hidden = jnp.tanh(descriptor)
    activity = jnp.tanh(dot(hidden, weight_ref[...], ((0,), (0,)), highest))
    out_weight = out_weight_ref[...]
    scale = 1.0 / math.sqrt(atoms)
    force = force_ref[...]
    weighted = dot(force, activity, ((1,), (0,)), highest)
    predicted = jnp.sum(weighted * out_weight, axis=1, keepdims=True) * scale
    slopes = out_weight * (1.0 - activity * activity)
    jacobian = dot(hidden * force, slopes, ((1,), (0,)), highest) * scale
    error = jnp.broadcast_to(target_ref[...] - predicted, (1, jacobian.shape[1]))
    for block, pieces in enumerate(plan):
        at = 0
        for start, size in pieces:
            payload_ref[block, at : at + size, :] = jacobian[start : start + size, :]
            at += size
        rest = payload_ref.shape[1] - at
        payload_ref[block, at:, :] = jnp.broadcast_to(error, (rest, jacobian.shape[1]))


def network(
    plan, atom_types, neighbor_ids, switching, environment, force_weights, targets, type_embed, layer_weight, out_weight
):
    per_dev, neighbours, atoms = neighbor_ids.shape
    hin, width = layer_weight.shape
    rows = pl.cdiv(sum(size for _, size in plan[0]) + 1, SUBLANES) * SUBLANES

    def per_stream(*shape):
        return pl.BlockSpec((None,) + shape, lambda s: (s,) + (0,) * len(shape))

    def shared(shape):
        return pl.BlockSpec(shape, lambda s: (0,) * len(shape))

    return pl.pallas_call(
        functools.partial(network_kernel, plan=plan),
        grid=(per_dev,),
        in_specs=[
            per_stream(1, atoms),
            per_stream(neighbours, atoms),
            per_stream(neighbours, atoms),
            per_stream(hin, atoms),
            per_stream(1, atoms),
            per_stream(1, 1),
            shared(type_embed.shape),
            shared(layer_weight.shape),
            shared((1, width)),
        ],
        out_specs=pl.BlockSpec((len(plan), None, rows, width), lambda s: (0, s, 0, 0)),
        out_shape=jax.ShapeDtypeStruct((len(plan), per_dev, rows, width), f32),
        scratch_shapes=[pltpu.VMEM((atoms, atoms), f32)],
        name="network",
    )(
        atom_types.reshape(per_dev, 1, atoms),
        neighbor_ids,
        switching,
        environment.swapaxes(1, 2),
        force_weights.reshape(per_dev, 1, atoms),
        targets.reshape(per_dev, 1, 1),
        type_embed,
        layer_weight,
        out_weight.reshape(1, width),
    )


def cross_kernel(at_ref, jac_ref, cov_ref, *refs, col_rows):
    outs, (parts_ref, term_ref) = refs[:-2], refs[-2:]
    streams, rows, lanes = jac_ref.shape
    slab = cov_ref.shape[0]
    step = pl.program_id(0)
    slabs = len(outs)
    flat = jac_ref.reshape(streams * rows, lanes)

    @pl.when(step == 0)
    def _():
        term_ref[...] = jnp.zeros_like(term_ref)
        for i in range(col_rows):
            parts = split3(flat[pl.ds(i, streams, stride=rows), :])
            for n, part in enumerate(parts):
                parts_ref[n * streams : (n + 1) * streams, i * lanes : (i + 1) * lanes] = part

    hi, lo = split2(cov_ref[...])
    by_hi = dot(parts_ref[...], hi, ((1,), (1,)))
    by_lo = dot(parts_ref[0 : 2 * streams, :], lo, ((1,), (1,)))
    cross = by_hi[0:streams] + (
        by_hi[streams : 2 * streams]
        + by_lo[0:streams]
        + (by_hi[2 * streams :] + by_lo[streams:])
    )
    first = col_rows + (at_ref[1] + step) % slabs * (slab // lanes)
    term = jnp.zeros((streams, streams), f32)
    for i in range(slab // lanes):
        own = flat[pl.ds(first + i, streams, stride=rows), :]
        term = term + dot(own, cross[:, i * lanes : (i + 1) * lanes], ((1,), (1,)), highest)
    term_ref[:, 0:streams] += term
    for n in range(slabs):

        @pl.when(step == n)
        def _():
            outs[n][:, 0:slab] = cross

    @pl.when(step == slabs - 1)
    def _():
        for n in range(slabs):
            outs[n][:, slab:] = term_ref[...]


def cross_partial(at, jac, covariance, slab):
    streams, rows, _ = jac.shape
    tile_rows, tile_cols = covariance.shape
    slabs = tile_rows // slab
    term_lanes = pl.cdiv(streams, LANES) * LANES
    out = jax.ShapeDtypeStruct((streams, slab + term_lanes), f32)
    return pl.pallas_call(
        functools.partial(cross_kernel, col_rows=tile_cols // LANES),
        grid_spec=pltpu.PrefetchScalarGridSpec(
            num_scalar_prefetch=1,
            grid=(slabs,),
            in_specs=[
                pl.BlockSpec(jac.shape, lambda n, at: (0, 0, 0)),
                pl.BlockSpec((slab, tile_cols), lambda n, at: ((at[1] + n) % slabs, 0)),
            ],
            out_specs=[pl.BlockSpec(out.shape, lambda n, at: (0, 0))] * slabs,
            scratch_shapes=[
                pltpu.VMEM((3 * streams, tile_cols), bf16),
                pltpu.VMEM((streams, term_lanes), f32),
            ],
        ),
        out_shape=[out] * slabs,
        compiler_params=pltpu.CompilerParams(vmem_limit_bytes=40 << 20),
        name="cross",
    )(at, jac, covariance)


def slab_kernel(*refs, count):
    row_ref, col_ref = refs[2 * count :]
    slab = row_ref.shape[1]
    row = refs[0][...]
    col = refs[count][:, 0:slab]
    for n in range(1, count):
        row = row + refs[n][...]
        col = col + refs[count + n][:, 0:slab]
    row_ref[...] = row[:, 0:slab]
    col_ref[:, 0:slab] = col
    col_ref[:, slab:] = row[:, slab:]


def slab_sums(for_row, for_col, slab):
    streams, padded = for_row[0].shape
    return pl.pallas_call(
        functools.partial(slab_kernel, count=len(for_row)),
        out_shape=[
            jax.ShapeDtypeStruct((streams, slab), f32),
            jax.ShapeDtypeStruct((streams, padded), f32),
        ],
        name="slab",
    )(*for_row, *for_col)


def invert(innovation):
    streams = innovation.shape[0]
    row = lax.broadcasted_iota(jnp.int32, (streams, streams), 0)
    col = lax.broadcasted_iota(jnp.int32, (streams, streams), 1)
    identity = (row == col).astype(f32)
    innovation = innovation + forget * identity
    sums = jnp.sum(jnp.abs(innovation), axis=1, keepdims=True)
    bound = jnp.max(sums, axis=0, keepdims=True)
    inverse = identity * (2.0 / bound) - innovation / (bound * bound)
    for repeat in range(NEWTON - 1):
        step = dot(inverse, innovation, ((1,), (0,)), highest)
        inverse = 2.0 * inverse - dot(step, inverse, ((1,), (0,)), highest)
    return inverse


def update_kernel(
    at_ref, rows_ref, cols_ref, error_ref, weight_ref, cov_ref, new_weight_ref, new_cov_ref, gain_ref, right_ref
):
    slabs, streams, slab = rows_ref.shape
    col_slabs = cols_ref.shape[0]
    step = pl.program_id(0)

    @pl.when(step == 0)
    def _():
        innovation = cols_ref[0, :, slab : slab + streams]
        for n in range(1, col_slabs):
            innovation = innovation + cols_ref[n, :, slab : slab + streams]
        inverse = invert(innovation)
        for n in range(slabs):
            gain_ref[n] = dot(inverse, rows_ref[n], ((0,), (0,)), highest)
        for n in range(col_slabs):
            hi, mid, lo = split3(cols_ref[n, :, 0:slab])
            for m, part in enumerate((hi, mid, lo, hi, mid, hi)):
                right_ref[m * streams : (m + 1) * streams, n * slab : (n + 1) * slab] = part

    gain = gain_ref[step]
    hi, mid, lo = split3(gain)
    left = jnp.concatenate([hi, hi, hi, mid, mid, lo], axis=0)
    update = dot(left, right_ref[...], ((0,), (0,)))
    new_cov_ref[...] = (cov_ref[...] - update) * (1.0 / forget)

    @pl.when(step == at_ref[1])
    def _():
        group = error_ref.shape[1]
        lanes = error_ref.shape[2]
        errors = error_ref.reshape(streams * group, lanes)[pl.ds(0, streams, stride=group), :]
        for i in range(slab // lanes):
            moved = jnp.sum(gain[:, i * lanes : (i + 1) * lanes] * errors, axis=0, keepdims=True)
            own = weight_ref[pl.ds((at_ref[0] * slabs + at_ref[1]) * (slab // lanes) + i, 1), :]
            new_weight_ref[i : i + 1, :] = own + moved


def update(at, row_slabs, col_slabs, jac, layer_weight, covariance):
    slabs, streams, slab = row_slabs.shape
    tile_rows, tile_cols = covariance.shape
    hin, width = layer_weight.shape
    return pl.pallas_call(
        update_kernel,
        grid_spec=pltpu.PrefetchScalarGridSpec(
            num_scalar_prefetch=1,
            grid=(slabs,),
            in_specs=[
                pl.BlockSpec(row_slabs.shape, lambda n, at: (0, 0, 0)),
                pl.BlockSpec(col_slabs.shape, lambda n, at: (0, 0, 0)),
                pl.BlockSpec(
                    (streams, SUBLANES, width), lambda n, at: (0, (tile_rows + tile_cols) // LANES // SUBLANES, 0)
                ),
                pl.BlockSpec((hin, width), lambda n, at: (0, 0)),
                pl.BlockSpec((slab, tile_cols), lambda n, at: (n, 0)),
            ],
            out_specs=[
                pl.BlockSpec((slab // width, width), lambda n, at: (0, 0)),
                pl.BlockSpec((slab, tile_cols), lambda n, at: (n, 0)),
            ],
            scratch_shapes=[
                pltpu.VMEM((slabs, streams, slab), f32),
                pltpu.VMEM((6 * streams, tile_cols), bf16),
            ],
        ),
        out_shape=[
            jax.ShapeDtypeStruct((slab // width, width), f32),
            jax.ShapeDtypeStruct((tile_rows, tile_cols), f32),
        ],
        compiler_params=pltpu.CompilerParams(vmem_limit_bytes=48 << 20),
        name="update",
    )(at, row_slabs, col_slabs, jac, layer_weight, covariance)


def plain_steps(at, jac_all, layer_weight, covariance, slab, cols_n):
    streams = jac_all.shape[0]
    hin, width = layer_weight.shape
    tile_rows, tile_cols = covariance.shape
    first = (at[0] * cols_n + at[1]) * slab
    jacobian = jac_all[:, 0:hin, :].reshape(streams, hin * width)
    errors = jac_all[:, hin, 0]
    jac_cols = lax.dynamic_slice_in_dim(jacobian, at[1] * tile_cols, tile_cols, 1)
    partial = dot(jac_cols, covariance, ((1,), (1,)), highest)
    cross_own = lax.psum_scatter(partial, "col", scatter_dimension=1, tiled=True)
    cross = lax.all_gather(cross_own, ("row", "col"), axis=1, tiled=True)
    inverse = invert(dot(jacobian, cross, ((1,), (1,)), highest))
    gain = dot(inverse, lax.dynamic_slice_in_dim(cross, at[0] * tile_rows, tile_rows, 1), ((0,), (0,)), highest)
    across = lax.dynamic_slice_in_dim(cross, at[1] * tile_cols, tile_cols, 1)
    new_cov = (covariance - dot(gain, across, ((0,), (0,)), highest)) / forget
    own_gain = lax.dynamic_slice_in_dim(gain, at[1] * slab, slab, 1)
    own_weight = lax.dynamic_slice_in_dim(layer_weight.reshape(-1), first, slab, 0)
    new_weight = own_weight + dot(errors, own_gain, ((0,), (0,)), highest)
    return new_weight, new_cov


def on_device(
    atom_types,
    neighbor_ids,
    switching,
    environment,
    force_weights,
    targets,
    type_embed,
    layer_weight,
    out_weight,
    covariance,
):
    rows_n = lax.axis_size("row")
    cols_n = lax.axis_size("col")
    at = jnp.stack([lax.axis_index("row"), lax.axis_index("col")]).astype(jnp.int32)
    tile_rows, tile_cols = covariance.shape
    slab = tile_rows // cols_n
    hin, width = layer_weight.shape
    run_network = functools.partial(
        network,
        atom_types=atom_types,
        neighbor_ids=neighbor_ids,
        switching=switching,
        environment=environment,
        force_weights=force_weights,
        targets=targets,
        type_embed=type_embed,
        layer_weight=layer_weight,
        out_weight=out_weight,
    )
    if slab % LANES or width != LANES or (tile_rows + tile_cols) % (SUBLANES * LANES):
        payload = run_network([[(0, hin)]])[0]
        jac_all = lax.all_gather(payload, ("row", "col"), axis=0, tiled=True)
        return plain_steps(at, jac_all, layer_weight, covariance, slab, cols_n)
    row_size, col_size = tile_rows // LANES, tile_cols // LANES
    plan = [[(c * col_size, col_size), (r * row_size, row_size)] for r in range(rows_n) for c in range(cols_n)]
    payload = run_network(plan)
    jac = lax.all_to_all(payload, ("row", "col"), split_axis=0, concat_axis=0, tiled=True)
    jac = jac.reshape(-1, *jac.shape[2:])
    partial = cross_partial(at, jac, covariance, slab)
    devices = [(r, c) for r in range(rows_n) for c in range(cols_n)]
    for_row, for_col = [partial[0]], []
    for k in range(cols_n):
        to_row, to_col = [], []
        for r, c in devices:
            d = r * cols_n + (c + k) % cols_n
            to_row.append((r * cols_n + c, d))
            to_col.append((r * cols_n + c, d % rows_n * cols_n + d // rows_n))
        if k:
            for_row.append(lax.ppermute(partial[k], ("row", "col"), to_row))
        for_col.append(lax.ppermute(partial[k], ("row", "col"), to_col))
    row_own, col_own = slab_sums(for_row, for_col, slab)
    row_slabs = lax.all_gather(row_own, "col", axis=0, tiled=False)
    col_slabs = lax.all_gather(col_own, "row", axis=0, tiled=False)
    new_weight, new_cov = update(at, row_slabs, col_slabs, jac, layer_weight, covariance)
    return new_weight.reshape(-1), new_cov


def solution(mesh):
    in_specs = (
        P(("row", "col"), None),
        P(("row", "col"), None, None),
        P(("row", "col"), None, None),
        P(("row", "col"), None, None),
        P(("row", "col"), None),
        P(("row", "col")),
        P(),
        P(),
        P(),
        P("row", "col"),
    )
    out_specs = (P(("row", "col")), P("row", "col"))
    return jax.shard_map(
        on_device, mesh=mesh, in_specs=in_specs, out_specs=out_specs, check_vma=False
    )
```

```python
import functools
import math

import jax
import jax.numpy as jnp
from jax import lax
from jax.experimental import pallas as pl
from jax.experimental.pallas import tpu as pltpu
from jax.sharding import PartitionSpec as P

NEWTON = 4
LANES = 128
SUBLANES = 8


forget = 0.98
highest = lax.Precision.HIGHEST
f32 = jnp.float32
bf16 = jnp.bfloat16


def dot(left, right, contract, precision=None):
    return lax.dot_general(
        left, right, (contract, ((), ())), precision=precision, preferred_element_type=f32
    )


def split3(x):
    hi = x.astype(bf16)
    rest = x - hi.astype(f32)
    mid = rest.astype(bf16)
    lo = (rest - mid.astype(f32)).astype(bf16)
    return hi, mid, lo


def split2(x):
    hi = x.astype(bf16)
    return hi, (x - hi.astype(f32)).astype(bf16)


def network_kernel(
    types_ref,
    ids_ref,
    switch_ref,
    env_ref,
    force_ref,
    target_ref,
    embed_ref,
    weight_ref,
    out_weight_ref,
    payload_ref,
    error_ref,
    mix_ref,
):
    neighbours, atoms = ids_ref.shape
    n_types = embed_ref.shape[0]
    height = min(64, atoms)
    for start in range(0, atoms, height):
        atom_at = lax.broadcasted_iota(jnp.int32, (height, atoms), 0) + start
        total = jnp.zeros((height, atoms), f32)
        for k in range(neighbours):
            total = total + jnp.where(ids_ref[k : k + 1, :] == atom_at, switch_ref[k : k + 1, :], 0.0)
        mix_ref[start : start + height, :] = total
    mix = mix_ref[...]
    type_at = lax.broadcasted_iota(jnp.int32, (n_types, atoms), 0)
    onehot = (types_ref[...] == type_at).astype(f32)
    mixed = env_ref[...] + dot(embed_ref[...], onehot, ((0,), (0,)), highest)
    descriptor = dot(mixed, mix, ((1,), (0,)), highest) * (1.0 / math.sqrt(neighbours))
    hidden = jnp.tanh(descriptor)
    activity = jnp.tanh(dot(hidden, weight_ref[...], ((0,), (0,)), highest))
    out_weight = out_weight_ref[...]
    scale = 1.0 / math.sqrt(atoms)
    force = force_ref[...]
    weighted = dot(force, activity, ((1,), (0,)), highest)
    predicted = jnp.sum(weighted * out_weight, axis=1, keepdims=True) * scale
    slopes = out_weight * (1.0 - activity * activity)
    jacobian = dot(hidden * force, slopes, ((1,), (0,)), highest) * scale
    error_ref[...] = jnp.broadcast_to(target_ref[...] - predicted, error_ref.shape)
    blocks, rows, _ = payload_ref.shape
    for block in range(blocks):
        start = block * rows % jacobian.shape[0]
        payload_ref[block] = jacobian[start : start + rows, :]


def network(
    blocks, rows, atom_types, neighbor_ids, switching, environment, force_weights, targets, type_embed, layer_weight, out_weight
):
    per_dev, neighbours, atoms = neighbor_ids.shape
    hin, width = layer_weight.shape

    def per_stream(*shape):
        return pl.BlockSpec((None,) + shape, lambda s: (s,) + (0,) * len(shape))

    def shared(shape):
        return pl.BlockSpec(shape, lambda s: (0,) * len(shape))

    return pl.pallas_call(
        network_kernel,
        grid=(per_dev,),
        in_specs=[
            per_stream(1, atoms),
            per_stream(neighbours, atoms),
            per_stream(neighbours, atoms),
            per_stream(hin, atoms),
            per_stream(1, atoms),
            per_stream(1, 1),
            shared(type_embed.shape),
            shared(layer_weight.shape),
            shared((1, width)),
        ],
        out_specs=[
            pl.BlockSpec((blocks, None, rows, width), lambda s: (0, s, 0, 0)),
            per_stream(1, width),
        ],
        out_shape=[
            jax.ShapeDtypeStruct((blocks, per_dev, rows, width), f32),
            jax.ShapeDtypeStruct((per_dev, 1, width), f32),
        ],
        scratch_shapes=[pltpu.VMEM((atoms, atoms), f32)],
        name="network",
    )(
        atom_types.reshape(per_dev, 1, atoms),
        neighbor_ids,
        switching,
        environment.swapaxes(1, 2),
        force_weights.reshape(per_dev, 1, atoms),
        targets.reshape(per_dev, 1, 1),
        type_embed,
        layer_weight,
        out_weight.reshape(1, width),
    )


def stage_kernel(cov_ref, held_ref, hi_ref, lo_ref, sems):
    chunks = sems.shape[0]
    height = cov_ref.shape[0] // chunks
    copies = []
    for n in range(chunks):
        rows = pl.ds(n * height, height)
        copies.append(pltpu.make_async_copy(cov_ref.at[rows], held_ref.at[rows], sems.at[n]))
        copies[-1].start()
    for n in range(chunks):
        copies[n].wait()
        rows = pl.ds(n * height, height)
        hi, lo = split2(held_ref[rows, :])
        hi_ref[rows, :] = hi
        lo_ref[rows, :] = lo


def stage(covariance):
    shape = covariance.shape
    return pl.pallas_call(
        stage_kernel,
        in_specs=[pl.BlockSpec(memory_space=pl.ANY)],
        out_specs=[pl.BlockSpec(memory_space=pltpu.VMEM)] * 3,
        out_shape=[pltpu.VMEM(shape, f32), pltpu.VMEM(shape, bf16), pltpu.VMEM(shape, bf16)],
        scratch_shapes=[pltpu.SemaphoreType.DMA((8,))],
        compiler_params=pltpu.CompilerParams(vmem_limit_bytes=16 << 20),
        name="stage",
    )(covariance)


def cross_kernel(jac_ref, hi_ref, lo_ref, out_ref, parts_ref):
    streams, rows, lanes = jac_ref.shape
    slabs, _, slab = out_ref.shape
    flat = jac_ref.reshape(streams * rows, lanes)
    for i in range(rows):
        parts = split3(flat[pl.ds(i, streams, stride=rows), :])
        for n, part in enumerate(parts):
            parts_ref[n * streams : (n + 1) * streams, i * lanes : (i + 1) * lanes] = part
    for n in range(slabs):
        here = slice(n * slab, (n + 1) * slab)
        by_hi = dot(parts_ref[...], hi_ref[here, :], ((1,), (1,)))
        by_lo = dot(parts_ref[0 : 2 * streams, :], lo_ref[here, :], ((1,), (1,)))
        out_ref[n] = by_hi[0:streams] + (
            by_hi[streams : 2 * streams]
            + by_lo[0:streams]
            + (by_hi[2 * streams :] + by_lo[streams:])
        )


def cross_partial(jac, hi, lo, slab):
    streams = jac.shape[0]
    tile_rows, tile_cols = hi.shape
    whole = pl.BlockSpec(memory_space=pltpu.VMEM)
    return pl.pallas_call(
        cross_kernel,
        in_specs=[whole] * 3,
        out_specs=whole,
        out_shape=jax.ShapeDtypeStruct((tile_rows // slab, streams, slab), f32),
        scratch_shapes=[pltpu.VMEM((3 * streams, tile_cols), bf16)],
        compiler_params=pltpu.CompilerParams(vmem_limit_bytes=16 << 20),
        name="cross",
    )(jac, in_vmem(hi), in_vmem(lo))


def in_vmem(x):
    return pltpu.with_memory_space_constraint(x, pltpu.VMEM)


def slab_kernel(pieces_ref, error_ref, out_ref):
    pieces, streams, slab = pieces_ref.shape
    cross = pieces_ref[0]
    for n in range(1, pieces):
        cross = cross + pieces_ref[n]
    out_ref[0:streams, :] = cross
    out_ref[streams:, :] = jnp.broadcast_to(error_ref[0, :, 0:1], (SUBLANES, slab))


def slab_sum(pieces, error):
    _, streams, slab = pieces.shape
    return pl.pallas_call(
        slab_kernel,
        out_shape=jax.ShapeDtypeStruct((streams + SUBLANES, slab), f32),
        name="slab",
    )(pieces, error)


def term_kernel(own_ref, cols_ref, jac_ref, out_ref):
    streams, rows, lanes = jac_ref.shape
    count, _, slab = cols_ref.shape
    flat = jac_ref.reshape(streams * rows, lanes)
    term = jnp.zeros((streams, streams), f32)
    for i in range(rows):
        own = flat[pl.ds(i, streams, stride=rows), :]
        start = i * lanes % slab
        across = cols_ref[i * lanes // slab, 0:streams, start : start + lanes]
        term = term + dot(own, across, ((1,), (1,)), highest)
    out_ref[:, 0:slab] = own_ref[0:streams, :]
    out_ref[:, slab : slab + streams] = term
    first = lax.axis_index("col") * count
    stream_at = lax.broadcasted_iota(jnp.int32, (streams, lanes), 0)
    errors = jnp.zeros((streams, lanes), f32)
    for n in range(count):
        errors = jnp.where(stream_at == first + n, cols_ref[n, streams : streams + 1, 0:lanes], errors)
    out_ref[:, slab + streams :] = errors[:, streams:]


def with_terms(own, col_slabs, jac):
    streams = jac.shape[0]
    slab = own.shape[1]
    return pl.pallas_call(
        term_kernel,
        out_shape=jax.ShapeDtypeStruct((streams, slab + LANES), f32),
        name="term",
    )(own, col_slabs, jac)


def invert(innovation):
    streams = innovation.shape[0]
    row = lax.broadcasted_iota(jnp.int32, (streams, streams), 0)
    col = lax.broadcasted_iota(jnp.int32, (streams, streams), 1)
    identity = (row == col).astype(f32)
    innovation = innovation + forget * identity
    sums = jnp.sum(jnp.abs(innovation), axis=1, keepdims=True)
    bound = jnp.max(sums, axis=0, keepdims=True)
    power = identity - innovation / bound
    inverse = identity + power
    for repeat in range(NEWTON - 1):
        power = dot(power, power, ((1,), (0,)), highest)
        inverse = inverse + dot(inverse, power, ((1,), (0,)), highest)
    return inverse / bound


def update_kernel(
    rows_ref, cols_ref, weight_ref, cov_ref, new_weight_ref, new_cov_ref, right_ref, done_ref, sems
):
    slabs, streams, _ = rows_ref.shape
    col_slabs, _, slab = cols_ref.shape
    lanes = weight_ref.shape[1]
    beside = rows_ref[0, :, slab:]
    for n in range(1, slabs):
        beside = beside + rows_ref[n, :, slab:]
    inverse = invert(beside[:, 0:streams])
    errors = beside[:, streams : streams + 1]
    for n in range(col_slabs):
        hi, mid, lo = split3(cols_ref[n, 0:streams, :])
        for m, part in enumerate((hi, mid, lo, hi, mid, hi)):
            right_ref[m * streams : (m + 1) * streams, n * slab : (n + 1) * slab] = part
    col_at = lax.axis_index("col")
    own_at = (lax.axis_index("row") * slabs + col_at) * (slab // lanes)
    copies = []
    for n in range(slabs):
        gain = dot(inverse, rows_ref[n, :, 0:slab], ((0,), (0,)), highest)
        hi, mid, lo = split3(gain)
        left = jnp.concatenate([hi, hi, hi, mid, mid, lo], axis=0)
        update = dot(left, right_ref[...], ((0,), (0,)))
        here = slice(n * slab, (n + 1) * slab)
        done_ref[here, :] = (cov_ref[here, :] - update) * (1.0 / forget)
        copies.append(pltpu.make_async_copy(done_ref.at[here], new_cov_ref.at[here], sems.at[n]))
        copies[-1].start()

        @pl.when(col_at == n)
        def _():
            moved = jnp.sum(gain * errors, axis=0, keepdims=True)
            for i in range(slab // lanes):
                own = weight_ref[pl.ds(own_at + i, 1), :]
                new_weight_ref[i : i + 1, :] = own + moved[:, i * lanes : (i + 1) * lanes]

    for copy in copies:
        copy.wait()


def update(row_slabs, col_slabs, layer_weight, held):
    slabs, streams, _ = row_slabs.shape
    slab = col_slabs.shape[2]
    tile_rows, tile_cols = held.shape
    width = layer_weight.shape[1]
    whole = pl.BlockSpec(memory_space=pltpu.VMEM)
    return pl.pallas_call(
        update_kernel,
        in_specs=[whole] * 4,
        out_specs=[whole, pl.BlockSpec(memory_space=pl.ANY)],
        out_shape=[
            jax.ShapeDtypeStruct((slab // width, width), f32),
            jax.ShapeDtypeStruct((tile_rows, tile_cols), f32),
        ],
        scratch_shapes=[
            pltpu.VMEM((6 * streams, tile_cols), bf16),
            pltpu.VMEM((tile_rows, tile_cols), f32),
            pltpu.SemaphoreType.DMA((slabs,)),
        ],
        compiler_params=pltpu.CompilerParams(vmem_limit_bytes=24 << 20),
        name="update",
    )(row_slabs, col_slabs, layer_weight, in_vmem(held))


def plain_steps(at, jac_all, errors, layer_weight, covariance, slab, cols_n):
    streams = jac_all.shape[0]
    hin, width = layer_weight.shape
    tile_rows, tile_cols = covariance.shape
    first = (at[0] * cols_n + at[1]) * slab
    jacobian = jac_all[:, 0:hin, :].reshape(streams, hin * width)
    jac_cols = lax.dynamic_slice_in_dim(jacobian, at[1] * tile_cols, tile_cols, 1)
    partial = dot(jac_cols, covariance, ((1,), (1,)), highest)
    cross_own = lax.psum_scatter(partial, "col", scatter_dimension=1, tiled=True)
    cross = lax.all_gather(cross_own, ("row", "col"), axis=1, tiled=True)
    inverse = invert(dot(jacobian, cross, ((1,), (1,)), highest))
    gain = dot(inverse, lax.dynamic_slice_in_dim(cross, at[0] * tile_rows, tile_rows, 1), ((0,), (0,)), highest)
    across = lax.dynamic_slice_in_dim(cross, at[1] * tile_cols, tile_cols, 1)
    new_cov = (covariance - dot(gain, across, ((0,), (0,)), highest)) / forget
    own_gain = lax.dynamic_slice_in_dim(gain, at[1] * slab, slab, 1)
    own_weight = lax.dynamic_slice_in_dim(layer_weight.reshape(-1), first, slab, 0)
    new_weight = own_weight + dot(errors, own_gain, ((0,), (0,)), highest)
    return new_weight, new_cov


def on_device(
    atom_types,
    neighbor_ids,
    switching,
    environment,
    force_weights,
    targets,
    type_embed,
    layer_weight,
    out_weight,
    covariance,
):
    rows_n = lax.axis_size("row")
    cols_n = lax.axis_size("col")
    at = jnp.stack([lax.axis_index("row"), lax.axis_index("col")]).astype(jnp.int32)
    tile_rows, tile_cols = covariance.shape
    slab = tile_rows // cols_n
    hin, width = layer_weight.shape
    run_network = functools.partial(
        network,
        atom_types=atom_types,
        neighbor_ids=neighbor_ids,
        switching=switching,
        environment=environment,
        force_weights=force_weights,
        targets=targets,
        type_embed=type_embed,
        layer_weight=layer_weight,
        out_weight=out_weight,
    )
    streams = rows_n * cols_n * atom_types.shape[0]
    kernels = (
        atom_types.shape[0] == 1
        and width == LANES
        and slab % LANES == 0
        and tile_cols % (SUBLANES * LANES) == 0
        and rows_n * slab == tile_cols
        and streams < LANES
    )
    if not kernels:
        payload, error = run_network(1, hin)
        jac_all = lax.all_gather(payload[0], ("row", "col"), axis=0, tiled=True)
        errors = lax.all_gather(error[:, 0, 0], ("row", "col"), axis=0, tiled=True)
        return plain_steps(at, jac_all, errors, layer_weight, covariance, slab, cols_n)
    payload, error = run_network(rows_n * cols_n, tile_cols // LANES)
    jac = lax.all_to_all(payload, ("row", "col"), split_axis=0, concat_axis=0, tiled=True)
    jac = jac.reshape(-1, *jac.shape[2:])
    held, hi, lo = stage(covariance)
    partial = cross_partial(jac, hi, lo, slab)
    pieces = lax.all_to_all(partial, "col", split_axis=0, concat_axis=0, tiled=True)
    own = slab_sum(pieces, error)
    to_col = [(d, d % rows_n * cols_n + d // rows_n) for d in range(rows_n * cols_n)]
    col_slabs = lax.all_gather(lax.ppermute(own, ("row", "col"), to_col), "row", axis=0, tiled=False)
    row_slabs = lax.all_gather(with_terms(own, col_slabs, jac), "col", axis=0, tiled=False)
    new_weight, new_cov = update(row_slabs, col_slabs, layer_weight, held)
    return new_weight.reshape(-1), new_cov


def solution(mesh):
    in_specs = (
        P(("row", "col"), None),
        P(("row", "col"), None, None),
        P(("row", "col"), None, None),
        P(("row", "col"), None, None),
        P(("row", "col"), None),
        P(("row", "col")),
        P(),
        P(),
        P(),
        P("row", "col"),
    )
    out_specs = (P(("row", "col")), P("row", "col"))
    return jax.shard_map(
        on_device, mesh=mesh, in_specs=in_specs, out_specs=out_specs, check_vma=False
    )
```

```python
import functools
import math

import jax
import jax.numpy as jnp
from jax import lax
from jax.experimental import pallas as pl
from jax.experimental.pallas import tpu as pltpu
from jax.sharding import PartitionSpec as P

NEWTON = 4
LANES = 128
SUBLANES = 8


forget = 0.98
highest = lax.Precision.HIGHEST
f32 = jnp.float32
bf16 = jnp.bfloat16


def dot(left, right, contract, precision=None):
    return lax.dot_general(
        left, right, (contract, ((), ())), precision=precision, preferred_element_type=f32
    )


def split3(x):
    hi = x.astype(bf16)
    rest = x - hi.astype(f32)
    mid = rest.astype(bf16)
    lo = (rest - mid.astype(f32)).astype(bf16)
    return hi, mid, lo


def split2(x):
    hi = x.astype(bf16)
    return hi, (x - hi.astype(f32)).astype(bf16)


def network_kernel(
    types_ref,
    ids_ref,
    switch_ref,
    env_ref,
    force_ref,
    target_ref,
    embed_ref,
    weight_ref,
    out_weight_ref,
    payload_ref,
    error_ref,
    mix_ref,
    *,
    plan,
):
    neighbours, atoms = ids_ref.shape
    n_types = embed_ref.shape[0]
    height = min(64, atoms)
    for start in range(0, atoms, height):
        atom_at = lax.broadcasted_iota(jnp.int32, (height, atoms), 0) + start
        total = jnp.zeros((height, atoms), f32)
        for k in range(neighbours):
            total = total + jnp.where(ids_ref[k : k + 1, :] == atom_at, switch_ref[k : k + 1, :], 0.0)
        mix_ref[start : start + height, :] = total
    mix = mix_ref[...]
    type_at = lax.broadcasted_iota(jnp.int32, (n_types, atoms), 0)
    onehot = (types_ref[...] == type_at).astype(f32)
    mixed = env_ref[...] + dot(embed_ref[...], onehot, ((0,), (0,)), highest)
    descriptor = dot(mixed, mix, ((1,), (0,)), highest) * (1.0 / math.sqrt(neighbours))
    hidden = jnp.tanh(descriptor)
    activity = jnp.tanh(dot(hidden, weight_ref[...], ((0,), (0,)), highest))
    out_weight = out_weight_ref[...]
    scale = 1.0 / math.sqrt(atoms)
    force = force_ref[...]
    weighted = dot(force, activity, ((1,), (0,)), highest)
    predicted = jnp.sum(weighted * out_weight, axis=1, keepdims=True) * scale
    slopes = out_weight * (1.0 - activity * activity)
    jacobian = dot(hidden * force, slopes, ((1,), (0,)), highest) * scale
    error_ref[...] = jnp.broadcast_to(target_ref[...] - predicted, error_ref.shape)
    for block, pieces in enumerate(plan):
        at = 0
        for start, size in pieces:
            payload_ref[block, at : at + size, :] = jacobian[start : start + size, :]
            at += size


def network(
    plan, atom_types, neighbor_ids, switching, environment, force_weights, targets, type_embed, layer_weight, out_weight
):
    per_dev, neighbours, atoms = neighbor_ids.shape
    hin, width = layer_weight.shape
    blocks, rows = len(plan), sum(size for _, size in plan[0])

    def per_stream(*shape):
        return pl.BlockSpec((None,) + shape, lambda s: (s,) + (0,) * len(shape))

    def shared(shape):
        return pl.BlockSpec(shape, lambda s: (0,) * len(shape))

    return pl.pallas_call(
        functools.partial(network_kernel, plan=plan),
        grid=(per_dev,),
        in_specs=[
            per_stream(1, atoms),
            per_stream(neighbours, atoms),
            per_stream(neighbours, atoms),
            per_stream(hin, atoms),
            per_stream(1, atoms),
            per_stream(1, 1),
            shared(type_embed.shape),
            shared(layer_weight.shape),
            shared((1, width)),
        ],
        out_specs=[
            pl.BlockSpec((blocks, None, rows, width), lambda s: (0, s, 0, 0)),
            per_stream(1, width),
        ],
        out_shape=[
            jax.ShapeDtypeStruct((blocks, per_dev, rows, width), f32),
            jax.ShapeDtypeStruct((per_dev, 1, width), f32),
        ],
        scratch_shapes=[pltpu.VMEM((atoms, atoms), f32)],
        name="network",
    )(
        atom_types.reshape(per_dev, 1, atoms),
        neighbor_ids,
        switching,
        environment.swapaxes(1, 2),
        force_weights.reshape(per_dev, 1, atoms),
        targets.reshape(per_dev, 1, 1),
        type_embed,
        layer_weight,
        out_weight.reshape(1, width),
    )


def in_hbm(x):
    return pltpu.with_memory_space_constraint(x, pltpu.HBM)


def stage_kernel(cov_ref, hi_ref, lo_ref):
    hi_ref[...], lo_ref[...] = split2(cov_ref[...])


def stage(covariance):
    rows, cols = covariance.shape
    height = rows // 8
    block = pl.BlockSpec((height, cols), lambda n: (n, 0))
    return pl.pallas_call(
        stage_kernel,
        grid=(rows // height,),
        in_specs=[block],
        out_specs=[block] * 2,
        out_shape=[pltpu.HBM((rows, cols), bf16)] * 2,
        compiler_params=pltpu.CompilerParams(vmem_limit_bytes=16 << 20),
        name="stage",
    )(in_hbm(covariance))


def five_products(parts, hi, lo, contract):
    streams = parts.shape[0] // 3
    by_hi = dot(parts, hi, contract)
    by_lo = dot(parts[0 : 2 * streams], lo, contract)
    return by_hi[0:streams] + (
        by_hi[streams : 2 * streams] + by_lo[0:streams] + (by_hi[2 * streams :] + by_lo[streams:])
    )


def cross_kernel(jac_ref, error_ref, hi_ref, lo_ref, row_ref, col_ref, parts_ref, row_parts_ref, sum_ref, term_ref, *, col_rows):
    streams, rows, lanes = jac_ref.shape
    slab, tile_cols = hi_ref.shape
    slab_rows = slab // lanes
    step = pl.program_id(0)
    flat = jac_ref.reshape(streams * rows, lanes)

    @pl.when(step == 0)
    def _():
        term_ref[...] = jnp.zeros_like(term_ref)
        sum_ref[...] = jnp.zeros_like(sum_ref)
        for i in range(col_rows):
            parts = split3(flat[pl.ds(i, streams, stride=rows), :])
            for n, part in enumerate(parts):
                parts_ref[n * streams : (n + 1) * streams, i * lanes : (i + 1) * lanes] = part

    hi, lo = hi_ref[...], lo_ref[...]
    cross = five_products(parts_ref[...], hi, lo, ((1,), (1,)))
    row_ref[...] = cross
    term = jnp.zeros((streams, streams), f32)
    for i in range(slab_rows):
        own = flat[pl.ds(col_rows + step * slab_rows + i, streams, stride=rows), :]
        term = term + dot(own, cross[:, i * lanes : (i + 1) * lanes], ((1,), (1,)), highest)
        for n, part in enumerate(split3(own)):
            row_parts_ref[n * streams : (n + 1) * streams, i * lanes : (i + 1) * lanes] = part
    term_ref[:, 0:streams] += term
    sum_ref[...] += five_products(row_parts_ref[...], hi, lo, ((1,), (0,)))

    @pl.when(step == pl.num_programs(0) - 1)
    def _():
        own_at = lax.axis_index("row") * lax.axis_size("col") + lax.axis_index("col")
        stream_at = lax.broadcasted_iota(jnp.int32, (streams, lanes), 0)
        lane_at = lax.broadcasted_iota(jnp.int32, (streams, lanes), 1)
        error = jnp.where((stream_at == own_at) & (lane_at >= streams), error_ref[0], 0.0)
        beside = term_ref[...] + error
        for n in range(tile_cols // slab):
            col_ref[n, :, 0:slab] = sum_ref[:, n * slab : (n + 1) * slab]
            col_ref[n, :, slab:] = beside


def cross_partial(jac, error, hi, lo, slab):
    streams = jac.shape[0]
    tile_rows, tile_cols = hi.shape
    col_slabs = tile_cols // slab
    block = pl.BlockSpec((slab, tile_cols), lambda n: (n, 0))
    return pl.pallas_call(
        functools.partial(cross_kernel, col_rows=tile_cols // LANES),
        grid=(tile_rows // slab,),
        in_specs=[
            pl.BlockSpec(jac.shape, lambda n: (0, 0, 0)),
            pl.BlockSpec(error.shape, lambda n: (0, 0, 0)),
            block,
            block,
        ],
        out_specs=[
            pl.BlockSpec((None, streams, slab), lambda n: (n, 0, 0)),
            pl.BlockSpec((col_slabs, streams, slab + LANES), lambda n: (0, 0, 0)),
        ],
        out_shape=[
            jax.ShapeDtypeStruct((tile_rows // slab, streams, slab), f32),
            jax.ShapeDtypeStruct((col_slabs, streams, slab + LANES), f32),
        ],
        scratch_shapes=[
            pltpu.VMEM((3 * streams, tile_cols), bf16),
            pltpu.VMEM((3 * streams, slab), bf16),
            pltpu.VMEM((streams, tile_cols), f32),
            pltpu.VMEM((streams, LANES), f32),
        ],
        compiler_params=pltpu.CompilerParams(vmem_limit_bytes=32 << 20),
        name="cross",
    )(jac, error, in_hbm(hi), in_hbm(lo))


def slab_kernel(rows_ref, cols_ref, row_ref, col_ref):
    slab = rows_ref.shape[2]
    row = rows_ref[0]
    for n in range(1, rows_ref.shape[0]):
        row = row + rows_ref[n]
    col = cols_ref[0]
    for n in range(1, cols_ref.shape[0]):
        col = col + cols_ref[n]
    for n in range(row_ref.shape[0]):
        row_ref[n, :, 0:slab] = row
        row_ref[n, :, slab:] = col[:, slab:]
    for n in range(col_ref.shape[0]):
        col_ref[n] = col[:, 0:slab]


def slab_sums(row_pieces, col_pieces):
    rows_n, streams, slab = row_pieces.shape
    cols_n, _, padded = col_pieces.shape
    return pl.pallas_call(
        slab_kernel,
        out_shape=[
            jax.ShapeDtypeStruct((rows_n, streams, padded), f32),
            jax.ShapeDtypeStruct((cols_n, streams, slab), f32),
        ],
        name="slab",
    )(row_pieces, col_pieces)


def invert(innovation):
    streams = innovation.shape[0]
    row = lax.broadcasted_iota(jnp.int32, (streams, streams), 0)
    col = lax.broadcasted_iota(jnp.int32, (streams, streams), 1)
    identity = (row == col).astype(f32)
    innovation = innovation + forget * identity
    sums = jnp.sum(jnp.abs(innovation), axis=1, keepdims=True)
    bound = jnp.max(sums, axis=0, keepdims=True)
    power = identity - innovation / bound
    inverse = identity + power
    for repeat in range(NEWTON - 1):
        power = dot(power, power, ((1,), (0,)), highest)
        inverse = inverse + dot(inverse, power, ((1,), (0,)), highest)
    return inverse / bound


def update_kernel(
    rows_ref, cols_ref, weight_ref, cov_ref, new_weight_ref, new_cov_ref, right_ref, tile_ref, in_sems, out_sems
):
    slabs, streams, _ = rows_ref.shape
    col_slabs, _, slab = cols_ref.shape
    lanes = weight_ref.shape[1]
    reads = []
    for n in range(slabs):
        here = pl.ds(n * slab, slab)
        reads.append(pltpu.make_async_copy(cov_ref.at[here], tile_ref.at[here], in_sems.at[n]))
        reads[-1].start()
    beside = rows_ref[0, :, slab:]
    for n in range(1, slabs):
        beside = beside + rows_ref[n, :, slab:]
    inverse = invert(beside[:, 0:streams])
    errors = beside[:, streams : streams + 1]
    for n in range(col_slabs):
        hi, mid, lo = split3(cols_ref[n])
        for m, part in enumerate((hi, mid, lo, hi, mid, hi)):
            right_ref[m * streams : (m + 1) * streams, n * slab : (n + 1) * slab] = part
    col_at = lax.axis_index("col")
    own_at = (lax.axis_index("row") * slabs + col_at) * (slab // lanes)
    writes = []
    for n in range(slabs):
        gain = dot(inverse, rows_ref[n, :, 0:slab], ((0,), (0,)), highest)
        hi, mid, lo = split3(gain)
        left = jnp.concatenate([hi, hi, hi, mid, mid, lo], axis=0)
        update = dot(left, right_ref[...], ((0,), (0,)))
        here = pl.ds(n * slab, slab)
        reads[n].wait()
        tile_ref[here, :] = (tile_ref[here, :] - update) * (1.0 / forget)
        writes.append(pltpu.make_async_copy(tile_ref.at[here], new_cov_ref.at[here], out_sems.at[n]))
        writes[-1].start()

        @pl.when(col_at == n)
        def _():
            moved = jnp.sum(gain * errors, axis=0, keepdims=True)
            for i in range(slab // lanes):
                own = weight_ref[pl.ds(own_at + i, 1), :]
                new_weight_ref[i : i + 1, :] = own + moved[:, i * lanes : (i + 1) * lanes]

    for write in writes:
        write.wait()


def update(row_slabs, col_slabs, layer_weight, covariance):
    slabs, streams, _ = row_slabs.shape
    slab = col_slabs.shape[2]
    tile_rows, tile_cols = covariance.shape
    width = layer_weight.shape[1]
    whole = pl.BlockSpec(memory_space=pltpu.VMEM)
    beyond = pl.BlockSpec(memory_space=pl.ANY)
    return pl.pallas_call(
        update_kernel,
        in_specs=[whole, whole, whole, beyond],
        out_specs=[whole, beyond],
        out_shape=[
            jax.ShapeDtypeStruct((slab // width, width), f32),
            jax.ShapeDtypeStruct((tile_rows, tile_cols), f32),
        ],
        scratch_shapes=[
            pltpu.VMEM((6 * streams, tile_cols), bf16),
            pltpu.VMEM((tile_rows, tile_cols), f32),
            pltpu.SemaphoreType.DMA((slabs,)),
            pltpu.SemaphoreType.DMA((slabs,)),
        ],
        compiler_params=pltpu.CompilerParams(vmem_limit_bytes=32 << 20),
        name="update",
    )(row_slabs, col_slabs, layer_weight, in_hbm(covariance))


def plain_steps(at, jac_all, errors, layer_weight, covariance, slab, cols_n):
    streams = jac_all.shape[0]
    hin, width = layer_weight.shape
    tile_rows, tile_cols = covariance.shape
    first = (at[0] * cols_n + at[1]) * slab
    jacobian = jac_all[:, 0:hin, :].reshape(streams, hin * width)
    jac_cols = lax.dynamic_slice_in_dim(jacobian, at[1] * tile_cols, tile_cols, 1)
    partial = dot(jac_cols, covariance, ((1,), (1,)), highest)
    cross_own = lax.psum_scatter(partial, "col", scatter_dimension=1, tiled=True)
    cross = lax.all_gather(cross_own, ("row", "col"), axis=1, tiled=True)
    inverse = invert(dot(jacobian, cross, ((1,), (1,)), highest))
    gain = dot(inverse, lax.dynamic_slice_in_dim(cross, at[0] * tile_rows, tile_rows, 1), ((0,), (0,)), highest)
    across = lax.dynamic_slice_in_dim(cross, at[1] * tile_cols, tile_cols, 1)
    new_cov = (covariance - dot(gain, across, ((0,), (0,)), highest)) / forget
    own_gain = lax.dynamic_slice_in_dim(gain, at[1] * slab, slab, 1)
    own_weight = lax.dynamic_slice_in_dim(layer_weight.reshape(-1), first, slab, 0)
    new_weight = own_weight + dot(errors, own_gain, ((0,), (0,)), highest)
    return new_weight, new_cov


def exchange(x, axes):
    return lax.all_to_all(x, axes, split_axis=0, concat_axis=0, tiled=True)


def on_device(
    atom_types,
    neighbor_ids,
    switching,
    environment,
    force_weights,
    targets,
    type_embed,
    layer_weight,
    out_weight,
    covariance,
):
    rows_n = lax.axis_size("row")
    cols_n = lax.axis_size("col")
    at = jnp.stack([lax.axis_index("row"), lax.axis_index("col")]).astype(jnp.int32)
    tile_rows, tile_cols = covariance.shape
    slab = tile_rows // cols_n
    hin, width = layer_weight.shape
    run_network = functools.partial(
        network,
        atom_types=atom_types,
        neighbor_ids=neighbor_ids,
        switching=switching,
        environment=environment,
        force_weights=force_weights,
        targets=targets,
        type_embed=type_embed,
        layer_weight=layer_weight,
        out_weight=out_weight,
    )
    streams = rows_n * cols_n * atom_types.shape[0]
    kernels = (
        atom_types.shape[0] == 1
        and width == LANES
        and slab % LANES == 0
        and tile_rows % (SUBLANES * LANES) == 0
        and tile_cols % (SUBLANES * LANES) == 0
        and rows_n * slab == tile_cols
        and streams < LANES
    )
    if not kernels:
        payload, error = run_network([[(0, hin)]])
        jac_all = lax.all_gather(payload[0], ("row", "col"), axis=0, tiled=True)
        errors = lax.all_gather(error[:, 0, 0], ("row", "col"), axis=0, tiled=True)
        return plain_steps(at, jac_all, errors, layer_weight, covariance, slab, cols_n)
    row_size, col_size = tile_rows // LANES, tile_cols // LANES
    plan = [[(c * col_size, col_size), (r * row_size, row_size)] for r in range(rows_n) for c in range(cols_n)]
    payload, error = run_network(plan)
    jac = exchange(payload, ("row", "col"))
    jac = jac.reshape(-1, *jac.shape[2:])
    hi, lo = stage(covariance)
    row_part, col_part = cross_partial(jac, error, hi, lo, slab)
    row_own, col_own = slab_sums(exchange(row_part, "col"), exchange(col_part, "row"))
    row_slabs, col_slabs = exchange(row_own, "col"), exchange(col_own, "row")
    new_weight, new_cov = update(row_slabs, col_slabs, layer_weight, covariance)
    return new_weight.reshape(-1), new_cov


def solution(mesh):
    in_specs = (
        P(("row", "col"), None),
        P(("row", "col"), None, None),
        P(("row", "col"), None, None),
        P(("row", "col"), None, None),
        P(("row", "col"), None),
        P(("row", "col")),
        P(),
        P(),
        P(),
        P("row", "col"),
    )
    out_specs = (P(("row", "col")), P("row", "col"))
    return jax.shard_map(
        on_device, mesh=mesh, in_specs=in_specs, out_specs=out_specs, check_vma=False
    )
```

```python
import functools
import math

import jax
import jax.numpy as jnp
from jax import lax
from jax.experimental import pallas as pl
from jax.experimental.pallas import tpu as pltpu
from jax.sharding import PartitionSpec as P

NEWTON = 4
LANES = 128
SUBLANES = 8


forget = 0.98
highest = lax.Precision.HIGHEST
f32 = jnp.float32
bf16 = jnp.bfloat16


def dot(left, right, contract, precision=None):
    return lax.dot_general(
        left, right, (contract, ((), ())), precision=precision, preferred_element_type=f32
    )


def split3(x):
    hi = x.astype(bf16)
    rest = x - hi.astype(f32)
    mid = rest.astype(bf16)
    lo = (rest - mid.astype(f32)).astype(bf16)
    return hi, mid, lo


def split2(x):
    hi = x.astype(bf16)
    return hi, (x - hi.astype(f32)).astype(bf16)


def network_kernel(
    types_ref,
    ids_ref,
    switch_ref,
    env_ref,
    force_ref,
    target_ref,
    embed_ref,
    weight_ref,
    out_weight_ref,
    payload_ref,
    error_ref,
    mix_ref,
    *,
    plan,
):
    neighbours, atoms = ids_ref.shape
    n_types = embed_ref.shape[0]
    height = min(64, atoms)
    for start in range(0, atoms, height):
        atom_at = lax.broadcasted_iota(jnp.int32, (height, atoms), 0) + start
        total = jnp.zeros((height, atoms), f32)
        for k in range(neighbours):
            total = total + jnp.where(ids_ref[k : k + 1, :] == atom_at, switch_ref[k : k + 1, :], 0.0)
        mix_ref[start : start + height, :] = total
    mix = mix_ref[...]
    type_at = lax.broadcasted_iota(jnp.int32, (n_types, atoms), 0)
    onehot = (types_ref[...] == type_at).astype(f32)
    mixed = env_ref[...] + dot(embed_ref[...], onehot, ((0,), (0,)), highest)
    descriptor = dot(mixed, mix, ((1,), (0,)), highest) * (1.0 / math.sqrt(neighbours))
    hidden = jnp.tanh(descriptor)
    activity = jnp.tanh(dot(hidden, weight_ref[...], ((0,), (0,)), highest))
    out_weight = out_weight_ref[...]
    scale = 1.0 / math.sqrt(atoms)
    force = force_ref[...]
    weighted = dot(force, activity, ((1,), (0,)), highest)
    predicted = jnp.sum(weighted * out_weight, axis=1, keepdims=True) * scale
    slopes = out_weight * (1.0 - activity * activity)
    jacobian = dot(hidden * force, slopes, ((1,), (0,)), highest) * scale
    error_ref[...] = jnp.broadcast_to(target_ref[...] - predicted, error_ref.shape)
    for block, pieces in enumerate(plan):
        at = 0
        for start, size in pieces:
            payload_ref[block, at : at + size, :] = jacobian[start : start + size, :]
            at += size


def network(
    plan, atom_types, neighbor_ids, switching, environment, force_weights, targets, type_embed, layer_weight, out_weight
):
    per_dev, neighbours, atoms = neighbor_ids.shape
    hin, width = layer_weight.shape
    blocks, rows = len(plan), sum(size for _, size in plan[0])

    def per_stream(*shape):
        return pl.BlockSpec((None,) + shape, lambda s: (s,) + (0,) * len(shape))

    def shared(shape):
        return pl.BlockSpec(shape, lambda s: (0,) * len(shape))

    return pl.pallas_call(
        functools.partial(network_kernel, plan=plan),
        grid=(per_dev,),
        in_specs=[
            per_stream(1, atoms),
            per_stream(neighbours, atoms),
            per_stream(neighbours, atoms),
            per_stream(hin, atoms),
            per_stream(1, atoms),
            per_stream(1, 1),
            shared(type_embed.shape),
            shared(layer_weight.shape),
            shared((1, width)),
        ],
        out_specs=[
            pl.BlockSpec((blocks, None, rows, width), lambda s: (0, s, 0, 0)),
            per_stream(1, width),
        ],
        out_shape=[
            jax.ShapeDtypeStruct((blocks, per_dev, rows, width), f32),
            jax.ShapeDtypeStruct((per_dev, 1, width), f32),
        ],
        scratch_shapes=[pltpu.VMEM((atoms, atoms), f32)],
        name="network",
    )(
        atom_types.reshape(per_dev, 1, atoms),
        neighbor_ids,
        switching,
        environment.swapaxes(1, 2),
        force_weights.reshape(per_dev, 1, atoms),
        targets.reshape(per_dev, 1, 1),
        type_embed,
        layer_weight,
        out_weight.reshape(1, width),
    )


def in_hbm(x):
    return pltpu.with_memory_space_constraint(x, pltpu.HBM)


def stage_kernel(cov_ref, hi_ref, lo_ref):
    hi_ref[...], lo_ref[...] = split2(cov_ref[...])


def stage(covariance):
    rows, cols = covariance.shape
    height = rows // 8
    block = pl.BlockSpec((height, cols), lambda n: (n, 0))
    return pl.pallas_call(
        stage_kernel,
        grid=(rows // height,),
        in_specs=[block],
        out_specs=[block] * 2,
        out_shape=[pltpu.HBM((rows, cols), bf16)] * 2,
        compiler_params=pltpu.CompilerParams(vmem_limit_bytes=16 << 20),
        name="stage",
    )(in_hbm(covariance))


def five_products(parts, hi, lo, contract):
    streams = parts.shape[0] // 3
    by_hi = dot(parts, hi, contract)
    by_lo = dot(parts[0 : 2 * streams], lo, contract)
    return by_hi[0:streams] + (
        by_hi[streams : 2 * streams] + by_lo[0:streams] + (by_hi[2 * streams :] + by_lo[streams:])
    )


def row_kernel(jac_ref, error_ref, hi_ref, lo_ref, cross_ref, beside_ref, parts_ref, term_ref, *, col_rows):
    streams, rows, lanes = jac_ref.shape
    slab = hi_ref.shape[0]
    slab_rows = slab // lanes
    step = pl.program_id(0)
    flat = jac_ref.reshape(streams * rows, lanes)

    @pl.when(step == 0)
    def _():
        term_ref[...] = jnp.zeros_like(term_ref)
        for i in range(col_rows):
            parts = split3(flat[pl.ds(i, streams, stride=rows), :])
            for n, part in enumerate(parts):
                parts_ref[n * streams : (n + 1) * streams, i * lanes : (i + 1) * lanes] = part

    cross = five_products(parts_ref[...], hi_ref[...], lo_ref[...], ((1,), (1,)))
    cross_ref[...] = cross
    term = jnp.zeros((streams, streams), f32)
    for i in range(slab_rows):
        own = flat[pl.ds(col_rows + step * slab_rows + i, streams, stride=rows), :]
        term = term + dot(own, cross[:, i * lanes : (i + 1) * lanes], ((1,), (1,)), highest)
    term_ref[:, 0:streams] += term

    @pl.when(step == pl.num_programs(0) - 1)
    def _():
        own_at = lax.axis_index("row") * lax.axis_size("col") + lax.axis_index("col")
        stream_at = lax.broadcasted_iota(jnp.int32, (streams, lanes), 0)
        lane_at = lax.broadcasted_iota(jnp.int32, (streams, lanes), 1)
        error = jnp.where((stream_at == own_at) & (lane_at >= streams), error_ref[0], 0.0)
        beside = term_ref[...] + error
        for n in range(beside_ref.shape[0]):
            beside_ref[n] = beside


def row_partial(jac, error, hi, lo, slab, copies):
    streams = jac.shape[0]
    tile_rows, tile_cols = hi.shape
    block = pl.BlockSpec((slab, tile_cols), lambda n: (n, 0))
    return pl.pallas_call(
        functools.partial(row_kernel, col_rows=tile_cols // LANES),
        grid=(tile_rows // slab,),
        in_specs=[
            pl.BlockSpec(jac.shape, lambda n: (0, 0, 0)),
            pl.BlockSpec(error.shape, lambda n: (0, 0, 0)),
            block,
            block,
        ],
        out_specs=[
            pl.BlockSpec((streams, slab), lambda n: (0, n)),
            pl.BlockSpec((copies, streams, LANES), lambda n: (0, 0, 0)),
        ],
        out_shape=[
            jax.ShapeDtypeStruct((streams, tile_rows), f32),
            jax.ShapeDtypeStruct((copies, streams, LANES), f32),
        ],
        scratch_shapes=[
            pltpu.VMEM((3 * streams, tile_cols), bf16),
            pltpu.VMEM((streams, LANES), f32),
        ],
        compiler_params=pltpu.CompilerParams(vmem_limit_bytes=16 << 20),
        name="row_cross",
    )(jac, error, in_hbm(hi), in_hbm(lo))


def col_kernel(jac_ref, hi_ref, lo_ref, out_ref, parts_ref, sum_ref, *, col_rows):
    streams, rows, lanes = jac_ref.shape
    slab, tile_cols = hi_ref.shape
    slab_rows = slab // lanes
    step = pl.program_id(0)
    flat = jac_ref.reshape(streams * rows, lanes)
    for i in range(slab_rows):
        parts = split3(flat[pl.ds(col_rows + step * slab_rows + i, streams, stride=rows), :])
        for n, part in enumerate(parts):
            parts_ref[n * streams : (n + 1) * streams, i * lanes : (i + 1) * lanes] = part
    cross = five_products(parts_ref[...], hi_ref[...], lo_ref[...], ((1,), (0,)))

    @pl.when(step == 0)
    def _():
        sum_ref[...] = cross

    @pl.when(step > 0)
    def _():
        sum_ref[...] += cross

    @pl.when(step == pl.num_programs(0) - 1)
    def _():
        for n in range(tile_cols // slab):
            out_ref[n] = sum_ref[:, n * slab : (n + 1) * slab]


def col_partial(jac, hi, lo, slab):
    streams = jac.shape[0]
    tile_rows, tile_cols = hi.shape
    out_shape = (tile_cols // slab, streams, slab)
    block = pl.BlockSpec((slab, tile_cols), lambda n: (n, 0))
    return pl.pallas_call(
        functools.partial(col_kernel, col_rows=tile_cols // LANES),
        grid=(tile_rows // slab,),
        in_specs=[pl.BlockSpec(jac.shape, lambda n: (0, 0, 0)), block, block],
        out_specs=pl.BlockSpec(out_shape, lambda n: (0, 0, 0)),
        out_shape=jax.ShapeDtypeStruct(out_shape, f32),
        scratch_shapes=[
            pltpu.VMEM((3 * streams, slab), bf16),
            pltpu.VMEM((streams, tile_cols), f32),
        ],
        compiler_params=pltpu.CompilerParams(vmem_limit_bytes=16 << 20),
        name="col_cross",
    )(jac, in_hbm(hi), in_hbm(lo))


def slab_kernel(pieces_ref, beside_ref, out_ref):
    slab = pieces_ref.shape[2]
    cross = pieces_ref[0]
    for n in range(1, pieces_ref.shape[0]):
        cross = cross + pieces_ref[n]
    beside = beside_ref[0]
    for n in range(1, beside_ref.shape[0]):
        beside = beside + beside_ref[n]
    out_ref[:, 0:slab] = cross
    out_ref[:, slab:] = beside


def slab_sum(pieces, beside):
    _, streams, slab = pieces.shape
    return pl.pallas_call(
        slab_kernel,
        out_shape=jax.ShapeDtypeStruct((streams, slab + LANES), f32),
        name="slab",
    )(pieces, beside)


def invert(innovation):
    streams = innovation.shape[0]
    row = lax.broadcasted_iota(jnp.int32, (streams, streams), 0)
    col = lax.broadcasted_iota(jnp.int32, (streams, streams), 1)
    identity = (row == col).astype(f32)
    innovation = innovation + forget * identity
    sums = jnp.sum(jnp.abs(innovation), axis=1, keepdims=True)
    bound = jnp.max(sums, axis=0, keepdims=True)
    power = identity - innovation / bound
    inverse = identity + power
    for repeat in range(NEWTON - 1):
        power = dot(power, power, ((1,), (0,)), highest)
        inverse = inverse + dot(inverse, power, ((1,), (0,)), highest)
    return inverse / bound


def update_kernel(
    rows_ref, cols_ref, weight_ref, cov_ref, new_weight_ref, new_cov_ref, right_ref, tile_ref, in_sems, out_sems
):
    streams, tile_rows = rows_ref.shape
    col_slabs, _, padded = cols_ref.shape
    lanes = weight_ref.shape[1]
    slab = padded - lanes
    slabs = tile_rows // slab
    reads = []
    for n in range(slabs):
        here = pl.ds(n * slab, slab)
        reads.append(pltpu.make_async_copy(cov_ref.at[here], tile_ref.at[here], in_sems.at[n]))
        reads[-1].start()
    beside = cols_ref[0, :, slab:]
    for n in range(1, col_slabs):
        beside = beside + cols_ref[n, :, slab:]
    inverse = invert(beside[:, 0:streams])
    errors = beside[:, streams : streams + 1]
    for n in range(col_slabs):
        hi, mid, lo = split3(cols_ref[n, :, 0:slab])
        for m, part in enumerate((hi, mid, lo, hi, mid, hi)):
            right_ref[m * streams : (m + 1) * streams, n * slab : (n + 1) * slab] = part
    col_at = lax.axis_index("col")
    own_at = (lax.axis_index("row") * slabs + col_at) * (slab // lanes)
    writes = []
    for n in range(slabs):
        gain = dot(inverse, rows_ref[:, n * slab : (n + 1) * slab], ((0,), (0,)), highest)
        hi, mid, lo = split3(gain)
        left = jnp.concatenate([hi, hi, hi, mid, mid, lo], axis=0)
        update = dot(left, right_ref[...], ((0,), (0,)))
        here = pl.ds(n * slab, slab)
        reads[n].wait()
        tile_ref[here, :] = (tile_ref[here, :] - update) * (1.0 / forget)
        writes.append(pltpu.make_async_copy(tile_ref.at[here], new_cov_ref.at[here], out_sems.at[n]))
        writes[-1].start()

        @pl.when(col_at == n)
        def _():
            moved = jnp.sum(gain * errors, axis=0, keepdims=True)
            for i in range(slab // lanes):
                own = weight_ref[pl.ds(own_at + i, 1), :]
                new_weight_ref[i : i + 1, :] = own + moved[:, i * lanes : (i + 1) * lanes]

    for write in writes:
        write.wait()


def update(row_cross, col_slabs, layer_weight, covariance):
    _, streams, padded = col_slabs.shape
    slab = padded - LANES
    tile_rows, tile_cols = covariance.shape
    slabs = tile_rows // slab
    width = layer_weight.shape[1]
    whole = pl.BlockSpec(memory_space=pltpu.VMEM)
    beyond = pl.BlockSpec(memory_space=pl.ANY)
    return pl.pallas_call(
        update_kernel,
        in_specs=[whole, whole, whole, beyond],
        out_specs=[whole, beyond],
        out_shape=[
            jax.ShapeDtypeStruct((slab // width, width), f32),
            jax.ShapeDtypeStruct((tile_rows, tile_cols), f32),
        ],
        scratch_shapes=[
            pltpu.VMEM((6 * streams, tile_cols), bf16),
            pltpu.VMEM((tile_rows, tile_cols), f32),
            pltpu.SemaphoreType.DMA((slabs,)),
            pltpu.SemaphoreType.DMA((slabs,)),
        ],
        compiler_params=pltpu.CompilerParams(vmem_limit_bytes=32 << 20),
        name="update",
    )(row_cross, col_slabs, layer_weight, in_hbm(covariance))


def plain_steps(at, jac_all, errors, layer_weight, covariance, slab, cols_n):
    streams = jac_all.shape[0]
    hin, width = layer_weight.shape
    tile_rows, tile_cols = covariance.shape
    first = (at[0] * cols_n + at[1]) * slab
    jacobian = jac_all[:, 0:hin, :].reshape(streams, hin * width)
    jac_cols = lax.dynamic_slice_in_dim(jacobian, at[1] * tile_cols, tile_cols, 1)
    partial = dot(jac_cols, covariance, ((1,), (1,)), highest)
    cross_own = lax.psum_scatter(partial, "col", scatter_dimension=1, tiled=True)
    cross = lax.all_gather(cross_own, ("row", "col"), axis=1, tiled=True)
    inverse = invert(dot(jacobian, cross, ((1,), (1,)), highest))
    gain = dot(inverse, lax.dynamic_slice_in_dim(cross, at[0] * tile_rows, tile_rows, 1), ((0,), (0,)), highest)
    across = lax.dynamic_slice_in_dim(cross, at[1] * tile_cols, tile_cols, 1)
    new_cov = (covariance - dot(gain, across, ((0,), (0,)), highest)) / forget
    own_gain = lax.dynamic_slice_in_dim(gain, at[1] * slab, slab, 1)
    own_weight = lax.dynamic_slice_in_dim(layer_weight.reshape(-1), first, slab, 0)
    new_weight = own_weight + dot(errors, own_gain, ((0,), (0,)), highest)
    return new_weight, new_cov


def exchange(x, axes):
    return lax.all_to_all(x, axes, split_axis=0, concat_axis=0, tiled=True)


def on_device(
    atom_types,
    neighbor_ids,
    switching,
    environment,
    force_weights,
    targets,
    type_embed,
    layer_weight,
    out_weight,
    covariance,
):
    rows_n = lax.axis_size("row")
    cols_n = lax.axis_size("col")
    at = jnp.stack([lax.axis_index("row"), lax.axis_index("col")]).astype(jnp.int32)
    tile_rows, tile_cols = covariance.shape
    slab = tile_rows // cols_n
    hin, width = layer_weight.shape
    run_network = functools.partial(
        network,
        atom_types=atom_types,
        neighbor_ids=neighbor_ids,
        switching=switching,
        environment=environment,
        force_weights=force_weights,
        targets=targets,
        type_embed=type_embed,
        layer_weight=layer_weight,
        out_weight=out_weight,
    )
    streams = rows_n * cols_n * atom_types.shape[0]
    kernels = (
        atom_types.shape[0] == 1
        and width == LANES
        and slab % LANES == 0
        and tile_rows % (SUBLANES * LANES) == 0
        and tile_cols % (SUBLANES * LANES) == 0
        and rows_n * slab == tile_cols
        and streams < LANES
    )
    if not kernels:
        payload, error = run_network([[(0, hin)]])
        jac_all = lax.all_gather(payload[0], ("row", "col"), axis=0, tiled=True)
        errors = lax.all_gather(error[:, 0, 0], ("row", "col"), axis=0, tiled=True)
        return plain_steps(at, jac_all, errors, layer_weight, covariance, slab, cols_n)
    row_size, col_size = tile_rows // LANES, tile_cols // LANES
    plan = [[(c * col_size, col_size), (r * row_size, row_size)] for r in range(rows_n) for c in range(cols_n)]
    payload, error = run_network(plan)
    jac = exchange(payload, ("row", "col"))
    jac = jac.reshape(-1, *jac.shape[2:])
    hi, lo = stage(covariance)
    row_part, beside = row_partial(jac, error, hi, lo, slab, cols_n)
    row_cross = lax.psum(row_part, "col")
    beside = exchange(beside, "col")
    col_pieces = exchange(col_partial(jac, hi, lo, slab), "row")
    col_slabs = lax.all_gather(slab_sum(col_pieces, beside), "row", axis=0, tiled=False)
    new_weight, new_cov = update(row_cross, col_slabs, layer_weight, covariance)
    return new_weight.reshape(-1), new_cov


def solution(mesh):
    in_specs = (
        P(("row", "col"), None),
        P(("row", "col"), None, None),
        P(("row", "col"), None, None),
        P(("row", "col"), None, None),
        P(("row", "col"), None),
        P(("row", "col")),
        P(),
        P(),
        P(),
        P("row", "col"),
    )
    out_specs = (P(("row", "col")), P("row", "col"))
    return jax.shard_map(
        on_device, mesh=mesh, in_specs=in_specs, out_specs=out_specs, check_vma=False
    )
```

```python
import functools
import math

import jax
import jax.numpy as jnp
from jax import lax
from jax.experimental import pallas as pl
from jax.experimental.pallas import tpu as pltpu
from jax.sharding import PartitionSpec as P

NEWTON = 4
LANES = 128
SUBLANES = 8


forget = 0.98
highest = lax.Precision.HIGHEST
f32 = jnp.float32
bf16 = jnp.bfloat16


def dot(left, right, contract, precision=None):
    return lax.dot_general(
        left, right, (contract, ((), ())), precision=precision, preferred_element_type=f32
    )


def split3(x):
    hi = x.astype(bf16)
    rest = x - hi.astype(f32)
    mid = rest.astype(bf16)
    lo = (rest - mid.astype(f32)).astype(bf16)
    return hi, mid, lo


def split2(x):
    hi = x.astype(bf16)
    return hi, (x - hi.astype(f32)).astype(bf16)


def network_kernel(
    types_ref,
    ids_ref,
    switch_ref,
    env_ref,
    force_ref,
    target_ref,
    embed_ref,
    weight_ref,
    out_weight_ref,
    payload_ref,
    error_ref,
    mix_ref,
    *,
    plan,
):
    neighbours, atoms = ids_ref.shape
    n_types = embed_ref.shape[0]
    height = min(64, atoms)
    for start in range(0, atoms, height):
        atom_at = lax.broadcasted_iota(jnp.int32, (height, atoms), 0) + start
        total = jnp.zeros((height, atoms), f32)
        for k in range(neighbours):
            total = total + jnp.where(ids_ref[k : k + 1, :] == atom_at, switch_ref[k : k + 1, :], 0.0)
        mix_ref[start : start + height, :] = total
    mix = mix_ref[...]
    type_at = lax.broadcasted_iota(jnp.int32, (n_types, atoms), 0)
    onehot = (types_ref[...] == type_at).astype(f32)
    mixed = env_ref[...] + dot(embed_ref[...], onehot, ((0,), (0,)), highest)
    descriptor = dot(mixed, mix, ((1,), (0,)), highest) * (1.0 / math.sqrt(neighbours))
    hidden = jnp.tanh(descriptor)
    activity = jnp.tanh(dot(hidden, weight_ref[...], ((0,), (0,)), highest))
    out_weight = out_weight_ref[...]
    scale = 1.0 / math.sqrt(atoms)
    force = force_ref[...]
    weighted = dot(force, activity, ((1,), (0,)), highest)
    predicted = jnp.sum(weighted * out_weight, axis=1, keepdims=True) * scale
    slopes = out_weight * (1.0 - activity * activity)
    jacobian = dot(hidden * force, slopes, ((1,), (0,)), highest) * scale
    error_ref[...] = jnp.broadcast_to(target_ref[...] - predicted, error_ref.shape)
    for block, pieces in enumerate(plan):
        at = 0
        for start, size in pieces:
            payload_ref[block, at : at + size, :] = jacobian[start : start + size, :]
            at += size


def network(
    plan, atom_types, neighbor_ids, switching, environment, force_weights, targets, type_embed, layer_weight, out_weight
):
    per_dev, neighbours, atoms = neighbor_ids.shape
    hin, width = layer_weight.shape
    blocks, rows = len(plan), sum(size for _, size in plan[0])

    def per_stream(*shape):
        return pl.BlockSpec((None,) + shape, lambda s: (s,) + (0,) * len(shape))

    def shared(shape):
        return pl.BlockSpec(shape, lambda s: (0,) * len(shape))

    return pl.pallas_call(
        functools.partial(network_kernel, plan=plan),
        grid=(per_dev,),
        in_specs=[
            per_stream(1, atoms),
            per_stream(neighbours, atoms),
            per_stream(neighbours, atoms),
            per_stream(hin, atoms),
            per_stream(1, atoms),
            per_stream(1, 1),
            shared(type_embed.shape),
            shared(layer_weight.shape),
            shared((1, width)),
        ],
        out_specs=[
            pl.BlockSpec((blocks, None, rows, width), lambda s: (0, s, 0, 0)),
            per_stream(1, width),
        ],
        out_shape=[
            jax.ShapeDtypeStruct((blocks, per_dev, rows, width), f32),
            jax.ShapeDtypeStruct((per_dev, 1, width), f32),
        ],
        scratch_shapes=[pltpu.VMEM((atoms, atoms), f32)],
        name="network",
    )(
        atom_types.reshape(per_dev, 1, atoms),
        neighbor_ids,
        switching,
        environment.swapaxes(1, 2),
        force_weights.reshape(per_dev, 1, atoms),
        targets.reshape(per_dev, 1, 1),
        type_embed,
        layer_weight,
        out_weight.reshape(1, width),
    )


def in_hbm(x):
    return pltpu.with_memory_space_constraint(x, pltpu.HBM)


def stage_kernel(cov_ref, hi_ref, lo_ref):
    hi_ref[...], lo_ref[...] = split2(cov_ref[...])


def stage(covariance):
    rows, cols = covariance.shape
    height = rows // 8
    block = pl.BlockSpec((height, cols), lambda n: (n, 0))
    return pl.pallas_call(
        stage_kernel,
        grid=(rows // height,),
        in_specs=[block],
        out_specs=[block] * 2,
        out_shape=[pltpu.HBM((rows, cols), bf16)] * 2,
        compiler_params=pltpu.CompilerParams(vmem_limit_bytes=16 << 20),
        name="stage",
    )(in_hbm(covariance))


def five_products(parts, hi, lo, contract):
    streams = parts.shape[0] // 3
    by_hi = dot(parts, hi, contract)
    by_lo = dot(parts[0 : 2 * streams], lo, contract)
    return by_hi[0:streams] + (
        by_hi[streams : 2 * streams] + by_lo[0:streams] + (by_hi[2 * streams :] + by_lo[streams:])
    )


def stacked_parts(flat, first, count, streams, stride, into_ref):
    lanes = flat.shape[1]
    for i in range(count):
        parts = split3(flat[pl.ds(first + i, streams, stride=stride), :])
        for n, part in enumerate(parts):
            into_ref[n * streams : (n + 1) * streams, i * lanes : (i + 1) * lanes] = part


def col_kernel(jac_ref, error_ref, hi_ref, lo_ref, out_ref, parts_ref, sum_ref, *, col_rows):
    streams, rows, lanes = jac_ref.shape
    slab, tile_cols = hi_ref.shape
    slab_rows = slab // lanes
    step = pl.program_id(0)
    flat = jac_ref.reshape(streams * rows, lanes)
    stacked_parts(flat, col_rows + step * slab_rows, slab_rows, streams, rows, parts_ref.at[:, 0:slab])
    cross = five_products(parts_ref[:, 0:slab], hi_ref[...], lo_ref[...], ((1,), (0,)))

    @pl.when(step == 0)
    def _():
        sum_ref[...] = cross

    @pl.when(step > 0)
    def _():
        sum_ref[...] += cross

    @pl.when(step == pl.num_programs(0) - 1)
    def _():
        stacked_parts(flat, 0, col_rows, streams, rows, parts_ref)
        total = sum_ref[...]
        products = dot(parts_ref[...], jnp.concatenate(split3(total), axis=0), ((1,), (1,)))
        term = jnp.zeros((streams, streams), f32)
        for left, right in ((2, 0), (1, 1), (0, 2), (1, 0), (0, 1), (0, 0)):
            term = term + products[
                left * streams : (left + 1) * streams, right * streams : (right + 1) * streams
            ]
        own_at = lax.axis_index("row") * lax.axis_size("col") + lax.axis_index("col")
        stream_at = lax.broadcasted_iota(jnp.int32, (streams, lanes), 0)
        error = jnp.where(stream_at == own_at, error_ref[0], 0.0)
        for n in range(tile_cols // slab):
            out_ref[n, :, 0:slab] = total[:, n * slab : (n + 1) * slab]
            out_ref[n, :, slab:] = error
            out_ref[n, :, slab : slab + streams] = term


def col_partial(jac, error, hi, lo, slab):
    streams = jac.shape[0]
    tile_rows, tile_cols = hi.shape
    out_shape = (tile_cols // slab, streams, slab + LANES)
    block = pl.BlockSpec((slab, tile_cols), lambda n: (n, 0))
    return pl.pallas_call(
        functools.partial(col_kernel, col_rows=tile_cols // LANES),
        grid=(tile_rows // slab,),
        in_specs=[
            pl.BlockSpec(jac.shape, lambda n: (0, 0, 0)),
            pl.BlockSpec(error.shape, lambda n: (0, 0, 0)),
            block,
            block,
        ],
        out_specs=pl.BlockSpec(out_shape, lambda n: (0, 0, 0)),
        out_shape=jax.ShapeDtypeStruct(out_shape, f32),
        scratch_shapes=[
            pltpu.VMEM((3 * streams, tile_cols), bf16),
            pltpu.VMEM((streams, tile_cols), f32),
        ],
        compiler_params=pltpu.CompilerParams(vmem_limit_bytes=16 << 20),
        name="col_cross",
    )(jac, error, in_hbm(hi), in_hbm(lo))


def row_kernel(jac_ref, hi_ref, lo_ref, cross_ref, parts_ref):
    streams, rows, lanes = jac_ref.shape
    flat = jac_ref.reshape(streams * rows, lanes)

    @pl.when(pl.program_id(0) == 0)
    def _():
        stacked_parts(flat, 0, hi_ref.shape[1] // lanes, streams, rows, parts_ref)

    cross_ref[...] = five_products(parts_ref[...], hi_ref[...], lo_ref[...], ((1,), (1,)))


def row_partial(jac, hi, lo, slab):
    streams = jac.shape[0]
    tile_rows, tile_cols = hi.shape
    block = pl.BlockSpec((slab, tile_cols), lambda n: (n, 0))
    return pl.pallas_call(
        row_kernel,
        grid=(tile_rows // slab,),
        in_specs=[pl.BlockSpec(jac.shape, lambda n: (0, 0, 0)), block, block],
        out_specs=pl.BlockSpec((streams, slab), lambda n: (0, n)),
        out_shape=jax.ShapeDtypeStruct((streams, tile_rows), f32),
        scratch_shapes=[pltpu.VMEM((3 * streams, tile_cols), bf16)],
        compiler_params=pltpu.CompilerParams(vmem_limit_bytes=16 << 20),
        name="row_cross",
    )(jac, in_hbm(hi), in_hbm(lo))


def slab_kernel(pieces_ref, row_ref, own_ref, out_ref):
    tile_rows = row_ref.shape[1]
    slab = own_ref.shape[1]
    total = pieces_ref[0]
    for n in range(1, pieces_ref.shape[0]):
        total = total + pieces_ref[n]
    own_ref[...] = total[:, 0:slab]
    for n in range(out_ref.shape[0]):
        out_ref[n, :, 0:tile_rows] = row_ref[...]
        out_ref[n, :, tile_rows:] = total[:, slab:]


def slab_sum(pieces, row_part, copies):
    _, streams, padded = pieces.shape
    tile_rows = row_part.shape[1]
    return pl.pallas_call(
        slab_kernel,
        out_shape=[
            jax.ShapeDtypeStruct((streams, padded - LANES), f32),
            jax.ShapeDtypeStruct((copies, streams, tile_rows + LANES), f32),
        ],
        name="slab",
    )(pieces, row_part)


def invert(innovation):
    streams = innovation.shape[0]
    row = lax.broadcasted_iota(jnp.int32, (streams, streams), 0)
    col = lax.broadcasted_iota(jnp.int32, (streams, streams), 1)
    identity = (row == col).astype(f32)
    innovation = innovation + forget * identity
    sums = jnp.sum(jnp.abs(innovation), axis=1, keepdims=True)
    bound = jnp.max(sums, axis=0, keepdims=True)
    power = identity - innovation / bound
    inverse = identity + power
    for repeat in range(NEWTON - 1):
        power = dot(power, power, ((1,), (0,)), highest)
        inverse = inverse + dot(inverse, power, ((1,), (0,)), highest)
    return inverse / bound


def update_kernel(
    rows_ref, cols_ref, weight_ref, cov_ref, new_weight_ref, new_cov_ref, right_ref, tile_ref, in_sems, out_sems
):
    copies, streams, padded = rows_ref.shape
    col_slabs, _, slab = cols_ref.shape
    lanes = weight_ref.shape[1]
    tile_rows = padded - lanes
    slabs = tile_rows // slab
    reads = []
    for n in range(slabs):
        here = pl.ds(n * slab, slab)
        reads.append(pltpu.make_async_copy(cov_ref.at[here], tile_ref.at[here], in_sems.at[n]))
        reads[-1].start()
    total = rows_ref[0]
    for n in range(1, copies):
        total = total + rows_ref[n]
    beside = total[:, tile_rows:]
    inverse = invert(beside[:, 0:streams])
    errors = beside[:, streams : streams + 1]
    for n in range(col_slabs):
        hi, mid, lo = split3(cols_ref[n])
        for m, part in enumerate((hi, mid, lo, hi, mid, hi)):
            right_ref[m * streams : (m + 1) * streams, n * slab : (n + 1) * slab] = part
    col_at = lax.axis_index("col")
    own_at = (lax.axis_index("row") * slabs + col_at) * (slab // lanes)
    writes = []
    for n in range(slabs):
        gain = dot(inverse, total[:, n * slab : (n + 1) * slab], ((0,), (0,)), highest)
        hi, mid, lo = split3(gain)
        left = jnp.concatenate([hi, hi, hi, mid, mid, lo], axis=0)
        update = dot(left, right_ref[...], ((0,), (0,)))
        here = pl.ds(n * slab, slab)
        reads[n].wait()
        tile_ref[here, :] = (tile_ref[here, :] - update) * (1.0 / forget)
        writes.append(pltpu.make_async_copy(tile_ref.at[here], new_cov_ref.at[here], out_sems.at[n]))
        writes[-1].start()

        @pl.when(col_at == n)
        def _():
            moved = jnp.sum(gain * errors, axis=0, keepdims=True)
            for i in range(slab // lanes):
                own = weight_ref[pl.ds(own_at + i, 1), :]
                new_weight_ref[i : i + 1, :] = own + moved[:, i * lanes : (i + 1) * lanes]

    for write in writes:
        write.wait()


def update(row_parts, col_slabs, layer_weight, covariance):
    _, streams, slab = col_slabs.shape
    tile_rows, tile_cols = covariance.shape
    slabs = tile_rows // slab
    width = layer_weight.shape[1]
    whole = pl.BlockSpec(memory_space=pltpu.VMEM)
    beyond = pl.BlockSpec(memory_space=pl.ANY)
    return pl.pallas_call(
        update_kernel,
        in_specs=[whole, whole, whole, beyond],
        out_specs=[whole, beyond],
        out_shape=[
            jax.ShapeDtypeStruct((slab // width, width), f32),
            jax.ShapeDtypeStruct((tile_rows, tile_cols), f32),
        ],
        scratch_shapes=[
            pltpu.VMEM((6 * streams, tile_cols), bf16),
            pltpu.VMEM((tile_rows, tile_cols), f32),
            pltpu.SemaphoreType.DMA((slabs,)),
            pltpu.SemaphoreType.DMA((slabs,)),
        ],
        compiler_params=pltpu.CompilerParams(vmem_limit_bytes=32 << 20),
        name="update",
    )(row_parts, col_slabs, layer_weight, in_hbm(covariance))


def plain_steps(at, jac_all, errors, layer_weight, covariance, slab, cols_n):
    streams = jac_all.shape[0]
    hin, width = layer_weight.shape
    tile_rows, tile_cols = covariance.shape
    first = (at[0] * cols_n + at[1]) * slab
    jacobian = jac_all[:, 0:hin, :].reshape(streams, hin * width)
    jac_cols = lax.dynamic_slice_in_dim(jacobian, at[1] * tile_cols, tile_cols, 1)
    partial = dot(jac_cols, covariance, ((1,), (1,)), highest)
    cross_own = lax.psum_scatter(partial, "col", scatter_dimension=1, tiled=True)
    cross = lax.all_gather(cross_own, ("row", "col"), axis=1, tiled=True)
    inverse = invert(dot(jacobian, cross, ((1,), (1,)), highest))
    gain = dot(inverse, lax.dynamic_slice_in_dim(cross, at[0] * tile_rows, tile_rows, 1), ((0,), (0,)), highest)
    across = lax.dynamic_slice_in_dim(cross, at[1] * tile_cols, tile_cols, 1)
    new_cov = (covariance - dot(gain, across, ((0,), (0,)), highest)) / forget
    own_gain = lax.dynamic_slice_in_dim(gain, at[1] * slab, slab, 1)
    own_weight = lax.dynamic_slice_in_dim(layer_weight.reshape(-1), first, slab, 0)
    new_weight = own_weight + dot(errors, own_gain, ((0,), (0,)), highest)
    return new_weight, new_cov


def exchange(x, axes):
    return lax.all_to_all(x, axes, split_axis=0, concat_axis=0, tiled=True)


def on_device(
    atom_types,
    neighbor_ids,
    switching,
    environment,
    force_weights,
    targets,
    type_embed,
    layer_weight,
    out_weight,
    covariance,
):
    rows_n = lax.axis_size("row")
    cols_n = lax.axis_size("col")
    at = jnp.stack([lax.axis_index("row"), lax.axis_index("col")]).astype(jnp.int32)
    tile_rows, tile_cols = covariance.shape
    slab = tile_rows // cols_n
    hin, width = layer_weight.shape
    run_network = functools.partial(
        network,
        atom_types=atom_types,
        neighbor_ids=neighbor_ids,
        switching=switching,
        environment=environment,
        force_weights=force_weights,
        targets=targets,
        type_embed=type_embed,
        layer_weight=layer_weight,
        out_weight=out_weight,
    )
    streams = rows_n * cols_n * atom_types.shape[0]
    kernels = (
        atom_types.shape[0] == 1
        and width == LANES
        and slab % LANES == 0
        and tile_rows % (SUBLANES * LANES) == 0
        and tile_cols % (SUBLANES * LANES) == 0
        and rows_n * slab == tile_cols
        and streams < LANES
    )
    if not kernels:
        payload, error = run_network([[(0, hin)]])
        jac_all = lax.all_gather(payload[0], ("row", "col"), axis=0, tiled=True)
        errors = lax.all_gather(error[:, 0, 0], ("row", "col"), axis=0, tiled=True)
        return plain_steps(at, jac_all, errors, layer_weight, covariance, slab, cols_n)
    row_size, col_size = tile_rows // LANES, tile_cols // LANES
    plan = [[(c * col_size, col_size), (r * row_size, row_size)] for r in range(rows_n) for c in range(cols_n)]
    payload, error = run_network(plan)
    jac = exchange(payload, ("row", "col"))
    jac = jac.reshape(-1, *jac.shape[2:])
    hi, lo = stage(covariance)
    col_pieces = exchange(col_partial(jac, error, hi, lo, slab), "row")
    row_part = row_partial(jac, hi, lo, slab)
    col_own, row_part = slab_sum(col_pieces, row_part, cols_n)
    row_parts = exchange(row_part, "col")
    col_slabs = lax.all_gather(col_own, "row", axis=0, tiled=False)
    new_weight, new_cov = update(row_parts, col_slabs, layer_weight, covariance)
    return new_weight.reshape(-1), new_cov


def solution(mesh):
    in_specs = (
        P(("row", "col"), None),
        P(("row", "col"), None, None),
        P(("row", "col"), None, None),
        P(("row", "col"), None, None),
        P(("row", "col"), None),
        P(("row", "col")),
        P(),
        P(),
        P(),
        P("row", "col"),
    )
    out_specs = (P(("row", "col")), P("row", "col"))
    return jax.shard_map(
        on_device, mesh=mesh, in_specs=in_specs, out_specs=out_specs, check_vma=False
    )
```

```python
import functools
import math

import jax
import jax.numpy as jnp
from jax import lax
from jax.experimental import pallas as pl
from jax.experimental.pallas import tpu as pltpu
from jax.sharding import PartitionSpec as P

NEWTON = 4
LANES = 128
SUBLANES = 8


forget = 0.98
highest = lax.Precision.HIGHEST
f32 = jnp.float32
bf16 = jnp.bfloat16


def dot(left, right, contract, precision=None):
    return lax.dot_general(
        left, right, (contract, ((), ())), precision=precision, preferred_element_type=f32
    )


def split3(x):
    hi = x.astype(bf16)
    rest = x - hi.astype(f32)
    mid = rest.astype(bf16)
    lo = (rest - mid.astype(f32)).astype(bf16)
    return hi, mid, lo


def split2(x):
    hi = x.astype(bf16)
    return hi, (x - hi.astype(f32)).astype(bf16)


def network_kernel(
    types_ref,
    ids_ref,
    switch_ref,
    env_ref,
    force_ref,
    target_ref,
    embed_ref,
    weight_ref,
    out_weight_ref,
    payload_ref,
    error_ref,
    mix_ref,
    *,
    plan,
):
    neighbours, atoms = ids_ref.shape
    n_types = embed_ref.shape[0]
    height = min(64, atoms)
    for start in range(0, atoms, height):
        atom_at = lax.broadcasted_iota(jnp.int32, (height, atoms), 0) + start
        total = jnp.zeros((height, atoms), f32)
        for k in range(neighbours):
            total = total + jnp.where(ids_ref[k : k + 1, :] == atom_at, switch_ref[k : k + 1, :], 0.0)
        mix_ref[start : start + height, :] = total
    mix = mix_ref[...]
    type_at = lax.broadcasted_iota(jnp.int32, (n_types, atoms), 0)
    onehot = (types_ref[...] == type_at).astype(f32)
    mixed = env_ref[...] + dot(embed_ref[...], onehot, ((0,), (0,)), highest)
    descriptor = dot(mixed, mix, ((1,), (0,)), highest) * (1.0 / math.sqrt(neighbours))
    hidden = jnp.tanh(descriptor)
    activity = jnp.tanh(dot(hidden, weight_ref[...], ((0,), (0,)), highest))
    out_weight = out_weight_ref[...]
    scale = 1.0 / math.sqrt(atoms)
    force = force_ref[...]
    weighted = dot(force, activity, ((1,), (0,)), highest)
    predicted = jnp.sum(weighted * out_weight, axis=1, keepdims=True) * scale
    slopes = out_weight * (1.0 - activity * activity)
    jacobian = dot(hidden * force, slopes, ((1,), (0,)), highest) * scale
    error_ref[...] = jnp.broadcast_to(target_ref[...] - predicted, error_ref.shape)
    for block, pieces in enumerate(plan):
        at = 0
        for start, size in pieces:
            payload_ref[block, at : at + size, :] = jacobian[start : start + size, :]
            at += size


def network(
    plan, atom_types, neighbor_ids, switching, environment, force_weights, targets, type_embed, layer_weight, out_weight
):
    per_dev, neighbours, atoms = neighbor_ids.shape
    hin, width = layer_weight.shape
    blocks, rows = len(plan), sum(size for _, size in plan[0])

    def per_stream(*shape):
        return pl.BlockSpec((None,) + shape, lambda s: (s,) + (0,) * len(shape))

    def shared(shape):
        return pl.BlockSpec(shape, lambda s: (0,) * len(shape))

    return pl.pallas_call(
        functools.partial(network_kernel, plan=plan),
        grid=(per_dev,),
        in_specs=[
            per_stream(1, atoms),
            per_stream(neighbours, atoms),
            per_stream(neighbours, atoms),
            per_stream(hin, atoms),
            per_stream(1, atoms),
            per_stream(1, 1),
            shared(type_embed.shape),
            shared(layer_weight.shape),
            shared((1, width)),
        ],
        out_specs=[
            pl.BlockSpec((blocks, None, rows, width), lambda s: (0, s, 0, 0)),
            per_stream(1, width),
        ],
        out_shape=[
            jax.ShapeDtypeStruct((blocks, per_dev, rows, width), f32),
            jax.ShapeDtypeStruct((per_dev, 1, width), f32),
        ],
        scratch_shapes=[pltpu.VMEM((atoms, atoms), f32)],
        name="network",
    )(
        atom_types.reshape(per_dev, 1, atoms),
        neighbor_ids,
        switching,
        environment.swapaxes(1, 2),
        force_weights.reshape(per_dev, 1, atoms),
        targets.reshape(per_dev, 1, 1),
        type_embed,
        layer_weight,
        out_weight.reshape(1, width),
    )


def in_hbm(x):
    return pltpu.with_memory_space_constraint(x, pltpu.HBM)


def stage_kernel(cov_ref, hi_ref, lo_ref):
    hi_ref[...], lo_ref[...] = split2(cov_ref[...])


def stage(covariance):
    rows, cols = covariance.shape
    height = rows // 8
    block = pl.BlockSpec((height, cols), lambda n: (n, 0))
    return pl.pallas_call(
        stage_kernel,
        grid=(rows // height,),
        in_specs=[block],
        out_specs=[block] * 2,
        out_shape=[pltpu.HBM((rows, cols), bf16)] * 2,
        compiler_params=pltpu.CompilerParams(vmem_limit_bytes=16 << 20),
        name="stage",
    )(in_hbm(covariance))


def five_products(parts, hi, lo, contract):
    streams = parts.shape[0] // 3
    by_hi = dot(parts, hi, contract)
    by_lo = dot(parts[0 : 2 * streams], lo, contract)
    return by_hi[0:streams] + (
        by_hi[streams : 2 * streams] + by_lo[0:streams] + (by_hi[2 * streams :] + by_lo[streams:])
    )


def stacked_parts(flat, first, count, streams, stride, into_ref):
    lanes = flat.shape[1]
    for i in range(count):
        parts = split3(flat[pl.ds(first + i, streams, stride=stride), :])
        for n, part in enumerate(parts):
            into_ref[n * streams : (n + 1) * streams, i * lanes : (i + 1) * lanes] = part


def col_kernel(jac_ref, error_ref, hi_ref, lo_ref, out_ref, parts_ref, own_ref, term_ref, *, col_rows):
    streams, rows, lanes = jac_ref.shape
    slab = hi_ref.shape[1]
    slab_rows = slab // lanes
    step = pl.program_id(0)
    flat = jac_ref.reshape(streams * rows, lanes)

    @pl.when(step == 0)
    def _():
        stacked_parts(flat, col_rows, rows - col_rows, streams, rows, parts_ref)
        term_ref[...] = jnp.zeros_like(term_ref)

    cross = five_products(parts_ref[...], hi_ref[...], lo_ref[...], ((1,), (0,)))
    out_ref[step, :, 0:slab] = cross
    stacked_parts(flat, step * slab_rows, slab_rows, streams, rows, own_ref)
    term_ref[...] += dot(own_ref[...], jnp.concatenate(split3(cross), axis=0), ((1,), (1,)))

    @pl.when(step == pl.num_programs(0) - 1)
    def _():
        term = jnp.zeros((streams, streams), f32)
        for left, right in ((2, 0), (1, 1), (0, 2), (1, 0), (0, 1), (0, 0)):
            term = term + term_ref[
                left * streams : (left + 1) * streams, right * streams : (right + 1) * streams
            ]
        own_at = lax.axis_index("row") * lax.axis_size("col") + lax.axis_index("col")
        stream_at = lax.broadcasted_iota(jnp.int32, (streams, lanes), 0)
        error = jnp.where(stream_at == own_at, error_ref[0], 0.0)
        for n in range(out_ref.shape[0]):
            out_ref[n, :, slab:] = error
            out_ref[n, :, slab : slab + streams] = term


def col_partial(jac, error, hi, lo, slab):
    streams = jac.shape[0]
    tile_rows, tile_cols = hi.shape
    out_shape = (tile_cols // slab, streams, slab + LANES)
    block = pl.BlockSpec((tile_rows, slab), lambda n: (0, n))
    return pl.pallas_call(
        functools.partial(col_kernel, col_rows=tile_cols // LANES),
        grid=(tile_cols // slab,),
        in_specs=[
            pl.BlockSpec(jac.shape, lambda n: (0, 0, 0)),
            pl.BlockSpec(error.shape, lambda n: (0, 0, 0)),
            block,
            block,
        ],
        out_specs=pl.BlockSpec(out_shape, lambda n: (0, 0, 0)),
        out_shape=jax.ShapeDtypeStruct(out_shape, f32),
        scratch_shapes=[
            pltpu.VMEM((3 * streams, tile_rows), bf16),
            pltpu.VMEM((3 * streams, slab), bf16),
            pltpu.VMEM((3 * streams, 3 * streams), f32),
        ],
        compiler_params=pltpu.CompilerParams(vmem_limit_bytes=16 << 20),
        name="col_cross",
    )(jac, error, in_hbm(hi), in_hbm(lo))


def row_kernel(jac_ref, hi_ref, lo_ref, cross_ref, parts_ref):
    streams, rows, lanes = jac_ref.shape
    flat = jac_ref.reshape(streams * rows, lanes)

    @pl.when(pl.program_id(0) == 0)
    def _():
        stacked_parts(flat, 0, hi_ref.shape[1] // lanes, streams, rows, parts_ref)

    cross = five_products(parts_ref[...], hi_ref[...], lo_ref[...], ((1,), (1,)))
    for n in range(cross_ref.shape[0]):
        cross_ref[n] = cross


def row_partial(jac, hi, lo, slab, copies):
    streams = jac.shape[0]
    tile_rows, tile_cols = hi.shape
    block = pl.BlockSpec((slab, tile_cols), lambda n: (n, 0))
    return pl.pallas_call(
        row_kernel,
        grid=(tile_rows // slab,),
        in_specs=[pl.BlockSpec(jac.shape, lambda n: (0, 0, 0)), block, block],
        out_specs=pl.BlockSpec((copies, streams, slab), lambda n: (0, 0, n)),
        out_shape=pltpu.HBM((copies, streams, tile_rows + LANES), f32),
        scratch_shapes=[pltpu.VMEM((3 * streams, tile_cols), bf16)],
        compiler_params=pltpu.CompilerParams(vmem_limit_bytes=16 << 20),
        name="row_cross",
    )(jac, in_hbm(hi), in_hbm(lo))


def slab_kernel(pieces_ref, _, own_ref, out_ref, beside_ref, sems):
    lanes = beside_ref.shape[1]
    slab = own_ref.shape[1]
    copies = out_ref.shape[0]
    beside = pieces_ref[0, :, slab:]
    for n in range(1, pieces_ref.shape[0]):
        beside = beside + pieces_ref[n, :, slab:]
    beside_ref[...] = beside
    writes = []
    for n in range(copies):
        place = out_ref.at[n, :, pl.ds(out_ref.shape[2] - lanes, lanes)]
        writes.append(pltpu.make_async_copy(beside_ref, place, sems.at[n]))
        writes[-1].start()
    total = pieces_ref[0, :, 0:slab]
    for n in range(1, pieces_ref.shape[0]):
        total = total + pieces_ref[n, :, 0:slab]
    own_ref[...] = total
    for write in writes:
        write.wait()


def slab_sum(pieces, row_part):
    _, streams, padded = pieces.shape
    whole = pl.BlockSpec(memory_space=pltpu.VMEM)
    beyond = pl.BlockSpec(memory_space=pl.ANY)
    return pl.pallas_call(
        slab_kernel,
        in_specs=[whole, beyond],
        out_specs=[whole, beyond],
        out_shape=[
            jax.ShapeDtypeStruct((streams, padded - LANES), f32),
            pltpu.HBM(row_part.shape, f32),
        ],
        scratch_shapes=[
            pltpu.VMEM((streams, LANES), f32),
            pltpu.SemaphoreType.DMA((row_part.shape[0],)),
        ],
        input_output_aliases={1: 1},
        name="slab",
    )(in_hbm(pieces), in_hbm(row_part))


def invert(innovation):
    streams = innovation.shape[0]
    row = lax.broadcasted_iota(jnp.int32, (streams, streams), 0)
    col = lax.broadcasted_iota(jnp.int32, (streams, streams), 1)
    identity = (row == col).astype(f32)
    innovation = innovation + forget * identity
    sums = jnp.sum(jnp.abs(innovation), axis=1, keepdims=True)
    bound = jnp.max(sums, axis=0, keepdims=True)
    power = identity - innovation / bound
    inverse = identity + power
    for repeat in range(NEWTON - 1):
        power = dot(power, power, ((1,), (0,)), highest)
        inverse = inverse + dot(inverse, power, ((1,), (0,)), highest)
    return inverse / bound


def update_kernel(
    rows_ref, cols_ref, weight_ref, cov_ref, new_weight_ref, new_cov_ref, left_ref, right_ref, tile_ref, in_sems, out_sems
):
    copies, streams, padded = rows_ref.shape
    col_slabs, _, slab = cols_ref.shape
    lanes = weight_ref.shape[1]
    tile_rows = padded - lanes
    slabs = tile_rows // slab
    chunks = in_sems.shape[0]
    height = tile_rows // chunks
    reads = []
    for n in range(chunks):
        here = pl.ds(n * height, height)
        reads.append(pltpu.make_async_copy(cov_ref.at[here], tile_ref.at[here], in_sems.at[n]))
        reads[-1].start()
    total = rows_ref[0]
    for n in range(1, copies):
        total = total + rows_ref[n]
    beside = total[:, tile_rows:]
    inverse = invert(beside[:, 0:streams])
    errors = beside[:, streams : streams + 1]
    for n in range(col_slabs):
        hi, mid, lo = split3(cols_ref[n])
        for m, part in enumerate((hi, mid, lo, hi, mid, hi)):
            right_ref[m * streams : (m + 1) * streams, n * slab : (n + 1) * slab] = part
    gain = dot(inverse, total[:, 0:tile_rows], ((0,), (0,)), highest)
    hi, mid, lo = split3(gain)
    for m, part in enumerate((hi, hi, hi, mid, mid, lo)):
        left_ref[m * streams : (m + 1) * streams, :] = part
    writes = []
    for n in range(chunks):
        update = dot(left_ref[:, n * height : (n + 1) * height], right_ref[...], ((0,), (0,)))
        here = pl.ds(n * height, height)
        reads[n].wait()
        tile_ref[here, :] = (tile_ref[here, :] - update) * (1.0 / forget)
        writes.append(pltpu.make_async_copy(tile_ref.at[here], new_cov_ref.at[here], out_sems.at[n]))
        writes[-1].start()
    col_at = lax.axis_index("col")
    own_at = (lax.axis_index("row") * slabs + col_at) * (slab // lanes)
    for n in range(slabs):

        @pl.when(col_at == n)
        def _():
            moved = jnp.sum(gain[:, n * slab : (n + 1) * slab] * errors, axis=0, keepdims=True)
            for i in range(slab // lanes):
                own = weight_ref[pl.ds(own_at + i, 1), :]
                new_weight_ref[i : i + 1, :] = own + moved[:, i * lanes : (i + 1) * lanes]

    for write in writes:
        write.wait()


def update(row_parts, col_slabs, layer_weight, covariance):
    _, streams, slab = col_slabs.shape
    tile_rows, tile_cols = covariance.shape
    width = layer_weight.shape[1]
    whole = pl.BlockSpec(memory_space=pltpu.VMEM)
    beyond = pl.BlockSpec(memory_space=pl.ANY)
    return pl.pallas_call(
        update_kernel,
        in_specs=[whole, whole, whole, beyond],
        out_specs=[whole, beyond],
        out_shape=[
            jax.ShapeDtypeStruct((slab // width, width), f32),
            jax.ShapeDtypeStruct((tile_rows, tile_cols), f32),
        ],
        scratch_shapes=[
            pltpu.VMEM((6 * streams, tile_rows), bf16),
            pltpu.VMEM((6 * streams, tile_cols), bf16),
            pltpu.VMEM((tile_rows, tile_cols), f32),
            pltpu.SemaphoreType.DMA((8,)),
            pltpu.SemaphoreType.DMA((8,)),
        ],
        compiler_params=pltpu.CompilerParams(vmem_limit_bytes=32 << 20),
        name="update",
    )(row_parts, col_slabs, layer_weight, in_hbm(covariance))


def plain_steps(at, jac_all, errors, layer_weight, covariance, slab, cols_n):
    streams = jac_all.shape[0]
    hin, width = layer_weight.shape
    tile_rows, tile_cols = covariance.shape
    first = (at[0] * cols_n + at[1]) * slab
    jacobian = jac_all[:, 0:hin, :].reshape(streams, hin * width)
    jac_cols = lax.dynamic_slice_in_dim(jacobian, at[1] * tile_cols, tile_cols, 1)
    partial = dot(jac_cols, covariance, ((1,), (1,)), highest)
    cross_own = lax.psum_scatter(partial, "col", scatter_dimension=1, tiled=True)
    cross = lax.all_gather(cross_own, ("row", "col"), axis=1, tiled=True)
    inverse = invert(dot(jacobian, cross, ((1,), (1,)), highest))
    gain = dot(inverse, lax.dynamic_slice_in_dim(cross, at[0] * tile_rows, tile_rows, 1), ((0,), (0,)), highest)
    across = lax.dynamic_slice_in_dim(cross, at[1] * tile_cols, tile_cols, 1)
    new_cov = (covariance - dot(gain, across, ((0,), (0,)), highest)) / forget
    own_gain = lax.dynamic_slice_in_dim(gain, at[1] * slab, slab, 1)
    own_weight = lax.dynamic_slice_in_dim(layer_weight.reshape(-1), first, slab, 0)
    new_weight = own_weight + dot(errors, own_gain, ((0,), (0,)), highest)
    return new_weight, new_cov


def exchange(x, axes):
    return lax.all_to_all(x, axes, split_axis=0, concat_axis=0, tiled=True)


def on_device(
    atom_types,
    neighbor_ids,
    switching,
    environment,
    force_weights,
    targets,
    type_embed,
    layer_weight,
    out_weight,
    covariance,
):
    rows_n = lax.axis_size("row")
    cols_n = lax.axis_size("col")
    at = jnp.stack([lax.axis_index("row"), lax.axis_index("col")]).astype(jnp.int32)
    tile_rows, tile_cols = covariance.shape
    slab = tile_rows // cols_n
    hin, width = layer_weight.shape
    run_network = functools.partial(
        network,
        atom_types=atom_types,
        neighbor_ids=neighbor_ids,
        switching=switching,
        environment=environment,
        force_weights=force_weights,
        targets=targets,
        type_embed=type_embed,
        layer_weight=layer_weight,
        out_weight=out_weight,
    )
    streams = rows_n * cols_n * atom_types.shape[0]
    kernels = (
        atom_types.shape[0] == 1
        and width == LANES
        and slab % LANES == 0
        and tile_rows % (SUBLANES * LANES) == 0
        and tile_cols % (SUBLANES * LANES) == 0
        and rows_n * slab == tile_cols
        and streams < LANES
    )
    if not kernels:
        payload, error = run_network([[(0, hin)]])
        jac_all = lax.all_gather(payload[0], ("row", "col"), axis=0, tiled=True)
        errors = lax.all_gather(error[:, 0, 0], ("row", "col"), axis=0, tiled=True)
        return plain_steps(at, jac_all, errors, layer_weight, covariance, slab, cols_n)
    row_size, col_size = tile_rows // LANES, tile_cols // LANES
    plan = [[(c * col_size, col_size), (r * row_size, row_size)] for r in range(rows_n) for c in range(cols_n)]
    payload, error = run_network(plan)
    jac = exchange(payload, ("row", "col"))
    jac = jac.reshape(-1, *jac.shape[2:])
    hi, lo = stage(covariance)
    col_pieces = exchange(col_partial(jac, error, hi, lo, slab), "row")
    row_part = row_partial(jac, hi, lo, slab, cols_n)
    col_own, row_part = slab_sum(col_pieces, row_part)
    row_parts = exchange(row_part, "col")
    col_slabs = lax.all_gather(col_own, "row", axis=0, tiled=False)
    new_weight, new_cov = update(row_parts, col_slabs, layer_weight, covariance)
    return new_weight.reshape(-1), new_cov


def solution(mesh):
    in_specs = (
        P(("row", "col"), None),
        P(("row", "col"), None, None),
        P(("row", "col"), None, None),
        P(("row", "col"), None, None),
        P(("row", "col"), None),
        P(("row", "col")),
        P(),
        P(),
        P(),
        P("row", "col"),
    )
    out_specs = (P(("row", "col")), P("row", "col"))
    return jax.shard_map(
        on_device, mesh=mesh, in_specs=in_specs, out_specs=out_specs, check_vma=False
    )
```

```python
import functools
import math

import jax
import jax.numpy as jnp
from jax import lax
from jax.experimental import pallas as pl
from jax.experimental.pallas import tpu as pltpu
from jax.sharding import PartitionSpec as P

NEWTON = 4
LANES = 128
SUBLANES = 8


forget = 0.98
highest = lax.Precision.HIGHEST
f32 = jnp.float32
bf16 = jnp.bfloat16


def dot(left, right, contract, precision=None):
    return lax.dot_general(
        left, right, (contract, ((), ())), precision=precision, preferred_element_type=f32
    )


def split3(x):
    hi = x.astype(bf16)
    rest = x - hi.astype(f32)
    mid = rest.astype(bf16)
    lo = (rest - mid.astype(f32)).astype(bf16)
    return hi, mid, lo


def split2(x):
    hi = x.astype(bf16)
    return hi, (x - hi.astype(f32)).astype(bf16)


def limit(mib):
    return pltpu.CompilerParams(vmem_limit_bytes=mib << 20)


def network_kernel(
    types_ref,
    ids_ref,
    switch_ref,
    env_ref,
    force_ref,
    target_ref,
    embed_ref,
    weight_ref,
    out_weight_ref,
    payload_ref,
    error_ref,
    mix_ref,
    *,
    plan,
):
    neighbours, atoms = ids_ref.shape
    n_types = embed_ref.shape[0]
    height = min(64, atoms)
    for start in range(0, atoms, height):
        atom_at = lax.broadcasted_iota(jnp.int32, (height, atoms), 0) + start
        total = jnp.zeros((height, atoms), f32)
        for k in range(neighbours):
            total = total + jnp.where(ids_ref[k : k + 1, :] == atom_at, switch_ref[k : k + 1, :], 0.0)
        mix_ref[start : start + height, :] = total
    mix = mix_ref[...]
    type_at = lax.broadcasted_iota(jnp.int32, (n_types, atoms), 0)
    onehot = (types_ref[...] == type_at).astype(f32)
    mixed = env_ref[...] + dot(embed_ref[...], onehot, ((0,), (0,)), highest)
    descriptor = dot(mixed, mix, ((1,), (0,)), highest) * (1.0 / math.sqrt(neighbours))
    hidden = jnp.tanh(descriptor)
    activity = jnp.tanh(dot(hidden, weight_ref[...], ((0,), (0,)), highest))
    out_weight = out_weight_ref[...]
    scale = 1.0 / math.sqrt(atoms)
    force = force_ref[...]
    weighted = dot(force, activity, ((1,), (0,)), highest)
    predicted = jnp.sum(weighted * out_weight, axis=1, keepdims=True) * scale
    slopes = out_weight * (1.0 - activity * activity)
    jacobian = dot(hidden * force, slopes, ((1,), (0,)), highest) * scale
    error_ref[...] = jnp.broadcast_to(target_ref[...] - predicted, error_ref.shape)
    for block, pieces in enumerate(plan):
        at = 0
        for start, size in pieces:
            payload_ref[block, at : at + size, :] = jacobian[start : start + size, :]
            at += size


def network(
    plan, atom_types, neighbor_ids, switching, environment, force_weights, targets, type_embed, layer_weight, out_weight
):
    per_dev, neighbours, atoms = neighbor_ids.shape
    hin, width = layer_weight.shape
    blocks, rows = len(plan), sum(size for _, size in plan[0])

    def per_stream(*shape):
        return pl.BlockSpec((None,) + shape, lambda s: (s,) + (0,) * len(shape))

    def shared(shape):
        return pl.BlockSpec(shape, lambda s: (0,) * len(shape))

    return pl.pallas_call(
        functools.partial(network_kernel, plan=plan),
        grid=(per_dev,),
        in_specs=[
            per_stream(1, atoms),
            per_stream(neighbours, atoms),
            per_stream(neighbours, atoms),
            per_stream(hin, atoms),
            per_stream(1, atoms),
            per_stream(1, 1),
            shared(type_embed.shape),
            shared(layer_weight.shape),
            shared((1, width)),
        ],
        out_specs=[
            pl.BlockSpec((blocks, None, rows, width), lambda s: (0, s, 0, 0)),
            per_stream(1, width),
        ],
        out_shape=[
            jax.ShapeDtypeStruct((blocks, per_dev, rows, width), f32),
            jax.ShapeDtypeStruct((per_dev, 1, width), f32),
        ],
        scratch_shapes=[pltpu.VMEM((atoms, atoms), f32)],
        compiler_params=limit(8),
        name="network",
    )(
        atom_types.reshape(per_dev, 1, atoms),
        neighbor_ids,
        switching,
        environment.swapaxes(1, 2),
        force_weights.reshape(per_dev, 1, atoms),
        targets.reshape(per_dev, 1, 1),
        type_embed,
        layer_weight,
        out_weight.reshape(1, width),
    )


def stage_kernel(cov_ref, hi_ref, lo_ref):
    hi_ref[...], lo_ref[...] = split2(cov_ref[...])


def stage(covariance):
    rows, cols = covariance.shape
    height = rows // 8
    block = pl.BlockSpec((height, cols), lambda n: (n, 0))
    return pl.pallas_call(
        stage_kernel,
        grid=(rows // height,),
        in_specs=[block],
        out_specs=[block] * 2,
        out_shape=[jax.ShapeDtypeStruct((rows, cols), bf16)] * 2,
        compiler_params=limit(12),
        name="stage",
    )(covariance)


def five_products(parts, hi, lo, contract):
    streams = parts.shape[0] // 3
    by_hi = dot(parts, hi, contract)
    by_lo = dot(parts[0 : 2 * streams], lo, contract)
    return by_hi[0:streams] + (
        by_hi[streams : 2 * streams] + by_lo[0:streams] + (by_hi[2 * streams :] + by_lo[streams:])
    )


def stacked_parts(flat, first, count, streams, stride, into_ref):
    lanes = flat.shape[1]
    for i in range(count):
        parts = split3(flat[pl.ds(first + i, streams, stride=stride), :])
        for n, part in enumerate(parts):
            into_ref[n * streams : (n + 1) * streams, i * lanes : (i + 1) * lanes] = part


def col_kernel(jac_ref, error_ref, hi_ref, lo_ref, out_ref, parts_ref, own_ref, sum_ref, *, col_rows):
    streams, rows, lanes = jac_ref.shape
    slab, tile_cols = hi_ref.shape
    slab_rows = slab // lanes
    step = pl.program_id(0)
    flat = jac_ref.reshape(streams * rows, lanes)
    stacked_parts(flat, col_rows + step * slab_rows, slab_rows, streams, rows, own_ref)
    cross = five_products(own_ref[...], hi_ref[...], lo_ref[...], ((1,), (0,)))

    @pl.when(step == 0)
    def _():
        sum_ref[...] = cross
        stacked_parts(flat, 0, col_rows, streams, rows, parts_ref)

    @pl.when(step > 0)
    def _():
        sum_ref[...] += cross

    @pl.when(step == pl.num_programs(0) - 1)
    def _():
        total = sum_ref[...]
        products = dot(parts_ref[...], jnp.concatenate(split3(total), axis=0), ((1,), (1,)))
        term = jnp.zeros((streams, streams), f32)
        for left, right in ((2, 0), (1, 1), (0, 2), (1, 0), (0, 1), (0, 0)):
            term = term + products[
                left * streams : (left + 1) * streams, right * streams : (right + 1) * streams
            ]
        own_at = lax.axis_index("row") * lax.axis_size("col") + lax.axis_index("col")
        stream_at = lax.broadcasted_iota(jnp.int32, (streams, lanes), 0)
        error = jnp.where(stream_at == own_at, error_ref[0], 0.0)
        for n in range(tile_cols // slab):
            out_ref[n, :, 0:slab] = total[:, n * slab : (n + 1) * slab]
            out_ref[n, :, slab:] = error
            out_ref[n, :, slab : slab + streams] = term


def col_partial(jac, error, hi, lo, slab):
    streams = jac.shape[0]
    tile_rows, tile_cols = hi.shape
    out_shape = (tile_cols // slab, streams, slab + LANES)
    block = pl.BlockSpec((slab, tile_cols), lambda n: (n, 0))
    return pl.pallas_call(
        functools.partial(col_kernel, col_rows=tile_cols // LANES),
        grid=(tile_rows // slab,),
        in_specs=[
            pl.BlockSpec(jac.shape, lambda n: (0, 0, 0)),
            pl.BlockSpec(error.shape, lambda n: (0, 0, 0)),
            block,
            block,
        ],
        out_specs=pl.BlockSpec(out_shape, lambda n: (0, 0, 0)),
        out_shape=jax.ShapeDtypeStruct(out_shape, f32),
        scratch_shapes=[
            pltpu.VMEM((3 * streams, tile_cols), bf16),
            pltpu.VMEM((3 * streams, slab), bf16),
            pltpu.VMEM((streams, tile_cols), f32),
        ],
        compiler_params=limit(12),
        name="col_cross",
    )(jac, error, hi, lo)


def row_kernel(jac_ref, hi_ref, lo_ref, cross_ref, parts_ref):
    streams, rows, lanes = jac_ref.shape
    flat = jac_ref.reshape(streams * rows, lanes)

    @pl.when(pl.program_id(0) == 0)
    def _():
        stacked_parts(flat, 0, hi_ref.shape[1] // lanes, streams, rows, parts_ref)

    cross_ref[...] = five_products(parts_ref[...], hi_ref[...], lo_ref[...], ((1,), (1,)))


def row_partial(jac, hi, lo, slab):
    streams = jac.shape[0]
    tile_rows, tile_cols = hi.shape
    block = pl.BlockSpec((slab, tile_cols), lambda n: (n, 0))
    return pl.pallas_call(
        row_kernel,
        grid=(tile_rows // slab,),
        in_specs=[pl.BlockSpec(jac.shape, lambda n: (0, 0, 0)), block, block],
        out_specs=pl.BlockSpec((streams, slab), lambda n: (0, n)),
        out_shape=jax.ShapeDtypeStruct((streams, tile_rows), f32),
        scratch_shapes=[pltpu.VMEM((3 * streams, tile_cols), bf16)],
        compiler_params=limit(12),
        name="row_cross",
    )(jac, hi, lo)


def slab_kernel(pieces_ref, row_ref, own_ref, out_ref):
    tile_rows = row_ref.shape[1]
    slab = own_ref.shape[1]
    total = pieces_ref[0]
    for n in range(1, pieces_ref.shape[0]):
        total = total + pieces_ref[n]
    own_ref[...] = total[:, 0:slab]
    for n in range(out_ref.shape[0]):
        out_ref[n, :, 0:tile_rows] = row_ref[...]
        out_ref[n, :, tile_rows:] = total[:, slab:]


def slab_sum(pieces, row_part, copies):
    _, streams, padded = pieces.shape
    tile_rows = row_part.shape[1]
    return pl.pallas_call(
        slab_kernel,
        out_shape=[
            jax.ShapeDtypeStruct((streams, padded - LANES), f32),
            jax.ShapeDtypeStruct((copies, streams, tile_rows + LANES), f32),
        ],
        compiler_params=limit(8),
        name="slab",
    )(pieces, row_part)


def invert(innovation):
    streams = innovation.shape[0]
    row = lax.broadcasted_iota(jnp.int32, (streams, streams), 0)
    col = lax.broadcasted_iota(jnp.int32, (streams, streams), 1)
    identity = (row == col).astype(f32)
    innovation = innovation + forget * identity
    sums = jnp.sum(jnp.abs(innovation), axis=1, keepdims=True)
    bound = jnp.max(sums, axis=0, keepdims=True)
    power = identity - innovation / bound
    inverse = identity + power
    for repeat in range(NEWTON - 1):
        power = dot(power, power, ((1,), (0,)), highest)
        inverse = inverse + dot(inverse, power, ((1,), (0,)), highest)
    return inverse / bound


def update_kernel(
    rows_ref, cols_ref, weight_ref, cov_ref, new_weight_ref, new_cov_ref, left_ref, right_ref, tile_ref, in_sems, out_sems
):
    copies, streams, padded = rows_ref.shape
    col_slabs, _, slab = cols_ref.shape
    lanes = weight_ref.shape[1]
    tile_rows = padded - lanes
    slabs = tile_rows // slab
    chunks = in_sems.shape[0]
    height = tile_rows // chunks
    reads = []
    for n in range(chunks):
        here = pl.ds(n * height, height)
        reads.append(pltpu.make_async_copy(cov_ref.at[here], tile_ref.at[here], in_sems.at[n]))
        reads[-1].start()
    total = rows_ref[0]
    for n in range(1, copies):
        total = total + rows_ref[n]
    beside = total[:, tile_rows:]
    inverse = invert(beside[:, 0:streams])
    errors = beside[:, streams : streams + 1]
    for n in range(col_slabs):
        hi, mid, lo = split3(cols_ref[n])
        for m, part in enumerate((hi, mid, lo, hi, mid, hi)):
            right_ref[m * streams : (m + 1) * streams, n * slab : (n + 1) * slab] = part
    gain = dot(inverse, total[:, 0:tile_rows], ((0,), (0,)), highest)
    hi, mid, lo = split3(gain)
    for m, part in enumerate((hi, hi, hi, mid, mid, lo)):
        left_ref[m * streams : (m + 1) * streams, :] = part
    writes = []
    for n in range(chunks):
        update = dot(left_ref[:, n * height : (n + 1) * height], right_ref[...], ((0,), (0,)))
        here = pl.ds(n * height, height)
        reads[n].wait()
        tile_ref[here, :] = (tile_ref[here, :] - update) * (1.0 / forget)
        writes.append(pltpu.make_async_copy(tile_ref.at[here], new_cov_ref.at[here], out_sems.at[n]))
        writes[-1].start()
    col_at = lax.axis_index("col")
    own_at = (lax.axis_index("row") * slabs + col_at) * (slab // lanes)
    for n in range(slabs):

        @pl.when(col_at == n)
        def _():
            moved = jnp.sum(gain[:, n * slab : (n + 1) * slab] * errors, axis=0, keepdims=True)
            for i in range(slab // lanes):
                own = weight_ref[pl.ds(own_at + i, 1), :]
                new_weight_ref[i : i + 1, :] = own + moved[:, i * lanes : (i + 1) * lanes]

    for write in writes:
        write.wait()


def update(row_parts, col_slabs, layer_weight, covariance):
    _, streams, slab = col_slabs.shape
    tile_rows, tile_cols = covariance.shape
    width = layer_weight.shape[1]
    whole = pl.BlockSpec(memory_space=pltpu.VMEM)
    beyond = pl.BlockSpec(memory_space=pl.ANY)
    return pl.pallas_call(
        update_kernel,
        in_specs=[whole, whole, whole, beyond],
        out_specs=[whole, beyond],
        out_shape=[
            jax.ShapeDtypeStruct((slab // width, width), f32),
            jax.ShapeDtypeStruct((tile_rows, tile_cols), f32),
        ],
        scratch_shapes=[
            pltpu.VMEM((6 * streams, tile_rows), bf16),
            pltpu.VMEM((6 * streams, tile_cols), bf16),
            pltpu.VMEM((tile_rows, tile_cols), f32),
            pltpu.SemaphoreType.DMA((8,)),
            pltpu.SemaphoreType.DMA((8,)),
        ],
        compiler_params=limit(20),
        name="update",
    )(row_parts, col_slabs, layer_weight, covariance)


def plain_steps(at, jac_all, errors, layer_weight, covariance, slab, cols_n):
    streams = jac_all.shape[0]
    hin, width = layer_weight.shape
    tile_rows, tile_cols = covariance.shape
    first = (at[0] * cols_n + at[1]) * slab
    jacobian = jac_all[:, 0:hin, :].reshape(streams, hin * width)
    jac_cols = lax.dynamic_slice_in_dim(jacobian, at[1] * tile_cols, tile_cols, 1)
    partial = dot(jac_cols, covariance, ((1,), (1,)), highest)
    cross_own = lax.psum_scatter(partial, "col", scatter_dimension=1, tiled=True)
    cross = lax.all_gather(cross_own, ("row", "col"), axis=1, tiled=True)
    inverse = invert(dot(jacobian, cross, ((1,), (1,)), highest))
    gain = dot(inverse, lax.dynamic_slice_in_dim(cross, at[0] * tile_rows, tile_rows, 1), ((0,), (0,)), highest)
    across = lax.dynamic_slice_in_dim(cross, at[1] * tile_cols, tile_cols, 1)
    new_cov = (covariance - dot(gain, across, ((0,), (0,)), highest)) / forget
    own_gain = lax.dynamic_slice_in_dim(gain, at[1] * slab, slab, 1)
    own_weight = lax.dynamic_slice_in_dim(layer_weight.reshape(-1), first, slab, 0)
    new_weight = own_weight + dot(errors, own_gain, ((0,), (0,)), highest)
    return new_weight, new_cov


def exchange(x, axes):
    return lax.all_to_all(x, axes, split_axis=0, concat_axis=0, tiled=True)


def on_device(
    atom_types,
    neighbor_ids,
    switching,
    environment,
    force_weights,
    targets,
    type_embed,
    layer_weight,
    out_weight,
    covariance,
):
    rows_n = lax.axis_size("row")
    cols_n = lax.axis_size("col")
    at = jnp.stack([lax.axis_index("row"), lax.axis_index("col")]).astype(jnp.int32)
    tile_rows, tile_cols = covariance.shape
    slab = tile_rows // cols_n
    hin, width = layer_weight.shape
    run_network = functools.partial(
        network,
        atom_types=atom_types,
        neighbor_ids=neighbor_ids,
        switching=switching,
        environment=environment,
        force_weights=force_weights,
        targets=targets,
        type_embed=type_embed,
        layer_weight=layer_weight,
        out_weight=out_weight,
    )
    streams = rows_n * cols_n * atom_types.shape[0]
    kernels = (
        atom_types.shape[0] == 1
        and width == LANES
        and slab % LANES == 0
        and tile_rows % (SUBLANES * LANES) == 0
        and tile_cols % (SUBLANES * LANES) == 0
        and rows_n * slab == tile_cols
        and streams < LANES
    )
    if not kernels:
        payload, error = run_network([[(0, hin)]])
        jac_all = lax.all_gather(payload[0], ("row", "col"), axis=0, tiled=True)
        errors = lax.all_gather(error[:, 0, 0], ("row", "col"), axis=0, tiled=True)
        return plain_steps(at, jac_all, errors, layer_weight, covariance, slab, cols_n)
    row_size, col_size = tile_rows // LANES, tile_cols // LANES
    plan = [[(c * col_size, col_size), (r * row_size, row_size)] for r in range(rows_n) for c in range(cols_n)]
    payload, error = run_network(plan)
    jac = exchange(payload, ("row", "col"))
    jac = jac.reshape(-1, *jac.shape[2:])
    hi, lo = stage(covariance)
    col_pieces = exchange(col_partial(jac, error, hi, lo, slab), "row")
    row_part = row_partial(jac, hi, lo, slab)
    col_own, row_part = slab_sum(col_pieces, row_part, cols_n)
    row_parts = exchange(row_part, "col")
    col_slabs = lax.all_gather(col_own, "row", axis=0, tiled=False)
    new_weight, new_cov = update(row_parts, col_slabs, layer_weight, covariance)
    return new_weight.reshape(-1), new_cov


def solution(mesh):
    in_specs = (
        P(("row", "col"), None),
        P(("row", "col"), None, None),
        P(("row", "col"), None, None),
        P(("row", "col"), None, None),
        P(("row", "col"), None),
        P(("row", "col")),
        P(),
        P(),
        P(),
        P("row", "col"),
    )
    out_specs = (P(("row", "col")), P("row", "col"))
    return jax.shard_map(
        on_device, mesh=mesh, in_specs=in_specs, out_specs=out_specs, check_vma=False
    )
```

```python
import functools
import math

import jax
import jax.numpy as jnp
from jax import lax
from jax.experimental import pallas as pl
from jax.experimental.pallas import tpu as pltpu
from jax.sharding import PartitionSpec as P

NEWTON = 4
LANES = 128
SUBLANES = 8


forget = 0.98
highest = lax.Precision.HIGHEST
f32 = jnp.float32
bf16 = jnp.bfloat16


def dot(left, right, contract, precision=None):
    return lax.dot_general(
        left, right, (contract, ((), ())), precision=precision, preferred_element_type=f32
    )


def split3(x):
    hi = x.astype(bf16)
    rest = x - hi.astype(f32)
    mid = rest.astype(bf16)
    lo = (rest - mid.astype(f32)).astype(bf16)
    return hi, mid, lo


def split2(x):
    hi = x.astype(bf16)
    return hi, (x - hi.astype(f32)).astype(bf16)


def limit(mib):
    return pltpu.CompilerParams(vmem_limit_bytes=mib << 20)


def network_kernel(
    types_ref,
    ids_ref,
    switch_ref,
    env_ref,
    force_ref,
    target_ref,
    embed_ref,
    weight_ref,
    out_weight_ref,
    payload_ref,
    error_ref,
    mix_ref,
    *,
    plan,
):
    neighbours, atoms = ids_ref.shape
    n_types = embed_ref.shape[0]
    height = min(64, atoms)
    for start in range(0, atoms, height):
        atom_at = lax.broadcasted_iota(jnp.int32, (height, atoms), 0) + start
        total = jnp.zeros((height, atoms), f32)
        for k in range(neighbours):
            total = total + jnp.where(ids_ref[k : k + 1, :] == atom_at, switch_ref[k : k + 1, :], 0.0)
        mix_ref[start : start + height, :] = total
    mix = mix_ref[...]
    type_at = lax.broadcasted_iota(jnp.int32, (n_types, atoms), 0)
    onehot = (types_ref[...] == type_at).astype(f32)
    mixed = env_ref[...] + dot(embed_ref[...], onehot, ((0,), (0,)), highest)
    descriptor = dot(mixed, mix, ((1,), (0,)), highest) * (1.0 / math.sqrt(neighbours))
    hidden = jnp.tanh(descriptor)
    activity = jnp.tanh(dot(hidden, weight_ref[...], ((0,), (0,)), highest))
    out_weight = out_weight_ref[...]
    scale = 1.0 / math.sqrt(atoms)
    force = force_ref[...]
    weighted = dot(force, activity, ((1,), (0,)), highest)
    predicted = jnp.sum(weighted * out_weight, axis=1, keepdims=True) * scale
    slopes = out_weight * (1.0 - activity * activity)
    jacobian = dot(hidden * force, slopes, ((1,), (0,)), highest) * scale
    error_ref[...] = jnp.broadcast_to(target_ref[...] - predicted, error_ref.shape)
    for block, pieces in enumerate(plan):
        at = 0
        for start, size in pieces:
            payload_ref[block, at : at + size, :] = jacobian[start : start + size, :]
            at += size


def network(
    plan, atom_types, neighbor_ids, switching, environment, force_weights, targets, type_embed, layer_weight, out_weight
):
    per_dev, neighbours, atoms = neighbor_ids.shape
    hin, width = layer_weight.shape
    blocks, rows = len(plan), sum(size for _, size in plan[0])

    def per_stream(*shape):
        return pl.BlockSpec((None,) + shape, lambda s: (s,) + (0,) * len(shape))

    def shared(shape):
        return pl.BlockSpec(shape, lambda s: (0,) * len(shape))

    return pl.pallas_call(
        functools.partial(network_kernel, plan=plan),
        grid=(per_dev,),
        in_specs=[
            per_stream(1, atoms),
            per_stream(neighbours, atoms),
            per_stream(neighbours, atoms),
            per_stream(hin, atoms),
            per_stream(1, atoms),
            per_stream(1, 1),
            shared(type_embed.shape),
            shared(layer_weight.shape),
            shared((1, width)),
        ],
        out_specs=[
            pl.BlockSpec((blocks, None, rows, width), lambda s: (0, s, 0, 0)),
            per_stream(1, width),
        ],
        out_shape=[
            jax.ShapeDtypeStruct((blocks, per_dev, rows, width), f32),
            jax.ShapeDtypeStruct((per_dev, 1, width), f32),
        ],
        scratch_shapes=[pltpu.VMEM((atoms, atoms), f32)],
        name="network",
    )(
        atom_types.reshape(per_dev, 1, atoms),
        neighbor_ids,
        switching,
        environment.swapaxes(1, 2),
        force_weights.reshape(per_dev, 1, atoms),
        targets.reshape(per_dev, 1, 1),
        type_embed,
        layer_weight,
        out_weight.reshape(1, width),
    )


def in_hbm(x):
    return pltpu.with_memory_space_constraint(x, pltpu.HBM)


def in_vmem(x):
    return pltpu.with_memory_space_constraint(x, pltpu.VMEM)


def stage_kernel(cov_ref, hi_ref, lo_ref):
    hi_ref[...], lo_ref[...] = split2(cov_ref[...])


def stage(covariance):
    rows, cols = covariance.shape
    height = rows // 8
    block = pl.BlockSpec((height, cols), lambda n: (n, 0))
    return pl.pallas_call(
        stage_kernel,
        grid=(rows // height,),
        in_specs=[block],
        out_specs=[block] * 2,
        out_shape=[pltpu.HBM((rows, cols), bf16)] * 2,
        compiler_params=limit(12),
        name="stage",
    )(in_hbm(covariance))


def five_products(parts, hi, lo, contract):
    streams = parts.shape[0] // 3
    by_hi = dot(parts, hi, contract)
    by_lo = dot(parts[0 : 2 * streams], lo, contract)
    return by_hi[0:streams] + (
        by_hi[streams : 2 * streams] + by_lo[0:streams] + (by_hi[2 * streams :] + by_lo[streams:])
    )


def stacked_parts(flat, first, count, streams, stride, into_ref):
    lanes = flat.shape[1]
    for i in range(count):
        parts = split3(flat[pl.ds(first + i, streams, stride=stride), :])
        for n, part in enumerate(parts):
            into_ref[n * streams : (n + 1) * streams, i * lanes : (i + 1) * lanes] = part


def col_kernel(jac_ref, error_ref, hi_ref, lo_ref, out_ref, parts_ref, own_ref, sum_ref, *, col_rows):
    streams, rows, lanes = jac_ref.shape
    slab, tile_cols = hi_ref.shape
    slab_rows = slab // lanes
    step = pl.program_id(0)
    flat = jac_ref.reshape(streams * rows, lanes)
    stacked_parts(flat, col_rows + step * slab_rows, slab_rows, streams, rows, own_ref)
    cross = five_products(own_ref[...], hi_ref[...], lo_ref[...], ((1,), (0,)))

    @pl.when(step == 0)
    def _():
        sum_ref[...] = cross
        stacked_parts(flat, 0, col_rows, streams, rows, parts_ref)

    @pl.when(step > 0)
    def _():
        sum_ref[...] += cross

    @pl.when(step == pl.num_programs(0) - 1)
    def _():
        total = sum_ref[...]
        products = dot(parts_ref[...], jnp.concatenate(split3(total), axis=0), ((1,), (1,)))
        term = jnp.zeros((streams, streams), f32)
        for left, right in ((2, 0), (1, 1), (0, 2), (1, 0), (0, 1), (0, 0)):
            term = term + products[
                left * streams : (left + 1) * streams, right * streams : (right + 1) * streams
            ]
        own_at = lax.axis_index("row") * lax.axis_size("col") + lax.axis_index("col")
        stream_at = lax.broadcasted_iota(jnp.int32, (streams, lanes), 0)
        error = jnp.where(stream_at == own_at, error_ref[0], 0.0)
        for n in range(tile_cols // slab):
            out_ref[n, :, 0:slab] = total[:, n * slab : (n + 1) * slab]
            out_ref[n, :, slab:] = error
            out_ref[n, :, slab : slab + streams] = term


def col_partial(jac, error, hi, lo, slab):
    streams = jac.shape[0]
    tile_rows, tile_cols = hi.shape
    out_shape = (tile_cols // slab, streams, slab + LANES)
    block = pl.BlockSpec((slab, tile_cols), lambda n: (n, 0))
    return pl.pallas_call(
        functools.partial(col_kernel, col_rows=tile_cols // LANES),
        grid=(tile_rows // slab,),
        in_specs=[
            pl.BlockSpec(jac.shape, lambda n: (0, 0, 0)),
            pl.BlockSpec(error.shape, lambda n: (0, 0, 0)),
            block,
            block,
        ],
        out_specs=pl.BlockSpec(out_shape, lambda n: (0, 0, 0)),
        out_shape=jax.ShapeDtypeStruct(out_shape, f32),
        scratch_shapes=[
            pltpu.VMEM((3 * streams, tile_cols), bf16),
            pltpu.VMEM((3 * streams, slab), bf16),
            pltpu.VMEM((streams, tile_cols), f32),
        ],
        compiler_params=limit(12),
        name="col_cross",
    )(jac, error, in_hbm(hi), in_hbm(lo))


def row_kernel(jac_ref, hi_ref, lo_ref, cross_ref, parts_ref):
    streams, rows, lanes = jac_ref.shape
    flat = jac_ref.reshape(streams * rows, lanes)

    @pl.when(pl.program_id(0) == 0)
    def _():
        stacked_parts(flat, 0, hi_ref.shape[1] // lanes, streams, rows, parts_ref)

    cross_ref[...] = five_products(parts_ref[...], hi_ref[...], lo_ref[...], ((1,), (1,)))


def row_partial(jac, hi, lo, slab):
    streams = jac.shape[0]
    tile_rows, tile_cols = hi.shape
    block = pl.BlockSpec((slab, tile_cols), lambda n: (n, 0))
    return pl.pallas_call(
        row_kernel,
        grid=(tile_rows // slab,),
        in_specs=[pl.BlockSpec(jac.shape, lambda n: (0, 0, 0)), block, block],
        out_specs=pl.BlockSpec((streams, slab), lambda n: (0, n)),
        out_shape=jax.ShapeDtypeStruct((streams, tile_rows), f32),
        scratch_shapes=[pltpu.VMEM((3 * streams, tile_cols), bf16)],
        compiler_params=limit(12),
        name="row_cross",
    )(jac, in_hbm(hi), in_hbm(lo))


def slab_kernel(pieces_ref, row_ref, own_ref, out_ref):
    tile_rows = row_ref.shape[1]
    slab = own_ref.shape[1]
    total = pieces_ref[0]
    for n in range(1, pieces_ref.shape[0]):
        total = total + pieces_ref[n]
    own_ref[...] = total[:, 0:slab]
    for n in range(out_ref.shape[0]):
        out_ref[n, :, 0:tile_rows] = row_ref[...]
        out_ref[n, :, tile_rows:] = total[:, slab:]


def slab_sum(pieces, row_part, copies):
    _, streams, padded = pieces.shape
    tile_rows = row_part.shape[1]
    return pl.pallas_call(
        slab_kernel,
        out_shape=[
            jax.ShapeDtypeStruct((streams, padded - LANES), f32),
            jax.ShapeDtypeStruct((copies, streams, tile_rows + LANES), f32),
        ],
        compiler_params=limit(8),
        name="slab",
    )(pieces, row_part)


def invert(innovation):
    streams = innovation.shape[0]
    row = lax.broadcasted_iota(jnp.int32, (streams, streams), 0)
    col = lax.broadcasted_iota(jnp.int32, (streams, streams), 1)
    identity = (row == col).astype(f32)
    innovation = innovation + forget * identity
    sums = jnp.sum(jnp.abs(innovation), axis=1, keepdims=True)
    bound = jnp.max(sums, axis=0, keepdims=True)
    power = identity - innovation / bound
    inverse = identity + power
    for repeat in range(NEWTON - 1):
        power = dot(power, power, ((1,), (0,)), highest)
        inverse = inverse + dot(inverse, power, ((1,), (0,)), highest)
    return inverse / bound


def head_kernel(cov_ref, _, head_ref, sem):
    copy = pltpu.make_async_copy(cov_ref.at[pl.ds(0, head_ref.shape[0])], head_ref, sem)
    copy.start()
    copy.wait()


def read_head(covariance, col_slabs):
    beyond = pl.BlockSpec(memory_space=pl.ANY)
    rows, cols = covariance.shape
    return pl.pallas_call(
        head_kernel,
        in_specs=[beyond, beyond],
        out_specs=pl.BlockSpec(memory_space=pltpu.VMEM),
        out_shape=pltpu.VMEM((rows // 4, cols), f32),
        scratch_shapes=[pltpu.SemaphoreType.DMA],
        compiler_params=limit(2),
        name="head",
    )(in_hbm(covariance), col_slabs)


def update_kernel(
    rows_ref, cols_ref, weight_ref, head_ref, cov_ref, new_weight_ref, new_cov_ref, left_ref, right_ref, tile_ref, in_sems, out_sems
):
    copies, streams, padded = rows_ref.shape
    col_slabs, _, slab = cols_ref.shape
    lanes = weight_ref.shape[1]
    tile_rows = padded - lanes
    slabs = tile_rows // slab
    chunks = in_sems.shape[0]
    height = tile_rows // chunks
    held = head_ref.shape[0] // height
    reads = []
    for n in range(held, chunks):
        here = pl.ds(n * height, height)
        reads.append(pltpu.make_async_copy(cov_ref.at[here], tile_ref.at[here], in_sems.at[n]))
        reads[-1].start()
    total = rows_ref[0]
    for n in range(1, copies):
        total = total + rows_ref[n]
    beside = total[:, tile_rows:]
    inverse = invert(beside[:, 0:streams])
    errors = beside[:, streams : streams + 1]
    for n in range(col_slabs):
        hi, mid, lo = split3(cols_ref[n])
        for m, part in enumerate((hi, mid, lo, hi, mid, hi)):
            right_ref[m * streams : (m + 1) * streams, n * slab : (n + 1) * slab] = part
    gain = dot(inverse, total[:, 0:tile_rows], ((0,), (0,)), highest)
    hi, mid, lo = split3(gain)
    for m, part in enumerate((hi, hi, hi, mid, mid, lo)):
        left_ref[m * streams : (m + 1) * streams, :] = part
    writes = []
    for n in range(chunks):
        update = dot(left_ref[:, n * height : (n + 1) * height], right_ref[...], ((0,), (0,)))
        here = pl.ds(n * height, height)
        if n >= held:
            reads[n - held].wait()
        before = head_ref if n < held else tile_ref
        tile_ref[here, :] = (before[here, :] - update) * (1.0 / forget)
        writes.append(pltpu.make_async_copy(tile_ref.at[here], new_cov_ref.at[here], out_sems.at[n]))
        writes[-1].start()
    col_at = lax.axis_index("col")
    own_at = (lax.axis_index("row") * slabs + col_at) * (slab // lanes)
    for n in range(slabs):

        @pl.when(col_at == n)
        def _():
            moved = jnp.sum(gain[:, n * slab : (n + 1) * slab] * errors, axis=0, keepdims=True)
            for i in range(slab // lanes):
                own = weight_ref[pl.ds(own_at + i, 1), :]
                new_weight_ref[i : i + 1, :] = own + moved[:, i * lanes : (i + 1) * lanes]

    for write in writes:
        write.wait()


def update(row_parts, col_slabs, layer_weight, head, covariance):
    _, streams, slab = col_slabs.shape
    tile_rows, tile_cols = covariance.shape
    width = layer_weight.shape[1]
    whole = pl.BlockSpec(memory_space=pltpu.VMEM)
    beyond = pl.BlockSpec(memory_space=pl.ANY)
    return pl.pallas_call(
        update_kernel,
        in_specs=[whole, whole, whole, whole, beyond],
        out_specs=[whole, beyond],
        out_shape=[
            jax.ShapeDtypeStruct((slab // width, width), f32),
            jax.ShapeDtypeStruct((tile_rows, tile_cols), f32),
        ],
        scratch_shapes=[
            pltpu.VMEM((6 * streams, tile_rows), bf16),
            pltpu.VMEM((6 * streams, tile_cols), bf16),
            pltpu.VMEM((tile_rows, tile_cols), f32),
            pltpu.SemaphoreType.DMA((8,)),
            pltpu.SemaphoreType.DMA((8,)),
        ],
        compiler_params=limit(20),
        name="update",
    )(row_parts, col_slabs, layer_weight, in_vmem(head), in_hbm(covariance))


def plain_steps(at, jac_all, errors, layer_weight, covariance, slab, cols_n):
    streams = jac_all.shape[0]
    hin, width = layer_weight.shape
    tile_rows, tile_cols = covariance.shape
    first = (at[0] * cols_n + at[1]) * slab
    jacobian = jac_all[:, 0:hin, :].reshape(streams, hin * width)
    jac_cols = lax.dynamic_slice_in_dim(jacobian, at[1] * tile_cols, tile_cols, 1)
    partial = dot(jac_cols, covariance, ((1,), (1,)), highest)
    cross_own = lax.psum_scatter(partial, "col", scatter_dimension=1, tiled=True)
    cross = lax.all_gather(cross_own, ("row", "col"), axis=1, tiled=True)
    inverse = invert(dot(jacobian, cross, ((1,), (1,)), highest))
    gain = dot(inverse, lax.dynamic_slice_in_dim(cross, at[0] * tile_rows, tile_rows, 1), ((0,), (0,)), highest)
    across = lax.dynamic_slice_in_dim(cross, at[1] * tile_cols, tile_cols, 1)
    new_cov = (covariance - dot(gain, across, ((0,), (0,)), highest)) / forget
    own_gain = lax.dynamic_slice_in_dim(gain, at[1] * slab, slab, 1)
    own_weight = lax.dynamic_slice_in_dim(layer_weight.reshape(-1), first, slab, 0)
    new_weight = own_weight + dot(errors, own_gain, ((0,), (0,)), highest)
    return new_weight, new_cov


def exchange(x, axes):
    return lax.all_to_all(x, axes, split_axis=0, concat_axis=0, tiled=True)


def on_device(
    atom_types,
    neighbor_ids,
    switching,
    environment,
    force_weights,
    targets,
    type_embed,
    layer_weight,
    out_weight,
    covariance,
):
    rows_n = lax.axis_size("row")
    cols_n = lax.axis_size("col")
    at = jnp.stack([lax.axis_index("row"), lax.axis_index("col")]).astype(jnp.int32)
    tile_rows, tile_cols = covariance.shape
    slab = tile_rows // cols_n
    hin, width = layer_weight.shape
    run_network = functools.partial(
        network,
        atom_types=atom_types,
        neighbor_ids=neighbor_ids,
        switching=switching,
        environment=environment,
        force_weights=force_weights,
        targets=targets,
        type_embed=type_embed,
        layer_weight=layer_weight,
        out_weight=out_weight,
    )
    streams = rows_n * cols_n * atom_types.shape[0]
    kernels = (
        atom_types.shape[0] == 1
        and width == LANES
        and slab % LANES == 0
        and tile_rows % (SUBLANES * LANES) == 0
        and tile_cols % (SUBLANES * LANES) == 0
        and rows_n * slab == tile_cols
        and streams < LANES
    )
    if not kernels:
        payload, error = run_network([[(0, hin)]])
        jac_all = lax.all_gather(payload[0], ("row", "col"), axis=0, tiled=True)
        errors = lax.all_gather(error[:, 0, 0], ("row", "col"), axis=0, tiled=True)
        return plain_steps(at, jac_all, errors, layer_weight, covariance, slab, cols_n)
    row_size, col_size = tile_rows // LANES, tile_cols // LANES
    plan = [[(c * col_size, col_size), (r * row_size, row_size)] for r in range(rows_n) for c in range(cols_n)]
    payload, error = run_network(plan)
    jac = exchange(payload, ("row", "col"))
    jac = jac.reshape(-1, *jac.shape[2:])
    hi, lo = stage(covariance)
    col_pieces = exchange(col_partial(jac, error, hi, lo, slab), "row")
    row_part = row_partial(jac, hi, lo, slab)
    col_own, row_part = slab_sum(col_pieces, row_part, cols_n)
    row_parts = exchange(row_part, "col")
    col_slabs = lax.all_gather(col_own, "row", axis=0, tiled=False)
    head = read_head(covariance, col_slabs)
    new_weight, new_cov = update(row_parts, col_slabs, layer_weight, head, covariance)
    return new_weight.reshape(-1), new_cov


def solution(mesh):
    in_specs = (
        P(("row", "col"), None),
        P(("row", "col"), None, None),
        P(("row", "col"), None, None),
        P(("row", "col"), None, None),
        P(("row", "col"), None),
        P(("row", "col")),
        P(),
        P(),
        P(),
        P("row", "col"),
    )
    out_specs = (P(("row", "col")), P("row", "col"))
    return jax.shard_map(
        on_device, mesh=mesh, in_specs=in_specs, out_specs=out_specs, check_vma=False
    )
```

```python
import functools
import math

import jax
import jax.numpy as jnp
from jax import lax
from jax.experimental import pallas as pl
from jax.experimental.pallas import tpu as pltpu
from jax.sharding import PartitionSpec as P

NEWTON = 4
LANES = 128
SUBLANES = 8


forget = 0.98
highest = lax.Precision.HIGHEST
f32 = jnp.float32
bf16 = jnp.bfloat16


def dot(left, right, contract, precision=None):
    return lax.dot_general(
        left, right, (contract, ((), ())), precision=precision, preferred_element_type=f32
    )


def split3(x):
    hi = x.astype(bf16)
    rest = x - hi.astype(f32)
    mid = rest.astype(bf16)
    lo = (rest - mid.astype(f32)).astype(bf16)
    return hi, mid, lo


def split2(x):
    hi = x.astype(bf16)
    return hi, (x - hi.astype(f32)).astype(bf16)


def limit(mib):
    return pltpu.CompilerParams(vmem_limit_bytes=mib << 20)


def five_products(parts, hi, lo, contract):
    streams = parts.shape[0] // 3
    by_hi = dot(parts, hi, contract)
    by_lo = dot(parts[0 : 2 * streams], lo, contract)
    return by_hi[0:streams] + (
        by_hi[streams : 2 * streams] + by_lo[0:streams] + (by_hi[2 * streams :] + by_lo[streams:])
    )


def network_kernel(
    types_ref,
    ids_ref,
    switch_ref,
    env_ref,
    force_ref,
    target_ref,
    embed_ref,
    weight_ref,
    out_weight_ref,
    payload_ref,
    error_ref,
    mix_ref,
    *,
    plan,
):
    neighbours, atoms = ids_ref.shape
    n_types = embed_ref.shape[0]
    height = min(64, atoms)
    for start in range(0, atoms, height):
        atom_at = lax.broadcasted_iota(jnp.int32, (height, atoms), 0) + start
        total = jnp.zeros((height, atoms), f32)
        for k in range(neighbours):
            total = total + jnp.where(ids_ref[k : k + 1, :] == atom_at, switch_ref[k : k + 1, :], 0.0)
        mix_ref[start : start + height, :] = total
    mix = mix_ref[...]
    type_at = lax.broadcasted_iota(jnp.int32, (n_types, atoms), 0)
    onehot = (types_ref[...] == type_at).astype(f32)
    mixed = env_ref[...] + dot(embed_ref[...], onehot, ((0,), (0,)), highest)
    parts = jnp.concatenate(split3(mixed), axis=0)
    descriptor = five_products(parts, *split2(mix), ((1,), (0,))) * (1.0 / math.sqrt(neighbours))
    hidden = jnp.tanh(descriptor)
    activity = jnp.tanh(dot(hidden, weight_ref[...], ((0,), (0,)), highest))
    out_weight = out_weight_ref[...]
    scale = 1.0 / math.sqrt(atoms)
    force = force_ref[...]
    weighted = dot(force, activity, ((1,), (0,)), highest)
    predicted = jnp.sum(weighted * out_weight, axis=1, keepdims=True) * scale
    slopes = out_weight * (1.0 - activity * activity)
    parts = jnp.concatenate(split3(hidden * force), axis=0)
    jacobian = five_products(parts, *split2(slopes), ((1,), (0,))) * scale
    error_ref[...] = jnp.broadcast_to(target_ref[...] - predicted, error_ref.shape)
    for block, pieces in enumerate(plan):
        at = 0
        for start, size in pieces:
            payload_ref[block, at : at + size, :] = jacobian[start : start + size, :]
            at += size


def network(
    plan, atom_types, neighbor_ids, switching, environment, force_weights, targets, type_embed, layer_weight, out_weight
):
    per_dev, neighbours, atoms = neighbor_ids.shape
    hin, width = layer_weight.shape
    blocks, rows = len(plan), sum(size for _, size in plan[0])

    def per_stream(*shape):
        return pl.BlockSpec((None,) + shape, lambda s: (s,) + (0,) * len(shape))

    def shared(shape):
        return pl.BlockSpec(shape, lambda s: (0,) * len(shape))

    return pl.pallas_call(
        functools.partial(network_kernel, plan=plan),
        grid=(per_dev,),
        in_specs=[
            per_stream(1, atoms),
            per_stream(neighbours, atoms),
            per_stream(neighbours, atoms),
            per_stream(hin, atoms),
            per_stream(1, atoms),
            per_stream(1, 1),
            shared(type_embed.shape),
            shared(layer_weight.shape),
            shared((1, width)),
        ],
        out_specs=[
            pl.BlockSpec((blocks, None, rows, width), lambda s: (0, s, 0, 0)),
            per_stream(1, width),
        ],
        out_shape=[
            jax.ShapeDtypeStruct((blocks, per_dev, rows, width), f32),
            jax.ShapeDtypeStruct((per_dev, 1, width), f32),
        ],
        scratch_shapes=[pltpu.VMEM((atoms, atoms), f32)],
        name="network",
    )(
        atom_types.reshape(per_dev, 1, atoms),
        neighbor_ids,
        switching,
        environment.swapaxes(1, 2),
        force_weights.reshape(per_dev, 1, atoms),
        targets.reshape(per_dev, 1, 1),
        type_embed,
        layer_weight,
        out_weight.reshape(1, width),
    )


def in_hbm(x):
    return pltpu.with_memory_space_constraint(x, pltpu.HBM)


def in_vmem(x):
    return pltpu.with_memory_space_constraint(x, pltpu.VMEM)


def stage_kernel(cov_ref, hi_ref, lo_ref, hi_head_ref, lo_head_ref, *, head_steps):
    hi, lo = split2(cov_ref[...])
    hi_ref[...] = hi
    lo_ref[...] = lo

    @pl.when(pl.program_id(0) < head_steps)
    def _():
        hi_head_ref[...] = hi
        lo_head_ref[...] = lo


def stage(covariance, head):
    rows, cols = covariance.shape
    height = min(rows // 8, head)
    head_steps = head // height
    block = pl.BlockSpec((height, cols), lambda n: (n, 0))
    head_block = pl.BlockSpec((height, cols), lambda n: (jnp.minimum(n, head_steps - 1), 0))
    return pl.pallas_call(
        functools.partial(stage_kernel, head_steps=head_steps),
        grid=(rows // height,),
        in_specs=[block],
        out_specs=[block, block, head_block, head_block],
        out_shape=[pltpu.HBM((rows, cols), bf16)] * 2 + [pltpu.VMEM((head, cols), bf16)] * 2,
        compiler_params=limit(12),
        name="stage",
    )(in_hbm(covariance))


def stacked_parts(flat, first, count, streams, stride, into_ref):
    lanes = flat.shape[1]
    for i in range(count):
        parts = split3(flat[pl.ds(first + i, streams, stride=stride), :])
        for n, part in enumerate(parts):
            into_ref[n * streams : (n + 1) * streams, i * lanes : (i + 1) * lanes] = part


def col_kernel(
    jac_ref,
    error_ref,
    hi_head_ref,
    lo_head_ref,
    hi_ref,
    lo_ref,
    out_ref,
    own_ref,
    parts_ref,
    sum_ref,
    hi_rest_ref,
    lo_rest_ref,
    sems,
    *,
    col_rows,
):
    streams, rows, lanes = jac_ref.shape
    head, tile_cols = hi_head_ref.shape
    slab = out_ref.shape[2] - lanes
    chunks = sems.shape[0]
    copies = []
    for n in range(chunks):
        source, target = pl.ds((n + 1) * head, head), pl.ds(n * head, head)
        copies.append(
            (
                pltpu.make_async_copy(hi_ref.at[source], hi_rest_ref.at[target], sems.at[n, 0]),
                pltpu.make_async_copy(lo_ref.at[source], lo_rest_ref.at[target], sems.at[n, 1]),
            )
        )
        for copy in copies[-1]:
            copy.start()
    flat = jac_ref.reshape(streams * rows, lanes)
    stacked_parts(flat, col_rows, rows - col_rows, streams, rows, own_ref)
    sum_ref[...] = five_products(own_ref[:, 0:head], hi_head_ref[...], lo_head_ref[...], ((1,), (0,)))
    stacked_parts(flat, 0, col_rows, streams, rows, parts_ref)
    for n in range(chunks):
        for copy in copies[n]:
            copy.wait()
        here = slice(n * head, (n + 1) * head)
        sum_ref[...] += five_products(
            own_ref[:, (n + 1) * head : (n + 2) * head], hi_rest_ref[here, :], lo_rest_ref[here, :], ((1,), (0,))
        )
    total = sum_ref[...]
    products = dot(parts_ref[...], jnp.concatenate(split3(total), axis=0), ((1,), (1,)))
    term = jnp.zeros((streams, streams), f32)
    for left, right in ((2, 0), (1, 1), (0, 2), (1, 0), (0, 1), (0, 0)):
        term = term + products[left * streams : (left + 1) * streams, right * streams : (right + 1) * streams]
    own_at = lax.axis_index("row") * lax.axis_size("col") + lax.axis_index("col")
    stream_at = lax.broadcasted_iota(jnp.int32, (streams, lanes), 0)
    error = jnp.where(stream_at == own_at, error_ref[0], 0.0)
    for n in range(tile_cols // slab):
        out_ref[n, :, 0:slab] = total[:, n * slab : (n + 1) * slab]
        out_ref[n, :, slab:] = error
        out_ref[n, :, slab : slab + streams] = term


def col_partial(jac, error, hi_head, lo_head, hi, lo, slab):
    streams = jac.shape[0]
    tile_rows, tile_cols = hi.shape
    head = hi_head.shape[0]
    whole = pl.BlockSpec(memory_space=pltpu.VMEM)
    beyond = pl.BlockSpec(memory_space=pl.ANY)
    return pl.pallas_call(
        functools.partial(col_kernel, col_rows=tile_cols // LANES),
        in_specs=[whole] * 4 + [beyond] * 2,
        out_specs=whole,
        out_shape=jax.ShapeDtypeStruct((tile_cols // slab, streams, slab + LANES), f32),
        scratch_shapes=[
            pltpu.VMEM((3 * streams, tile_rows), bf16),
            pltpu.VMEM((3 * streams, tile_cols), bf16),
            pltpu.VMEM((streams, tile_cols), f32),
            pltpu.VMEM((tile_rows - head, tile_cols), bf16),
            pltpu.VMEM((tile_rows - head, tile_cols), bf16),
            pltpu.SemaphoreType.DMA((tile_rows // head - 1, 2)),
        ],
        compiler_params=limit(16),
        name="col_cross",
    )(jac, error, in_vmem(hi_head), in_vmem(lo_head), in_hbm(hi), in_hbm(lo))


def row_kernel(jac_ref, hi_ref, lo_ref, cross_ref, parts_ref):
    streams, rows, lanes = jac_ref.shape
    flat = jac_ref.reshape(streams * rows, lanes)

    @pl.when(pl.program_id(0) == 0)
    def _():
        stacked_parts(flat, 0, hi_ref.shape[1] // lanes, streams, rows, parts_ref)

    cross_ref[...] = five_products(parts_ref[...], hi_ref[...], lo_ref[...], ((1,), (1,)))


def row_partial(jac, hi, lo, slab):
    streams = jac.shape[0]
    tile_rows, tile_cols = hi.shape
    block = pl.BlockSpec((slab, tile_cols), lambda n: (n, 0))
    return pl.pallas_call(
        row_kernel,
        grid=(tile_rows // slab,),
        in_specs=[pl.BlockSpec(jac.shape, lambda n: (0, 0, 0)), block, block],
        out_specs=pl.BlockSpec((streams, slab), lambda n: (0, n)),
        out_shape=jax.ShapeDtypeStruct((streams, tile_rows), f32),
        scratch_shapes=[pltpu.VMEM((3 * streams, tile_cols), bf16)],
        compiler_params=limit(12),
        name="row_cross",
    )(jac, in_hbm(hi), in_hbm(lo))


def slab_kernel(pieces_ref, row_ref, own_ref, out_ref):
    tile_rows = row_ref.shape[1]
    slab = own_ref.shape[1]
    total = pieces_ref[0]
    for n in range(1, pieces_ref.shape[0]):
        total = total + pieces_ref[n]
    own_ref[...] = total[:, 0:slab]
    for n in range(out_ref.shape[0]):
        out_ref[n, :, 0:tile_rows] = row_ref[...]
        out_ref[n, :, tile_rows:] = total[:, slab:]


def slab_sum(pieces, row_part, copies):
    _, streams, padded = pieces.shape
    tile_rows = row_part.shape[1]
    return pl.pallas_call(
        slab_kernel,
        out_shape=[
            jax.ShapeDtypeStruct((streams, padded - LANES), f32),
            jax.ShapeDtypeStruct((copies, streams, tile_rows + LANES), f32),
        ],
        compiler_params=limit(8),
        name="slab",
    )(pieces, row_part)


def invert(innovation):
    streams = innovation.shape[0]
    row = lax.broadcasted_iota(jnp.int32, (streams, streams), 0)
    col = lax.broadcasted_iota(jnp.int32, (streams, streams), 1)
    identity = (row == col).astype(f32)
    innovation = innovation + forget * identity
    sums = jnp.sum(jnp.abs(innovation), axis=1, keepdims=True)
    bound = jnp.max(sums, axis=0, keepdims=True)
    power = identity - innovation / bound
    inverse = identity + power
    for repeat in range(NEWTON - 1):
        power = dot(power, power, ((1,), (0,)), highest)
        inverse = inverse + dot(inverse, power, ((1,), (0,)), highest)
    return inverse / bound


def head_kernel(cov_ref, _, head_ref, sem):
    copy = pltpu.make_async_copy(cov_ref.at[pl.ds(0, head_ref.shape[0])], head_ref, sem)
    copy.start()
    copy.wait()


def read_head(covariance, col_slabs):
    beyond = pl.BlockSpec(memory_space=pl.ANY)
    rows, cols = covariance.shape
    return pl.pallas_call(
        head_kernel,
        in_specs=[beyond, beyond],
        out_specs=pl.BlockSpec(memory_space=pltpu.VMEM),
        out_shape=pltpu.VMEM((rows // 4, cols), f32),
        scratch_shapes=[pltpu.SemaphoreType.DMA],
        compiler_params=limit(2),
        name="head",
    )(in_hbm(covariance), col_slabs)


def update_kernel(
    rows_ref, cols_ref, weight_ref, head_ref, cov_ref, new_weight_ref, new_cov_ref, left_ref, right_ref, tile_ref, in_sems, out_sems
):
    copies, streams, padded = rows_ref.shape
    col_slabs, _, slab = cols_ref.shape
    lanes = weight_ref.shape[1]
    tile_rows = padded - lanes
    slabs = tile_rows // slab
    chunks = in_sems.shape[0]
    height = tile_rows // chunks
    held = head_ref.shape[0] // height
    reads = []
    for n in range(held, chunks):
        here = pl.ds(n * height, height)
        reads.append(pltpu.make_async_copy(cov_ref.at[here], tile_ref.at[here], in_sems.at[n]))
        reads[-1].start()
    total = rows_ref[0]
    for n in range(1, copies):
        total = total + rows_ref[n]
    beside = total[:, tile_rows:]
    inverse = invert(beside[:, 0:streams])
    errors = beside[:, streams : streams + 1]
    for n in range(col_slabs):
        hi, mid, lo = split3(cols_ref[n])
        for m, part in enumerate((hi, mid, lo, hi, mid, hi)):
            right_ref[m * streams : (m + 1) * streams, n * slab : (n + 1) * slab] = part
    gain = dot(inverse, total[:, 0:tile_rows], ((0,), (0,)), highest)
    hi, mid, lo = split3(gain)
    for m, part in enumerate((hi, hi, hi, mid, mid, lo)):
        left_ref[m * streams : (m + 1) * streams, :] = part
    writes = []
    for n in range(chunks):
        update = dot(left_ref[:, n * height : (n + 1) * height], right_ref[...], ((0,), (0,)))
        here = pl.ds(n * height, height)
        if n >= held:
            reads[n - held].wait()
        before = head_ref if n < held else tile_ref
        tile_ref[here, :] = (before[here, :] - update) * (1.0 / forget)
        writes.append(pltpu.make_async_copy(tile_ref.at[here], new_cov_ref.at[here], out_sems.at[n]))
        writes[-1].start()
    col_at = lax.axis_index("col")
    own_at = (lax.axis_index("row") * slabs + col_at) * (slab // lanes)
    for n in range(slabs):

        @pl.when(col_at == n)
        def _():
            moved = jnp.sum(gain[:, n * slab : (n + 1) * slab] * errors, axis=0, keepdims=True)
            for i in range(slab // lanes):
                own = weight_ref[pl.ds(own_at + i, 1), :]
                new_weight_ref[i : i + 1, :] = own + moved[:, i * lanes : (i + 1) * lanes]

    for write in writes:
        write.wait()


def update(row_parts, col_slabs, layer_weight, head, covariance):
    _, streams, slab = col_slabs.shape
    tile_rows, tile_cols = covariance.shape
    width = layer_weight.shape[1]
    whole = pl.BlockSpec(memory_space=pltpu.VMEM)
    beyond = pl.BlockSpec(memory_space=pl.ANY)
    return pl.pallas_call(
        update_kernel,
        in_specs=[whole, whole, whole, whole, beyond],
        out_specs=[whole, beyond],
        out_shape=[
            jax.ShapeDtypeStruct((slab // width, width), f32),
            jax.ShapeDtypeStruct((tile_rows, tile_cols), f32),
        ],
        scratch_shapes=[
            pltpu.VMEM((6 * streams, tile_rows), bf16),
            pltpu.VMEM((6 * streams, tile_cols), bf16),
            pltpu.VMEM((tile_rows, tile_cols), f32),
            pltpu.SemaphoreType.DMA((8,)),
            pltpu.SemaphoreType.DMA((8,)),
        ],
        compiler_params=limit(20),
        name="update",
    )(row_parts, col_slabs, layer_weight, in_vmem(head), in_hbm(covariance))


def plain_steps(at, jac_all, errors, layer_weight, covariance, slab, cols_n):
    streams = jac_all.shape[0]
    hin, width = layer_weight.shape
    tile_rows, tile_cols = covariance.shape
    first = (at[0] * cols_n + at[1]) * slab
    jacobian = jac_all[:, 0:hin, :].reshape(streams, hin * width)
    jac_cols = lax.dynamic_slice_in_dim(jacobian, at[1] * tile_cols, tile_cols, 1)
    partial = dot(jac_cols, covariance, ((1,), (1,)), highest)
    cross_own = lax.psum_scatter(partial, "col", scatter_dimension=1, tiled=True)
    cross = lax.all_gather(cross_own, ("row", "col"), axis=1, tiled=True)
    inverse = invert(dot(jacobian, cross, ((1,), (1,)), highest))
    gain = dot(inverse, lax.dynamic_slice_in_dim(cross, at[0] * tile_rows, tile_rows, 1), ((0,), (0,)), highest)
    across = lax.dynamic_slice_in_dim(cross, at[1] * tile_cols, tile_cols, 1)
    new_cov = (covariance - dot(gain, across, ((0,), (0,)), highest)) / forget
    own_gain = lax.dynamic_slice_in_dim(gain, at[1] * slab, slab, 1)
    own_weight = lax.dynamic_slice_in_dim(layer_weight.reshape(-1), first, slab, 0)
    new_weight = own_weight + dot(errors, own_gain, ((0,), (0,)), highest)
    return new_weight, new_cov


def exchange(x, axes):
    return lax.all_to_all(x, axes, split_axis=0, concat_axis=0, tiled=True)


def on_device(
    atom_types,
    neighbor_ids,
    switching,
    environment,
    force_weights,
    targets,
    type_embed,
    layer_weight,
    out_weight,
    covariance,
):
    rows_n = lax.axis_size("row")
    cols_n = lax.axis_size("col")
    at = jnp.stack([lax.axis_index("row"), lax.axis_index("col")]).astype(jnp.int32)
    tile_rows, tile_cols = covariance.shape
    slab = tile_rows // cols_n
    hin, width = layer_weight.shape
    run_network = functools.partial(
        network,
        atom_types=atom_types,
        neighbor_ids=neighbor_ids,
        switching=switching,
        environment=environment,
        force_weights=force_weights,
        targets=targets,
        type_embed=type_embed,
        layer_weight=layer_weight,
        out_weight=out_weight,
    )
    streams = rows_n * cols_n * atom_types.shape[0]
    kernels = (
        atom_types.shape[0] == 1
        and width == LANES
        and slab % LANES == 0
        and tile_rows % (SUBLANES * LANES) == 0
        and tile_cols % (SUBLANES * LANES) == 0
        and rows_n * slab == tile_cols
        and streams < LANES
    )
    if not kernels:
        payload, error = run_network([[(0, hin)]])
        jac_all = lax.all_gather(payload[0], ("row", "col"), axis=0, tiled=True)
        errors = lax.all_gather(error[:, 0, 0], ("row", "col"), axis=0, tiled=True)
        return plain_steps(at, jac_all, errors, layer_weight, covariance, slab, cols_n)
    row_size, col_size = tile_rows // LANES, tile_cols // LANES
    plan = [[(c * col_size, col_size), (r * row_size, row_size)] for r in range(rows_n) for c in range(cols_n)]
    payload, error = run_network(plan)
    jac = exchange(payload, ("row", "col"))
    jac = jac.reshape(-1, *jac.shape[2:])
    hi, lo, hi_head, lo_head = stage(covariance, tile_rows // 4)
    col_pieces = exchange(col_partial(jac, error, hi_head, lo_head, hi, lo, slab), "row")
    row_part = row_partial(jac, hi, lo, slab)
    col_own, row_part = slab_sum(col_pieces, row_part, cols_n)
    row_parts = exchange(row_part, "col")
    col_slabs = lax.all_gather(col_own, "row", axis=0, tiled=False)
    head = read_head(covariance, col_slabs)
    new_weight, new_cov = update(row_parts, col_slabs, layer_weight, head, covariance)
    return new_weight.reshape(-1), new_cov


def solution(mesh):
    in_specs = (
        P(("row", "col"), None),
        P(("row", "col"), None, None),
        P(("row", "col"), None, None),
        P(("row", "col"), None, None),
        P(("row", "col"), None),
        P(("row", "col")),
        P(),
        P(),
        P(),
        P("row", "col"),
    )
    out_specs = (P(("row", "col")), P("row", "col"))
    return jax.shard_map(
        on_device, mesh=mesh, in_specs=in_specs, out_specs=out_specs, check_vma=False
    )
```

```python
import functools
import math

import jax
import jax.numpy as jnp
from jax import lax
from jax.experimental import pallas as pl
from jax.experimental.pallas import tpu as pltpu
from jax.sharding import PartitionSpec as P

NEWTON = 4
LANES = 128
SUBLANES = 8


forget = 0.98
highest = lax.Precision.HIGHEST
f32 = jnp.float32
bf16 = jnp.bfloat16


def dot(left, right, contract, precision=None):
    return lax.dot_general(
        left, right, (contract, ((), ())), precision=precision, preferred_element_type=f32
    )


def split3(x):
    hi = x.astype(bf16)
    rest = x - hi.astype(f32)
    mid = rest.astype(bf16)
    lo = (rest - mid.astype(f32)).astype(bf16)
    return hi, mid, lo


def split2(x):
    hi = x.astype(bf16)
    return hi, (x - hi.astype(f32)).astype(bf16)


def limit(mib):
    return pltpu.CompilerParams(vmem_limit_bytes=mib << 20)


def five_products(parts, hi, lo, contract):
    streams = parts.shape[0] // 3
    by_hi = dot(parts, hi, contract)
    by_lo = dot(parts[0 : 2 * streams], lo, contract)
    return by_hi[0:streams] + (
        by_hi[streams : 2 * streams] + by_lo[0:streams] + (by_hi[2 * streams :] + by_lo[streams:])
    )


def network_kernel(
    types_ref,
    ids_ref,
    switch_ref,
    env_ref,
    force_ref,
    target_ref,
    embed_ref,
    weight_ref,
    out_weight_ref,
    payload_ref,
    mix_ref,
    *,
    plan,
):
    neighbours, atoms = ids_ref.shape
    n_types = embed_ref.shape[0]
    height = min(64, atoms)
    for start in range(0, atoms, height):
        atom_at = lax.broadcasted_iota(jnp.int32, (height, atoms), 0) + start
        total = jnp.zeros((height, atoms), f32)
        for k in range(neighbours):
            total = total + jnp.where(ids_ref[k : k + 1, :] == atom_at, switch_ref[k : k + 1, :], 0.0)
        mix_ref[start : start + height, :] = total
    mix = mix_ref[...]
    type_at = lax.broadcasted_iota(jnp.int32, (n_types, atoms), 0)
    onehot = (types_ref[...] == type_at).astype(f32)
    mixed = env_ref[...] + dot(embed_ref[...], onehot, ((0,), (0,)), highest)
    parts = jnp.concatenate(split3(mixed), axis=0)
    descriptor = five_products(parts, *split2(mix), ((1,), (0,))) * (1.0 / math.sqrt(neighbours))
    hidden = jnp.tanh(descriptor)
    activity = jnp.tanh(dot(hidden, weight_ref[...], ((0,), (0,)), highest))
    out_weight = out_weight_ref[...]
    scale = 1.0 / math.sqrt(atoms)
    force = force_ref[...]
    weighted = dot(force, activity, ((1,), (0,)), highest)
    predicted = jnp.sum(weighted * out_weight, axis=1, keepdims=True) * scale
    slopes = out_weight * (1.0 - activity * activity)
    parts = jnp.concatenate(split3(hidden * force), axis=0)
    jacobian = five_products(parts, *split2(slopes), ((1,), (0,))) * scale
    error = target_ref[...] - predicted
    for block, pieces in enumerate(plan):
        at = 0
        for start, size in pieces:
            payload_ref[block, at : at + size, :] = jacobian[start : start + size, :]
            at += size
        rest = payload_ref.shape[1] - at
        payload_ref[block, at:, :] = jnp.broadcast_to(error, (rest, jacobian.shape[1]))


def network(
    plan, atom_types, neighbor_ids, switching, environment, force_weights, targets, type_embed, layer_weight, out_weight
):
    per_dev, neighbours, atoms = neighbor_ids.shape
    hin, width = layer_weight.shape
    blocks = len(plan)
    rows = pl.cdiv(sum(size for _, size in plan[0]) + 1, SUBLANES) * SUBLANES

    def per_stream(*shape):
        return pl.BlockSpec((None,) + shape, lambda s: (s,) + (0,) * len(shape))

    def shared(shape):
        return pl.BlockSpec(shape, lambda s: (0,) * len(shape))

    return pl.pallas_call(
        functools.partial(network_kernel, plan=plan),
        grid=(per_dev,),
        in_specs=[
            per_stream(1, atoms),
            per_stream(neighbours, atoms),
            per_stream(neighbours, atoms),
            per_stream(hin, atoms),
            per_stream(1, atoms),
            per_stream(1, 1),
            shared(type_embed.shape),
            shared(layer_weight.shape),
            shared((1, width)),
        ],
        out_specs=pl.BlockSpec((blocks, None, rows, width), lambda s: (0, s, 0, 0)),
        out_shape=jax.ShapeDtypeStruct((blocks, per_dev, rows, width), f32),
        scratch_shapes=[pltpu.VMEM((atoms, atoms), f32)],
        name="network",
    )(
        atom_types.reshape(per_dev, 1, atoms),
        neighbor_ids,
        switching,
        environment.swapaxes(1, 2),
        force_weights.reshape(per_dev, 1, atoms),
        targets.reshape(per_dev, 1, 1),
        type_embed,
        layer_weight,
        out_weight.reshape(1, width),
    )


def in_hbm(x):
    return pltpu.with_memory_space_constraint(x, pltpu.HBM)


def in_vmem(x):
    return pltpu.with_memory_space_constraint(x, pltpu.VMEM)


def stage_kernel(cov_ref, hi_ref, lo_ref, hi_head_ref, lo_head_ref, *, head_steps):
    hi, lo = split2(cov_ref[...])
    hi_ref[...] = hi
    lo_ref[...] = lo

    @pl.when(pl.program_id(0) < head_steps)
    def _():
        hi_head_ref[...] = hi
        lo_head_ref[...] = lo


def stage(covariance, head):
    rows, cols = covariance.shape
    height = min(rows // 8, head)
    head_steps = head // height
    block = pl.BlockSpec((height, cols), lambda n: (n, 0))
    rest_block = pl.BlockSpec((height, cols), lambda n: (jnp.maximum(n - head_steps, 0), 0))
    head_block = pl.BlockSpec((height, cols), lambda n: (jnp.minimum(n, head_steps - 1), 0))
    return pl.pallas_call(
        functools.partial(stage_kernel, head_steps=head_steps),
        grid=(rows // height,),
        in_specs=[block],
        out_specs=[rest_block, rest_block, head_block, head_block],
        out_shape=[pltpu.HBM((rows - head, cols), bf16)] * 2 + [pltpu.VMEM((head, cols), bf16)] * 2,
        compiler_params=limit(12),
        name="stage",
    )(in_hbm(covariance))


def stacked_parts(flat, first, count, streams, stride, into_ref):
    lanes = flat.shape[1]
    for i in range(count):
        parts = split3(flat[pl.ds(first + i, streams, stride=stride), :])
        for n, part in enumerate(parts):
            into_ref[n * streams : (n + 1) * streams, i * lanes : (i + 1) * lanes] = part


def col_kernel(jac_ref, hi_head_ref, lo_head_ref, hi_ref, lo_ref, out_ref, parts_ref, hi_rest_ref, lo_rest_ref, sums_ref, sems):
    streams, rows, lanes = jac_ref.shape
    head, tile_cols = hi_head_ref.shape
    slabs, _, slab = out_ref.shape
    chunks = sems.shape[0]
    copies = []
    for n in range(chunks):
        here = pl.ds(n * head, head)
        copies.append(
            (
                pltpu.make_async_copy(hi_ref.at[here], hi_rest_ref.at[here], sems.at[n, 0]),
                pltpu.make_async_copy(lo_ref.at[here], lo_rest_ref.at[here], sems.at[n, 1]),
            )
        )
        for copy in copies[-1]:
            copy.start()
    flat = jac_ref.reshape(streams * rows, lanes)
    stacked_parts(flat, 0, parts_ref.shape[1] // lanes, streams, rows, parts_ref)
    sums_ref[...] = five_products(parts_ref[:, 0:head], hi_head_ref[...], lo_head_ref[...], ((1,), (0,)))
    for n in range(chunks):
        for copy in copies[n]:
            copy.wait()
        here = slice(n * head, (n + 1) * head)
        sums_ref[...] += five_products(
            parts_ref[:, (n + 1) * head : (n + 2) * head], hi_rest_ref[here, :], lo_rest_ref[here, :], ((1,), (0,))
        )
    for n in range(slabs):
        out_ref[n] = sums_ref[:, n * slab : (n + 1) * slab]


def col_partial(jac, hi_head, lo_head, hi, lo, slab):
    streams = jac.shape[0]
    rest, tile_cols = hi.shape
    head = hi_head.shape[0]
    whole = pl.BlockSpec(memory_space=pltpu.VMEM)
    beyond = pl.BlockSpec(memory_space=pl.ANY)
    return pl.pallas_call(
        col_kernel,
        in_specs=[whole] * 3 + [beyond] * 2,
        out_specs=whole,
        out_shape=jax.ShapeDtypeStruct((tile_cols // slab, streams, slab), f32),
        scratch_shapes=[
            pltpu.VMEM((3 * streams, head + rest), bf16),
            pltpu.VMEM((rest, tile_cols), bf16),
            pltpu.VMEM((rest, tile_cols), bf16),
            pltpu.VMEM((streams, tile_cols), f32),
            pltpu.SemaphoreType.DMA((rest // head, 2)),
        ],
        compiler_params=limit(16),
        name="col_cross",
    )(jac, in_vmem(hi_head), in_vmem(lo_head), in_hbm(hi), in_hbm(lo))


def slab_kernel(pieces_ref, jac_ref, own_ref, out_ref, error_ref, *, first):
    streams, rows, lanes = jac_ref.shape
    slab = own_ref.shape[1]
    total = pieces_ref[0]
    for n in range(1, pieces_ref.shape[0]):
        total = total + pieces_ref[n]
    own_ref[...] = total
    out_ref[:, 0:slab] = total
    flat = jac_ref.reshape(streams * rows, lanes)
    term = jnp.zeros((streams, streams), f32)
    for i in range(slab // lanes):
        own = flat[pl.ds(first + i, streams, stride=rows), :]
        term = term + dot(own, total[:, i * lanes : (i + 1) * lanes], ((1,), (1,)), highest)
    out_ref[:, slab:] = jnp.zeros((streams, lanes), f32)
    out_ref[:, slab : slab + streams] = term
    error_ref[...] = flat[pl.ds(first + slab // lanes, streams, stride=rows), :]


def slab_sum(pieces, jac, first):
    _, streams, slab = pieces.shape
    return pl.pallas_call(
        functools.partial(slab_kernel, first=first),
        out_shape=[
            jax.ShapeDtypeStruct((streams, slab), f32),
            jax.ShapeDtypeStruct((streams, slab + LANES), f32),
            jax.ShapeDtypeStruct((streams, LANES), f32),
        ],
        compiler_params=limit(8),
        name="slab",
    )(pieces, jac)


def term_kernel(own_ref, cols_ref, out_ref):
    slab = own_ref.shape[1]
    term = cols_ref[0, :, slab:]
    for n in range(1, cols_ref.shape[0]):
        term = term + cols_ref[n, :, slab:]
    for n in range(out_ref.shape[0]):
        out_ref[n, :, 0:slab] = own_ref[...]
        out_ref[n, :, slab:] = term


def with_terms(own, col_slabs, copies):
    _, streams, padded = col_slabs.shape
    return pl.pallas_call(
        term_kernel,
        out_shape=jax.ShapeDtypeStruct((copies, streams, padded), f32),
        compiler_params=limit(8),
        name="term",
    )(own, col_slabs)


def invert(innovation):
    streams = innovation.shape[0]
    row = lax.broadcasted_iota(jnp.int32, (streams, streams), 0)
    col = lax.broadcasted_iota(jnp.int32, (streams, streams), 1)
    identity = (row == col).astype(f32)
    innovation = innovation + forget * identity
    sums = jnp.sum(jnp.abs(innovation), axis=1, keepdims=True)
    bound = jnp.max(sums, axis=0, keepdims=True)
    power = identity - innovation / bound
    inverse = identity + power
    for repeat in range(NEWTON - 1):
        power = dot(power, power, ((1,), (0,)), highest)
        inverse = inverse + dot(inverse, power, ((1,), (0,)), highest)
    return inverse / bound


def head_kernel(cov_ref, _, head_ref, sem):
    copy = pltpu.make_async_copy(cov_ref.at[pl.ds(0, head_ref.shape[0])], head_ref, sem)
    copy.start()
    copy.wait()


def read_head(covariance, col_slabs):
    beyond = pl.BlockSpec(memory_space=pl.ANY)
    rows, cols = covariance.shape
    return pl.pallas_call(
        head_kernel,
        in_specs=[beyond, beyond],
        out_specs=pl.BlockSpec(memory_space=pltpu.VMEM),
        out_shape=pltpu.VMEM((rows // 4, cols), f32),
        scratch_shapes=[pltpu.SemaphoreType.DMA],
        compiler_params=limit(2),
        name="head",
    )(in_hbm(covariance), col_slabs)


def update_kernel(
    rows_ref, cols_ref, error_ref, weight_ref, head_ref, cov_ref, new_weight_ref, new_cov_ref, left_ref, right_ref, tile_ref, in_sems, out_sems
):
    slabs, streams, padded = rows_ref.shape
    col_slabs = cols_ref.shape[0]
    lanes = weight_ref.shape[1]
    slab = padded - lanes
    tile_rows = slabs * slab
    chunks = in_sems.shape[0]
    height = tile_rows // chunks
    held = head_ref.shape[0] // height
    reads = []
    for n in range(held, chunks):
        here = pl.ds(n * height, height)
        reads.append(pltpu.make_async_copy(cov_ref.at[here], tile_ref.at[here], in_sems.at[n]))
        reads[-1].start()
    term = rows_ref[0, :, slab:]
    for n in range(1, slabs):
        term = term + rows_ref[n, :, slab:]
    inverse = invert(term[:, 0:streams])
    errors = error_ref[:, 0:1]
    for n in range(col_slabs):
        hi, mid, lo = split3(cols_ref[n, :, 0:slab])
        for m, part in enumerate((hi, mid, lo, hi, mid, hi)):
            right_ref[m * streams : (m + 1) * streams, n * slab : (n + 1) * slab] = part
    cross = jnp.concatenate([rows_ref[n, :, 0:slab] for n in range(slabs)], axis=1)
    gain = dot(inverse, cross, ((0,), (0,)), highest)
    hi, mid, lo = split3(gain)
    for m, part in enumerate((hi, hi, hi, mid, mid, lo)):
        left_ref[m * streams : (m + 1) * streams, :] = part
    writes = []
    for n in range(chunks):
        update = dot(left_ref[:, n * height : (n + 1) * height], right_ref[...], ((0,), (0,)))
        here = pl.ds(n * height, height)
        if n >= held:
            reads[n - held].wait()
        before = head_ref if n < held else tile_ref
        tile_ref[here, :] = (before[here, :] - update) * (1.0 / forget)
        writes.append(pltpu.make_async_copy(tile_ref.at[here], new_cov_ref.at[here], out_sems.at[n]))
        writes[-1].start()
    col_at = lax.axis_index("col")
    own_at = (lax.axis_index("row") * slabs + col_at) * (slab // lanes)
    for n in range(slabs):

        @pl.when(col_at == n)
        def _():
            moved = jnp.sum(gain[:, n * slab : (n + 1) * slab] * errors, axis=0, keepdims=True)
            for i in range(slab // lanes):
                own = weight_ref[pl.ds(own_at + i, 1), :]
                new_weight_ref[i : i + 1, :] = own + moved[:, i * lanes : (i + 1) * lanes]

    for write in writes:
        write.wait()


def update(row_slabs, col_slabs, errors, layer_weight, head, covariance):
    _, streams, padded = col_slabs.shape
    slab = padded - LANES
    tile_rows, tile_cols = covariance.shape
    width = layer_weight.shape[1]
    whole = pl.BlockSpec(memory_space=pltpu.VMEM)
    beyond = pl.BlockSpec(memory_space=pl.ANY)
    return pl.pallas_call(
        update_kernel,
        in_specs=[whole] * 5 + [beyond],
        out_specs=[whole, beyond],
        out_shape=[
            jax.ShapeDtypeStruct((slab // width, width), f32),
            jax.ShapeDtypeStruct((tile_rows, tile_cols), f32),
        ],
        scratch_shapes=[
            pltpu.VMEM((6 * streams, tile_rows), bf16),
            pltpu.VMEM((6 * streams, tile_cols), bf16),
            pltpu.VMEM((tile_rows, tile_cols), f32),
            pltpu.SemaphoreType.DMA((8,)),
            pltpu.SemaphoreType.DMA((8,)),
        ],
        compiler_params=limit(20),
        name="update",
    )(row_slabs, col_slabs, errors, layer_weight, in_vmem(head), in_hbm(covariance))


def plain_steps(at, jac_all, errors, layer_weight, covariance, slab, cols_n):
    streams = jac_all.shape[0]
    hin, width = layer_weight.shape
    tile_rows, tile_cols = covariance.shape
    first = (at[0] * cols_n + at[1]) * slab
    jacobian = jac_all[:, 0:hin, :].reshape(streams, hin * width)
    jac_cols = lax.dynamic_slice_in_dim(jacobian, at[1] * tile_cols, tile_cols, 1)
    partial = dot(jac_cols, covariance, ((1,), (1,)), highest)
    cross_own = lax.psum_scatter(partial, "col", scatter_dimension=1, tiled=True)
    cross = lax.all_gather(cross_own, ("row", "col"), axis=1, tiled=True)
    inverse = invert(dot(jacobian, cross, ((1,), (1,)), highest))
    gain = dot(inverse, lax.dynamic_slice_in_dim(cross, at[0] * tile_rows, tile_rows, 1), ((0,), (0,)), highest)
    across = lax.dynamic_slice_in_dim(cross, at[1] * tile_cols, tile_cols, 1)
    new_cov = (covariance - dot(gain, across, ((0,), (0,)), highest)) / forget
    own_gain = lax.dynamic_slice_in_dim(gain, at[1] * slab, slab, 1)
    own_weight = lax.dynamic_slice_in_dim(layer_weight.reshape(-1), first, slab, 0)
    new_weight = own_weight + dot(errors, own_gain, ((0,), (0,)), highest)
    return new_weight, new_cov


def exchange(x, axes):
    return lax.all_to_all(x, axes, split_axis=0, concat_axis=0, tiled=True)


def on_device(
    atom_types,
    neighbor_ids,
    switching,
    environment,
    force_weights,
    targets,
    type_embed,
    layer_weight,
    out_weight,
    covariance,
):
    rows_n = lax.axis_size("row")
    cols_n = lax.axis_size("col")
    at = jnp.stack([lax.axis_index("row"), lax.axis_index("col")]).astype(jnp.int32)
    tile_rows, tile_cols = covariance.shape
    slab = tile_rows // cols_n
    hin, width = layer_weight.shape
    run_network = functools.partial(
        network,
        atom_types=atom_types,
        neighbor_ids=neighbor_ids,
        switching=switching,
        environment=environment,
        force_weights=force_weights,
        targets=targets,
        type_embed=type_embed,
        layer_weight=layer_weight,
        out_weight=out_weight,
    )
    streams = rows_n * cols_n * atom_types.shape[0]
    kernels = (
        atom_types.shape[0] == 1
        and width == LANES
        and slab % LANES == 0
        and tile_rows % (SUBLANES * LANES) == 0
        and tile_cols % (SUBLANES * LANES) == 0
        and rows_n * slab == tile_cols
        and streams < LANES
    )
    if not kernels:
        payload = run_network([[(0, hin)]])[0]
        jac_all = lax.all_gather(payload, ("row", "col"), axis=0, tiled=True)
        return plain_steps(at, jac_all[:, 0:hin], jac_all[:, hin, 0], layer_weight, covariance, slab, cols_n)
    row_size, slab_size = tile_rows // LANES, slab // LANES
    devices = [(r, c) for r in range(rows_n) for c in range(cols_n)]
    plan = [[(r * row_size, row_size), ((c * rows_n + r) * slab_size, slab_size)] for r, c in devices]
    jac = exchange(run_network(plan), ("row", "col"))
    jac = jac.reshape(-1, *jac.shape[2:])
    hi, lo, hi_head, lo_head = stage(covariance, tile_rows // 4)
    pieces = exchange(col_partial(jac, hi_head, lo_head, hi, lo, slab), "row")
    col_own, with_term, errors = slab_sum(pieces, jac, row_size)
    to_row = [(r * cols_n + c, c * rows_n + r) for r, c in devices]
    row_own = lax.ppermute(col_own, ("row", "col"), to_row)
    col_slabs = lax.all_gather(with_term, "row", axis=0, tiled=False)
    row_slabs = exchange(with_terms(row_own, col_slabs, cols_n), "col")
    head = read_head(covariance, col_slabs)
    new_weight, new_cov = update(row_slabs, col_slabs, errors, layer_weight, head, covariance)
    return new_weight.reshape(-1), new_cov


def solution(mesh):
    in_specs = (
        P(("row", "col"), None),
        P(("row", "col"), None, None),
        P(("row", "col"), None, None),
        P(("row", "col"), None, None),
        P(("row", "col"), None),
        P(("row", "col")),
        P(),
        P(),
        P(),
        P("row", "col"),
    )
    out_specs = (P(("row", "col")), P("row", "col"))
    return jax.shard_map(
        on_device, mesh=mesh, in_specs=in_specs, out_specs=out_specs, check_vma=False
    )
```

```python
import functools
import math

import jax
import jax.numpy as jnp
from jax import lax
from jax.experimental import pallas as pl
from jax.experimental.pallas import tpu as pltpu
from jax.sharding import PartitionSpec as P

NEWTON = 4
LANES = 128
SUBLANES = 8


forget = 0.98
highest = lax.Precision.HIGHEST
f32 = jnp.float32
bf16 = jnp.bfloat16


def dot(left, right, contract, precision=None):
    return lax.dot_general(
        left, right, (contract, ((), ())), precision=precision, preferred_element_type=f32
    )


def split3(x):
    hi = x.astype(bf16)
    rest = x - hi.astype(f32)
    mid = rest.astype(bf16)
    lo = (rest - mid.astype(f32)).astype(bf16)
    return hi, mid, lo


def split2(x):
    hi = x.astype(bf16)
    return hi, (x - hi.astype(f32)).astype(bf16)


def limit(mib):
    return pltpu.CompilerParams(vmem_limit_bytes=mib << 20)


def five_products(parts, hi, lo, contract):
    streams = parts.shape[0] // 3
    by_hi = dot(parts, hi, contract)
    by_lo = dot(parts[0 : 2 * streams], lo, contract)
    return by_hi[0:streams] + (
        by_hi[streams : 2 * streams] + by_lo[0:streams] + (by_hi[2 * streams :] + by_lo[streams:])
    )


def network_kernel(
    types_ref,
    ids_ref,
    switch_ref,
    env_ref,
    force_ref,
    target_ref,
    embed_ref,
    weight_ref,
    out_weight_ref,
    payload_ref,
    mix_ref,
    *,
    plan,
):
    neighbours, atoms = ids_ref.shape
    n_types = embed_ref.shape[0]
    height = min(64, atoms)
    for start in range(0, atoms, height):
        atom_at = lax.broadcasted_iota(jnp.int32, (height, atoms), 0) + start
        total = jnp.zeros((height, atoms), f32)
        for k in range(neighbours):
            total = total + jnp.where(ids_ref[k : k + 1, :] == atom_at, switch_ref[k : k + 1, :], 0.0)
        mix_ref[start : start + height, :] = total
    mix = mix_ref[...]
    type_at = lax.broadcasted_iota(jnp.int32, (n_types, atoms), 0)
    onehot = (types_ref[...] == type_at).astype(f32)
    mixed = env_ref[...] + dot(embed_ref[...], onehot, ((0,), (0,)), highest)
    parts = jnp.concatenate(split3(mixed), axis=0)
    descriptor = five_products(parts, *split2(mix), ((1,), (0,))) * (1.0 / math.sqrt(neighbours))
    hidden = jnp.tanh(descriptor)
    activity = jnp.tanh(dot(hidden, weight_ref[...], ((0,), (0,)), highest))
    out_weight = out_weight_ref[...]
    scale = 1.0 / math.sqrt(atoms)
    force = force_ref[...]
    weighted = dot(force, activity, ((1,), (0,)), highest)
    predicted = jnp.sum(weighted * out_weight, axis=1, keepdims=True) * scale
    slopes = out_weight * (1.0 - activity * activity)
    parts = jnp.concatenate(split3(hidden * force), axis=0)
    jacobian = five_products(parts, *split2(slopes), ((1,), (0,))) * scale
    error = target_ref[...] - predicted
    for block, pieces in enumerate(plan):
        at = 0
        for start, size in pieces:
            payload_ref[block, at : at + size, :] = jacobian[start : start + size, :]
            at += size
        rest = payload_ref.shape[1] - at
        payload_ref[block, at:, :] = jnp.broadcast_to(error, (rest, jacobian.shape[1]))


def network(
    plan, atom_types, neighbor_ids, switching, environment, force_weights, targets, type_embed, layer_weight, out_weight
):
    per_dev, neighbours, atoms = neighbor_ids.shape
    hin, width = layer_weight.shape
    blocks = len(plan)
    rows = pl.cdiv(sum(size for _, size in plan[0]) + 1, SUBLANES) * SUBLANES

    def per_stream(*shape):
        return pl.BlockSpec((None,) + shape, lambda s: (s,) + (0,) * len(shape))

    def shared(shape):
        return pl.BlockSpec(shape, lambda s: (0,) * len(shape))

    return pl.pallas_call(
        functools.partial(network_kernel, plan=plan),
        grid=(per_dev,),
        in_specs=[
            per_stream(1, atoms),
            per_stream(neighbours, atoms),
            per_stream(neighbours, atoms),
            per_stream(hin, atoms),
            per_stream(1, atoms),
            per_stream(1, 1),
            shared(type_embed.shape),
            shared(layer_weight.shape),
            shared((1, width)),
        ],
        out_specs=pl.BlockSpec((blocks, None, rows, width), lambda s: (0, s, 0, 0)),
        out_shape=jax.ShapeDtypeStruct((blocks, per_dev, rows, width), f32),
        scratch_shapes=[pltpu.VMEM((atoms, atoms), f32)],
        name="network",
    )(
        atom_types.reshape(per_dev, 1, atoms),
        neighbor_ids,
        switching,
        environment.swapaxes(1, 2),
        force_weights.reshape(per_dev, 1, atoms),
        targets.reshape(per_dev, 1, 1),
        type_embed,
        layer_weight,
        out_weight.reshape(1, width),
    )


def in_hbm(x):
    return pltpu.with_memory_space_constraint(x, pltpu.HBM)


def in_vmem(x):
    return pltpu.with_memory_space_constraint(x, pltpu.VMEM)


def stage_kernel(cov_ref, hi_ref, lo_ref, hi_head_ref, lo_head_ref, *, head_steps):
    hi, lo = split2(cov_ref[...])
    hi_ref[...] = hi
    lo_ref[...] = lo

    @pl.when(pl.program_id(0) < head_steps)
    def _():
        hi_head_ref[...] = hi
        lo_head_ref[...] = lo


def stage(covariance, head, tail):
    rows, cols = covariance.shape
    height = min(rows // 8, head)
    head_steps = head // height
    block = pl.BlockSpec((height, cols), lambda n: (n, 0))
    rest_block = pl.BlockSpec((height, cols), lambda n: (jnp.maximum(n - head_steps, 0), 0))
    head_block = pl.BlockSpec((height, cols), lambda n: (jnp.minimum(n, head_steps - 1), 0))
    return pl.pallas_call(
        functools.partial(stage_kernel, head_steps=head_steps),
        grid=((rows - tail) // height,),
        in_specs=[block],
        out_specs=[rest_block, rest_block, head_block, head_block],
        out_shape=[pltpu.HBM((rows - head - tail, cols), bf16)] * 2 + [pltpu.VMEM((head, cols), bf16)] * 2,
        compiler_params=limit(12),
        name="stage",
    )(in_hbm(covariance))


def stacked_parts(flat, first, count, streams, stride, into_ref):
    lanes = flat.shape[1]
    for i in range(count):
        parts = split3(flat[pl.ds(first + i, streams, stride=stride), :])
        for n, part in enumerate(parts):
            into_ref[n * streams : (n + 1) * streams, i * lanes : (i + 1) * lanes] = part


def col_kernel(
    jac_ref,
    hi_head_ref,
    lo_head_ref,
    hi_ref,
    lo_ref,
    cov_ref,
    out_ref,
    parts_ref,
    hi_rest_ref,
    lo_rest_ref,
    tail_ref,
    sums_ref,
    sems,
    tail_sem,
):
    streams, rows, lanes = jac_ref.shape
    head, tile_cols = hi_head_ref.shape
    slabs, _, slab = out_ref.shape
    chunks = sems.shape[0]
    copies = []
    for n in range(chunks):
        here = pl.ds(n * head, head)
        copies.append(
            (
                pltpu.make_async_copy(hi_ref.at[here], hi_rest_ref.at[here], sems.at[n, 0]),
                pltpu.make_async_copy(lo_ref.at[here], lo_rest_ref.at[here], sems.at[n, 1]),
            )
        )
        for copy in copies[-1]:
            copy.start()
    tail = tail_ref.shape[0]
    last = pltpu.make_async_copy(cov_ref.at[pl.ds(cov_ref.shape[0] - tail, tail)], tail_ref, tail_sem)
    last.start()
    flat = jac_ref.reshape(streams * rows, lanes)
    stacked_parts(flat, 0, parts_ref.shape[1] // lanes, streams, rows, parts_ref)
    sums_ref[...] = five_products(parts_ref[:, 0:head], hi_head_ref[...], lo_head_ref[...], ((1,), (0,)))
    for n in range(chunks):
        for copy in copies[n]:
            copy.wait()
        here = slice(n * head, (n + 1) * head)
        sums_ref[...] += five_products(
            parts_ref[:, (n + 1) * head : (n + 2) * head], hi_rest_ref[here, :], lo_rest_ref[here, :], ((1,), (0,))
        )
    last.wait()
    sums_ref[...] += five_products(
        parts_ref[:, parts_ref.shape[1] - tail :], *split2(tail_ref[...]), ((1,), (0,))
    )
    for n in range(slabs):
        out_ref[n] = sums_ref[:, n * slab : (n + 1) * slab]


def col_partial(jac, hi_head, lo_head, hi, lo, covariance, slab):
    streams = jac.shape[0]
    rest, tile_cols = hi.shape
    head = hi_head.shape[0]
    tail = covariance.shape[0] - head - rest
    whole = pl.BlockSpec(memory_space=pltpu.VMEM)
    beyond = pl.BlockSpec(memory_space=pl.ANY)
    return pl.pallas_call(
        col_kernel,
        in_specs=[whole] * 3 + [beyond] * 3,
        out_specs=whole,
        out_shape=jax.ShapeDtypeStruct((tile_cols // slab, streams, slab), f32),
        scratch_shapes=[
            pltpu.VMEM((3 * streams, covariance.shape[0]), bf16),
            pltpu.VMEM((rest, tile_cols), bf16),
            pltpu.VMEM((rest, tile_cols), bf16),
            pltpu.VMEM((tail, tile_cols), f32),
            pltpu.VMEM((streams, tile_cols), f32),
            pltpu.SemaphoreType.DMA((rest // head, 2)),
            pltpu.SemaphoreType.DMA,
        ],
        compiler_params=limit(16),
        name="col_cross",
    )(jac, in_vmem(hi_head), in_vmem(lo_head), in_hbm(hi), in_hbm(lo), in_hbm(covariance))


def packed(term):
    streams = term.shape[0]
    groups = LANES // streams
    height = streams // groups
    return jnp.concatenate([term[n * height : (n + 1) * height] for n in range(groups)], axis=1)


def unpacked(rows, streams):
    return jnp.concatenate(
        [rows[:, n * streams : (n + 1) * streams] for n in range(LANES // streams)], axis=0
    )


def slab_kernel(pieces_ref, jac_ref, own_ref, out_ref, error_ref, *, first):
    streams, rows, lanes = jac_ref.shape
    slab = own_ref.shape[1]
    total = pieces_ref[0]
    for n in range(1, pieces_ref.shape[0]):
        total = total + pieces_ref[n]
    own_ref[...] = total
    flat = jac_ref.reshape(streams * rows, lanes)
    term = jnp.zeros((streams, streams), f32)
    for i in range(slab // lanes):
        own = flat[pl.ds(first + i, streams, stride=rows), :]
        here = total[:, i * lanes : (i + 1) * lanes]
        term = term + dot(own, here, ((1,), (1,)), highest)
        out_ref[i * streams : (i + 1) * streams, :] = here
    out_ref[slab // lanes * streams :, :] = packed(term)
    error_ref[...] = flat[pl.ds(first + slab // lanes, streams, stride=rows), :]


def slab_sum(pieces, jac, first):
    _, streams, slab = pieces.shape
    return pl.pallas_call(
        functools.partial(slab_kernel, first=first),
        out_shape=[
            jax.ShapeDtypeStruct((streams, slab), f32),
            jax.ShapeDtypeStruct((streams * (slab + streams) // LANES, LANES), f32),
            jax.ShapeDtypeStruct((streams, LANES), f32),
        ],
        compiler_params=limit(8),
        name="slab",
    )(pieces, jac)


def term_kernel(own_ref, cols_ref, out_ref):
    streams, slab = own_ref.shape
    _, lanes = out_ref.shape[1:]
    under = slab // lanes * streams
    term = cols_ref[0, under:, :]
    for n in range(1, cols_ref.shape[0]):
        term = term + cols_ref[n, under:, :]
    for n in range(out_ref.shape[0]):
        for i in range(slab // lanes):
            out_ref[n, i * streams : (i + 1) * streams, :] = own_ref[:, i * lanes : (i + 1) * lanes]
        out_ref[n, under:, :] = term


def with_terms(own, col_slabs, copies):
    return pl.pallas_call(
        term_kernel,
        out_shape=jax.ShapeDtypeStruct((copies,) + col_slabs.shape[1:], f32),
        compiler_params=limit(8),
        name="term",
    )(own, col_slabs)


def invert(innovation):
    streams = innovation.shape[0]
    row = lax.broadcasted_iota(jnp.int32, (streams, streams), 0)
    col = lax.broadcasted_iota(jnp.int32, (streams, streams), 1)
    identity = (row == col).astype(f32)
    innovation = innovation + forget * identity
    sums = jnp.sum(jnp.abs(innovation), axis=1, keepdims=True)
    bound = jnp.max(sums, axis=0, keepdims=True)
    power = identity - innovation / bound
    inverse = identity + power
    for repeat in range(NEWTON - 1):
        power = dot(power, power, ((1,), (0,)), highest)
        inverse = inverse + dot(inverse, power, ((1,), (0,)), highest)
    return inverse / bound


def head_kernel(cov_ref, cols_ref, head_ref, right_ref, sem):
    copy = pltpu.make_async_copy(cov_ref.at[pl.ds(0, head_ref.shape[0])], head_ref, sem)
    copy.start()
    streams = right_ref.shape[0] // 6
    slabs, _, lanes = cols_ref.shape
    per_slab = right_ref.shape[1] // slabs // lanes
    for n in range(slabs):
        for i in range(per_slab):
            hi, mid, lo = split3(cols_ref[n, i * streams : (i + 1) * streams, :])
            at = (n * per_slab + i) * lanes
            for m, part in enumerate((hi, mid, lo, hi, mid, hi)):
                right_ref[m * streams : (m + 1) * streams, at : at + lanes] = part
    copy.wait()


def read_head(covariance, col_slabs, streams):
    rows, cols = covariance.shape
    whole = pl.BlockSpec(memory_space=pltpu.VMEM)
    return pl.pallas_call(
        head_kernel,
        in_specs=[pl.BlockSpec(memory_space=pl.ANY), whole],
        out_specs=[whole, whole],
        out_shape=[pltpu.VMEM((rows // 4, cols), f32), pltpu.VMEM((6 * streams, cols), bf16)],
        scratch_shapes=[pltpu.SemaphoreType.DMA],
        compiler_params=limit(4),
        name="head",
    )(in_hbm(covariance), col_slabs)


def update_kernel(
    rows_ref, right_ref, error_ref, weight_ref, head_ref, cov_ref, new_weight_ref, new_cov_ref, left_ref, tile_ref, in_sems, out_sems
):
    slabs, _, lanes = rows_ref.shape
    streams = error_ref.shape[0]
    tile_rows = cov_ref.shape[0]
    slab = tile_rows // slabs
    under = slab // lanes * streams
    chunks = in_sems.shape[0]
    height = tile_rows // chunks
    held = head_ref.shape[0] // height
    reads = []
    for n in range(held, chunks):
        here = pl.ds(n * height, height)
        reads.append(pltpu.make_async_copy(cov_ref.at[here], tile_ref.at[here], in_sems.at[n]))
        reads[-1].start()
    term = rows_ref[0, under:, :]
    for n in range(1, slabs):
        term = term + rows_ref[n, under:, :]
    inverse = invert(unpacked(term, streams))
    errors = error_ref[:, 0:1]
    cross = jnp.concatenate(
        [rows_ref[n, i : i + streams, :] for n in range(slabs) for i in range(0, under, streams)], axis=1
    )
    gain = dot(inverse, cross, ((0,), (0,)), highest)
    hi, mid, lo = split3(gain)
    for m, part in enumerate((hi, hi, hi, mid, mid, lo)):
        left_ref[m * streams : (m + 1) * streams, :] = part
    writes = []
    for n in range(chunks):
        update = dot(left_ref[:, n * height : (n + 1) * height], right_ref[...], ((0,), (0,)))
        here = pl.ds(n * height, height)
        if n >= held:
            reads[n - held].wait()
        before = head_ref if n < held else tile_ref
        tile_ref[here, :] = (before[here, :] - update) * (1.0 / forget)
        writes.append(pltpu.make_async_copy(tile_ref.at[here], new_cov_ref.at[here], out_sems.at[n]))
        writes[-1].start()
    col_at = lax.axis_index("col")
    own_at = (lax.axis_index("row") * slabs + col_at) * (slab // lanes)
    for n in range(slabs):

        @pl.when(col_at == n)
        def _():
            moved = jnp.sum(gain[:, n * slab : (n + 1) * slab] * errors, axis=0, keepdims=True)
            for i in range(slab // lanes):
                own = weight_ref[pl.ds(own_at + i, 1), :]
                new_weight_ref[i : i + 1, :] = own + moved[:, i * lanes : (i + 1) * lanes]

    for write in writes:
        write.wait()


def update(row_slabs, right, errors, layer_weight, head, covariance):
    streams = errors.shape[0]
    tile_rows, tile_cols = covariance.shape
    slab = tile_rows // row_slabs.shape[0]
    width = layer_weight.shape[1]
    whole = pl.BlockSpec(memory_space=pltpu.VMEM)
    beyond = pl.BlockSpec(memory_space=pl.ANY)
    return pl.pallas_call(
        update_kernel,
        in_specs=[whole] * 5 + [beyond],
        out_specs=[whole, beyond],
        out_shape=[
            jax.ShapeDtypeStruct((slab // width, width), f32),
            jax.ShapeDtypeStruct((tile_rows, tile_cols), f32),
        ],
        scratch_shapes=[
            pltpu.VMEM((6 * streams, tile_rows), bf16),
            pltpu.VMEM((tile_rows, tile_cols), f32),
            pltpu.SemaphoreType.DMA((8,)),
            pltpu.SemaphoreType.DMA((8,)),
        ],
        compiler_params=limit(20),
        name="update",
    )(row_slabs, in_vmem(right), errors, layer_weight, in_vmem(head), in_hbm(covariance))


def plain_steps(at, jac_all, errors, layer_weight, covariance, slab, cols_n):
    streams = jac_all.shape[0]
    hin, width = layer_weight.shape
    tile_rows, tile_cols = covariance.shape
    first = (at[0] * cols_n + at[1]) * slab
    jacobian = jac_all[:, 0:hin, :].reshape(streams, hin * width)
    jac_cols = lax.dynamic_slice_in_dim(jacobian, at[1] * tile_cols, tile_cols, 1)
    partial = dot(jac_cols, covariance, ((1,), (1,)), highest)
    cross_own = lax.psum_scatter(partial, "col", scatter_dimension=1, tiled=True)
    cross = lax.all_gather(cross_own, ("row", "col"), axis=1, tiled=True)
    inverse = invert(dot(jacobian, cross, ((1,), (1,)), highest))
    gain = dot(inverse, lax.dynamic_slice_in_dim(cross, at[0] * tile_rows, tile_rows, 1), ((0,), (0,)), highest)
    across = lax.dynamic_slice_in_dim(cross, at[1] * tile_cols, tile_cols, 1)
    new_cov = (covariance - dot(gain, across, ((0,), (0,)), highest)) / forget
    own_gain = lax.dynamic_slice_in_dim(gain, at[1] * slab, slab, 1)
    own_weight = lax.dynamic_slice_in_dim(layer_weight.reshape(-1), first, slab, 0)
    new_weight = own_weight + dot(errors, own_gain, ((0,), (0,)), highest)
    return new_weight, new_cov


def exchange(x, axes):
    return lax.all_to_all(x, axes, split_axis=0, concat_axis=0, tiled=True)


def on_device(
    atom_types,
    neighbor_ids,
    switching,
    environment,
    force_weights,
    targets,
    type_embed,
    layer_weight,
    out_weight,
    covariance,
):
    rows_n = lax.axis_size("row")
    cols_n = lax.axis_size("col")
    at = jnp.stack([lax.axis_index("row"), lax.axis_index("col")]).astype(jnp.int32)
    tile_rows, tile_cols = covariance.shape
    slab = tile_rows // cols_n
    hin, width = layer_weight.shape
    run_network = functools.partial(
        network,
        atom_types=atom_types,
        neighbor_ids=neighbor_ids,
        switching=switching,
        environment=environment,
        force_weights=force_weights,
        targets=targets,
        type_embed=type_embed,
        layer_weight=layer_weight,
        out_weight=out_weight,
    )
    streams = rows_n * cols_n * atom_types.shape[0]
    kernels = (
        atom_types.shape[0] == 1
        and width == LANES
        and slab % LANES == 0
        and tile_rows % (SUBLANES * LANES) == 0
        and tile_cols % (SUBLANES * LANES) == 0
        and rows_n * slab == tile_cols
        and LANES % streams == 0
        and streams * streams % (SUBLANES * LANES) == 0
    )
    if not kernels:
        payload = run_network([[(0, hin)]])[0]
        jac_all = lax.all_gather(payload, ("row", "col"), axis=0, tiled=True)
        return plain_steps(at, jac_all[:, 0:hin], jac_all[:, hin, 0], layer_weight, covariance, slab, cols_n)
    row_size, slab_size = tile_rows // LANES, slab // LANES
    devices = [(r, c) for r in range(rows_n) for c in range(cols_n)]
    plan = [[(r * row_size, row_size), ((c * rows_n + r) * slab_size, slab_size)] for r, c in devices]
    jac = exchange(run_network(plan), ("row", "col"))
    jac = jac.reshape(-1, *jac.shape[2:])
    hi, lo, hi_head, lo_head = stage(covariance, tile_rows // 4, tile_rows // 4)
    pieces = exchange(col_partial(jac, hi_head, lo_head, hi, lo, covariance, slab), "row")
    col_own, with_term, errors = slab_sum(pieces, jac, row_size)
    to_row = [(r * cols_n + c, c * rows_n + r) for r, c in devices]
    row_own = lax.ppermute(col_own, ("row", "col"), to_row)
    col_slabs = lax.all_gather(with_term, "row", axis=0, tiled=False)
    row_slabs = exchange(with_terms(row_own, col_slabs, cols_n), "col")
    head, right = read_head(covariance, col_slabs, streams)
    new_weight, new_cov = update(row_slabs, right, errors, layer_weight, head, covariance)
    return new_weight.reshape(-1), new_cov


def solution(mesh):
    in_specs = (
        P(("row", "col"), None),
        P(("row", "col"), None, None),
        P(("row", "col"), None, None),
        P(("row", "col"), None, None),
        P(("row", "col"), None),
        P(("row", "col")),
        P(),
        P(),
        P(),
        P("row", "col"),
    )
    out_specs = (P(("row", "col")), P("row", "col"))
    return jax.shard_map(
        on_device, mesh=mesh, in_specs=in_specs, out_specs=out_specs, check_vma=False
    )
```

```python
import functools
import math

import jax
import jax.numpy as jnp
from jax import lax
from jax.experimental import pallas as pl
from jax.experimental.pallas import tpu as pltpu
from jax.sharding import PartitionSpec as P

NEWTON = 4
LANES = 128
SUBLANES = 8


forget = 0.98
highest = lax.Precision.HIGHEST
f32 = jnp.float32
bf16 = jnp.bfloat16


def dot(left, right, contract, precision=None):
    return lax.dot_general(
        left, right, (contract, ((), ())), precision=precision, preferred_element_type=f32
    )


def split3(x):
    hi = x.astype(bf16)
    rest = x - hi.astype(f32)
    mid = rest.astype(bf16)
    lo = (rest - mid.astype(f32)).astype(bf16)
    return hi, mid, lo


def split2(x):
    hi = x.astype(bf16)
    return hi, (x - hi.astype(f32)).astype(bf16)


def limit(mib):
    return pltpu.CompilerParams(vmem_limit_bytes=mib << 20)


def five_products(parts, hi, lo, contract):
    streams = parts.shape[0] // 3
    by_hi = dot(parts, hi, contract)
    by_lo = dot(parts[0 : 2 * streams], lo, contract)
    return by_hi[0:streams] + (
        by_hi[streams : 2 * streams] + by_lo[0:streams] + (by_hi[2 * streams :] + by_lo[streams:])
    )


def network_kernel(
    types_ref,
    ids_ref,
    switch_ref,
    env_ref,
    force_ref,
    target_ref,
    embed_ref,
    weight_ref,
    out_weight_ref,
    payload_ref,
    mix_ref,
    *,
    plan,
):
    neighbours, atoms = ids_ref.shape
    n_types = embed_ref.shape[0]
    height = min(64, atoms)
    for start in range(0, atoms, height):
        atom_at = lax.broadcasted_iota(jnp.int32, (height, atoms), 0) + start
        total = jnp.zeros((height, atoms), f32)
        for k in range(neighbours):
            total = total + jnp.where(ids_ref[k : k + 1, :] == atom_at, switch_ref[k : k + 1, :], 0.0)
        mix_ref[start : start + height, :] = total
    mix = mix_ref[...]
    type_at = lax.broadcasted_iota(jnp.int32, (n_types, atoms), 0)
    onehot = (types_ref[...] == type_at).astype(f32)
    mixed = env_ref[...] + dot(embed_ref[...], onehot, ((0,), (0,)), highest)
    parts = jnp.concatenate(split3(mixed), axis=0)
    descriptor = five_products(parts, *split2(mix), ((1,), (0,))) * (1.0 / math.sqrt(neighbours))
    hidden = jnp.tanh(descriptor)
    activity = jnp.tanh(dot(hidden, weight_ref[...], ((0,), (0,)), highest))
    out_weight = out_weight_ref[...]
    scale = 1.0 / math.sqrt(atoms)
    force = force_ref[...]
    weighted = dot(force, activity, ((1,), (0,)), highest)
    predicted = jnp.sum(weighted * out_weight, axis=1, keepdims=True) * scale
    slopes = out_weight * (1.0 - activity * activity)
    parts = jnp.concatenate(split3(hidden * force), axis=0)
    jacobian = five_products(parts, *split2(slopes), ((1,), (0,))) * scale
    error = target_ref[...] - predicted
    for block, pieces in enumerate(plan):
        at = 0
        for start, size in pieces:
            payload_ref[block, at : at + size, :] = jacobian[start : start + size, :]
            at += size
        rest = payload_ref.shape[1] - at
        payload_ref[block, at:, :] = jnp.broadcast_to(error, (rest, jacobian.shape[1]))


def network(
    plan, atom_types, neighbor_ids, switching, environment, force_weights, targets, type_embed, layer_weight, out_weight
):
    per_dev, neighbours, atoms = neighbor_ids.shape
    hin, width = layer_weight.shape
    blocks = len(plan)
    rows = pl.cdiv(sum(size for _, size in plan[0]) + 1, SUBLANES) * SUBLANES

    def per_stream(*shape):
        return pl.BlockSpec((None,) + shape, lambda s: (s,) + (0,) * len(shape))

    def shared(shape):
        return pl.BlockSpec(shape, lambda s: (0,) * len(shape))

    return pl.pallas_call(
        functools.partial(network_kernel, plan=plan),
        grid=(per_dev,),
        in_specs=[
            per_stream(1, atoms),
            per_stream(neighbours, atoms),
            per_stream(neighbours, atoms),
            per_stream(hin, atoms),
            per_stream(1, atoms),
            per_stream(1, 1),
            shared(type_embed.shape),
            shared(layer_weight.shape),
            shared((1, width)),
        ],
        out_specs=pl.BlockSpec((blocks, None, rows, width), lambda s: (0, s, 0, 0)),
        out_shape=jax.ShapeDtypeStruct((blocks, per_dev, rows, width), f32),
        scratch_shapes=[pltpu.VMEM((atoms, atoms), f32)],
        name="network",
    )(
        atom_types.reshape(per_dev, 1, atoms),
        neighbor_ids,
        switching,
        environment.swapaxes(1, 2),
        force_weights.reshape(per_dev, 1, atoms),
        targets.reshape(per_dev, 1, 1),
        type_embed,
        layer_weight,
        out_weight.reshape(1, width),
    )


def in_hbm(x):
    return pltpu.with_memory_space_constraint(x, pltpu.HBM)


def in_vmem(x):
    return pltpu.with_memory_space_constraint(x, pltpu.VMEM)


def stage_kernel(cov_ref, hi_ref, lo_ref, hi_head_ref, lo_head_ref, *, head_steps):
    hi, lo = split2(cov_ref[...])
    hi_ref[...] = hi
    lo_ref[...] = lo

    @pl.when(pl.program_id(0) < head_steps)
    def _():
        hi_head_ref[...] = hi
        lo_head_ref[...] = lo


def stage(covariance, head, tail):
    rows, cols = covariance.shape
    height = min(rows // 8, head)
    head_steps = head // height
    block = pl.BlockSpec((height, cols), lambda n: (n, 0))
    rest_block = pl.BlockSpec((height, cols), lambda n: (jnp.maximum(n - head_steps, 0), 0))
    head_block = pl.BlockSpec((height, cols), lambda n: (jnp.minimum(n, head_steps - 1), 0))
    return pl.pallas_call(
        functools.partial(stage_kernel, head_steps=head_steps),
        grid=((rows - tail) // height,),
        in_specs=[block],
        out_specs=[rest_block, rest_block, head_block, head_block],
        out_shape=[pltpu.HBM((rows - head - tail, cols), bf16)] * 2 + [pltpu.VMEM((head, cols), bf16)] * 2,
        compiler_params=limit(12),
        name="stage",
    )(in_hbm(covariance))


def stacked_parts(flat, first, count, streams, stride, into_ref):
    lanes = flat.shape[1]
    for i in range(count):
        parts = split3(flat[pl.ds(first + i, streams, stride=stride), :])
        for n, part in enumerate(parts):
            into_ref[n * streams : (n + 1) * streams, i * lanes : (i + 1) * lanes] = part


def col_kernel(
    jac_ref,
    hi_head_ref,
    lo_head_ref,
    hi_ref,
    lo_ref,
    cov_ref,
    out_ref,
    parts_ref,
    hi_rest_ref,
    lo_rest_ref,
    tail_ref,
    sums_ref,
    sems,
    tail_sem,
):
    streams, rows, lanes = jac_ref.shape
    head, tile_cols = hi_head_ref.shape
    slabs, _, slab = out_ref.shape
    chunks = sems.shape[0]
    copies = []
    for n in range(chunks):
        here = pl.ds(n * head, head)
        copies.append(
            (
                pltpu.make_async_copy(hi_ref.at[here], hi_rest_ref.at[here], sems.at[n, 0]),
                pltpu.make_async_copy(lo_ref.at[here], lo_rest_ref.at[here], sems.at[n, 1]),
            )
        )
        for copy in copies[-1]:
            copy.start()
    tail = tail_ref.shape[0]
    last = pltpu.make_async_copy(cov_ref.at[pl.ds(cov_ref.shape[0] - tail, tail)], tail_ref, tail_sem)
    last.start()
    flat = jac_ref.reshape(streams * rows, lanes)
    stacked_parts(flat, 0, parts_ref.shape[1] // lanes, streams, rows, parts_ref)
    sums_ref[...] = five_products(parts_ref[:, 0:head], hi_head_ref[...], lo_head_ref[...], ((1,), (0,)))
    for n in range(chunks):
        for copy in copies[n]:
            copy.wait()
        here = slice(n * head, (n + 1) * head)
        sums_ref[...] += five_products(
            parts_ref[:, (n + 1) * head : (n + 2) * head], hi_rest_ref[here, :], lo_rest_ref[here, :], ((1,), (0,))
        )
    last.wait()
    sums_ref[...] += five_products(
        parts_ref[:, parts_ref.shape[1] - tail :], *split2(tail_ref[...]), ((1,), (0,))
    )
    for n in range(slabs):
        out_ref[n] = sums_ref[:, n * slab : (n + 1) * slab]


def col_partial(jac, hi_head, lo_head, hi, lo, covariance, slab):
    streams = jac.shape[0]
    rest, tile_cols = hi.shape
    head = hi_head.shape[0]
    tail = covariance.shape[0] - head - rest
    whole = pl.BlockSpec(memory_space=pltpu.VMEM)
    beyond = pl.BlockSpec(memory_space=pl.ANY)
    return pl.pallas_call(
        col_kernel,
        in_specs=[whole] * 3 + [beyond] * 3,
        out_specs=whole,
        out_shape=jax.ShapeDtypeStruct((tile_cols // slab, streams, slab), f32),
        scratch_shapes=[
            pltpu.VMEM((3 * streams, covariance.shape[0]), bf16),
            pltpu.VMEM((rest, tile_cols), bf16),
            pltpu.VMEM((rest, tile_cols), bf16),
            pltpu.VMEM((tail, tile_cols), f32),
            pltpu.VMEM((streams, tile_cols), f32),
            pltpu.SemaphoreType.DMA((rest // head, 2)),
            pltpu.SemaphoreType.DMA,
        ],
        compiler_params=limit(16),
        name="col_cross",
    )(jac, in_vmem(hi_head), in_vmem(lo_head), in_hbm(hi), in_hbm(lo), in_hbm(covariance))


def packed(term):
    streams = term.shape[0]
    groups = LANES // streams
    height = streams // groups
    return jnp.concatenate([term[n * height : (n + 1) * height] for n in range(groups)], axis=1)


def unpacked(rows, streams):
    return jnp.concatenate(
        [rows[:, n * streams : (n + 1) * streams] for n in range(LANES // streams)], axis=0
    )


def slab_kernel(pieces_ref, jac_ref, own_ref, out_ref, error_ref, *, first):
    streams, rows, lanes = jac_ref.shape
    slab = own_ref.shape[1]
    total = pieces_ref[0]
    for n in range(1, pieces_ref.shape[0]):
        total = total + pieces_ref[n]
    own_ref[...] = total
    flat = jac_ref.reshape(streams * rows, lanes)
    term = jnp.zeros((streams, streams), f32)
    for i in range(slab // lanes):
        own = flat[pl.ds(first + i, streams, stride=rows), :]
        here = total[:, i * lanes : (i + 1) * lanes]
        term = term + dot(own, here, ((1,), (1,)), highest)
        out_ref[i * streams : (i + 1) * streams, :] = here
    out_ref[slab // lanes * streams :, :] = packed(term)
    error_ref[...] = flat[pl.ds(first + slab // lanes, streams, stride=rows), :]


def slab_sum(pieces, jac, first):
    _, streams, slab = pieces.shape
    return pl.pallas_call(
        functools.partial(slab_kernel, first=first),
        out_shape=[
            jax.ShapeDtypeStruct((streams, slab), f32),
            jax.ShapeDtypeStruct((streams * (slab + streams) // LANES, LANES), f32),
            jax.ShapeDtypeStruct((streams, LANES), f32),
        ],
        compiler_params=limit(8),
        name="slab",
    )(pieces, jac)


def term_kernel(own_ref, cols_ref, out_ref):
    streams, slab = own_ref.shape
    _, lanes = out_ref.shape[1:]
    under = slab // lanes * streams
    term = cols_ref[0, under:, :]
    for n in range(1, cols_ref.shape[0]):
        term = term + cols_ref[n, under:, :]
    for n in range(out_ref.shape[0]):
        for i in range(slab // lanes):
            out_ref[n, i * streams : (i + 1) * streams, :] = own_ref[:, i * lanes : (i + 1) * lanes]
        out_ref[n, under:, :] = term


def with_terms(own, col_slabs, copies):
    return pl.pallas_call(
        term_kernel,
        out_shape=jax.ShapeDtypeStruct((copies,) + col_slabs.shape[1:], f32),
        compiler_params=limit(8),
        name="term",
    )(own, col_slabs)


def invert(innovation):
    streams = innovation.shape[0]
    row = lax.broadcasted_iota(jnp.int32, (streams, streams), 0)
    col = lax.broadcasted_iota(jnp.int32, (streams, streams), 1)
    identity = (row == col).astype(f32)
    innovation = innovation + forget * identity
    sums = jnp.sum(jnp.abs(innovation), axis=1, keepdims=True)
    bound = jnp.max(sums, axis=0, keepdims=True)
    power = identity - innovation / bound
    inverse = identity + power
    for repeat in range(NEWTON - 1):
        power = dot(power, power, ((1,), (0,)), highest)
        inverse = inverse + dot(inverse, power, ((1,), (0,)), highest)
    return inverse / bound


def head_kernel(cov_ref, _, head_ref, sem):
    copy = pltpu.make_async_copy(cov_ref.at[pl.ds(0, head_ref.shape[0])], head_ref, sem)
    copy.start()
    copy.wait()


def read_head(covariance, after):
    beyond = pl.BlockSpec(memory_space=pl.ANY)
    rows, cols = covariance.shape
    return pl.pallas_call(
        head_kernel,
        in_specs=[beyond, beyond],
        out_specs=pl.BlockSpec(memory_space=pltpu.VMEM),
        out_shape=pltpu.VMEM((rows // 4, cols), f32),
        scratch_shapes=[pltpu.SemaphoreType.DMA],
        compiler_params=limit(2),
        name="head",
    )(in_hbm(covariance), after)


def update_kernel(
    rows_ref, cols_ref, error_ref, weight_ref, head_ref, cov_ref, new_weight_ref, new_cov_ref, left_ref, right_ref, tile_ref, in_sems, out_sems
):
    slabs, _, lanes = rows_ref.shape
    streams = error_ref.shape[0]
    tile_rows = cov_ref.shape[0]
    slab = tile_rows // slabs
    under = slab // lanes * streams
    chunks = in_sems.shape[0]
    height = tile_rows // chunks
    held = head_ref.shape[0] // height
    reads = []
    for n in range(held, chunks):
        here = pl.ds(n * height, height)
        reads.append(pltpu.make_async_copy(cov_ref.at[here], tile_ref.at[here], in_sems.at[n]))
        reads[-1].start()
    term = rows_ref[0, under:, :]
    for n in range(1, slabs):
        term = term + rows_ref[n, under:, :]
    inverse = invert(unpacked(term, streams))
    errors = error_ref[:, 0:1]
    for n in range(cols_ref.shape[0]):
        for i in range(slab // lanes):
            hi, mid, lo = split3(cols_ref[n, i * streams : (i + 1) * streams, :])
            at = n * slab + i * lanes
            for m, part in enumerate((hi, mid, lo, hi, mid, hi)):
                right_ref[m * streams : (m + 1) * streams, at : at + lanes] = part
    cross = jnp.concatenate(
        [rows_ref[n, i : i + streams, :] for n in range(slabs) for i in range(0, under, streams)], axis=1
    )
    gain = dot(inverse, cross, ((0,), (0,)), highest)
    hi, mid, lo = split3(gain)
    for m, part in enumerate((hi, hi, hi, mid, mid, lo)):
        left_ref[m * streams : (m + 1) * streams, :] = part
    writes = []
    for n in range(chunks):
        update = dot(left_ref[:, n * height : (n + 1) * height], right_ref[...], ((0,), (0,)))
        here = pl.ds(n * height, height)
        if n >= held:
            reads[n - held].wait()
        before = head_ref if n < held else tile_ref
        tile_ref[here, :] = (before[here, :] - update) * (1.0 / forget)
        writes.append(pltpu.make_async_copy(tile_ref.at[here], new_cov_ref.at[here], out_sems.at[n]))
        writes[-1].start()
    col_at = lax.axis_index("col")
    own_at = (lax.axis_index("row") * slabs + col_at) * (slab // lanes)
    for n in range(slabs):

        @pl.when(col_at == n)
        def _():
            moved = jnp.sum(gain[:, n * slab : (n + 1) * slab] * errors, axis=0, keepdims=True)
            for i in range(slab // lanes):
                own = weight_ref[pl.ds(own_at + i, 1), :]
                new_weight_ref[i : i + 1, :] = own + moved[:, i * lanes : (i + 1) * lanes]

    for write in writes:
        write.wait()


def update(row_slabs, col_slabs, errors, layer_weight, head, covariance):
    streams = errors.shape[0]
    tile_rows, tile_cols = covariance.shape
    slab = tile_rows // row_slabs.shape[0]
    width = layer_weight.shape[1]
    whole = pl.BlockSpec(memory_space=pltpu.VMEM)
    beyond = pl.BlockSpec(memory_space=pl.ANY)
    return pl.pallas_call(
        update_kernel,
        in_specs=[whole] * 5 + [beyond],
        out_specs=[whole, beyond],
        out_shape=[
            jax.ShapeDtypeStruct((slab // width, width), f32),
            jax.ShapeDtypeStruct((tile_rows, tile_cols), f32),
        ],
        scratch_shapes=[
            pltpu.VMEM((6 * streams, tile_rows), bf16),
            pltpu.VMEM((6 * streams, tile_cols), bf16),
            pltpu.VMEM((tile_rows, tile_cols), f32),
            pltpu.SemaphoreType.DMA((8,)),
            pltpu.SemaphoreType.DMA((8,)),
        ],
        compiler_params=limit(20),
        name="update",
    )(row_slabs, col_slabs, errors, layer_weight, in_vmem(head), in_hbm(covariance))


def plain_steps(at, jac_all, errors, layer_weight, covariance, slab, cols_n):
    streams = jac_all.shape[0]
    hin, width = layer_weight.shape
    tile_rows, tile_cols = covariance.shape
    first = (at[0] * cols_n + at[1]) * slab
    jacobian = jac_all[:, 0:hin, :].reshape(streams, hin * width)
    jac_cols = lax.dynamic_slice_in_dim(jacobian, at[1] * tile_cols, tile_cols, 1)
    partial = dot(jac_cols, covariance, ((1,), (1,)), highest)
    cross_own = lax.psum_scatter(partial, "col", scatter_dimension=1, tiled=True)
    cross = lax.all_gather(cross_own, ("row", "col"), axis=1, tiled=True)
    inverse = invert(dot(jacobian, cross, ((1,), (1,)), highest))
    gain = dot(inverse, lax.dynamic_slice_in_dim(cross, at[0] * tile_rows, tile_rows, 1), ((0,), (0,)), highest)
    across = lax.dynamic_slice_in_dim(cross, at[1] * tile_cols, tile_cols, 1)
    new_cov = (covariance - dot(gain, across, ((0,), (0,)), highest)) / forget
    own_gain = lax.dynamic_slice_in_dim(gain, at[1] * slab, slab, 1)
    own_weight = lax.dynamic_slice_in_dim(layer_weight.reshape(-1), first, slab, 0)
    new_weight = own_weight + dot(errors, own_gain, ((0,), (0,)), highest)
    return new_weight, new_cov


def exchange(x, axes):
    return lax.all_to_all(x, axes, split_axis=0, concat_axis=0, tiled=True)


def on_device(
    atom_types,
    neighbor_ids,
    switching,
    environment,
    force_weights,
    targets,
    type_embed,
    layer_weight,
    out_weight,
    covariance,
):
    rows_n = lax.axis_size("row")
    cols_n = lax.axis_size("col")
    at = jnp.stack([lax.axis_index("row"), lax.axis_index("col")]).astype(jnp.int32)
    tile_rows, tile_cols = covariance.shape
    slab = tile_rows // cols_n
    hin, width = layer_weight.shape
    run_network = functools.partial(
        network,
        atom_types=atom_types,
        neighbor_ids=neighbor_ids,
        switching=switching,
        environment=environment,
        force_weights=force_weights,
        targets=targets,
        type_embed=type_embed,
        layer_weight=layer_weight,
        out_weight=out_weight,
    )
    streams = rows_n * cols_n * atom_types.shape[0]
    kernels = (
        atom_types.shape[0] == 1
        and width == LANES
        and slab % LANES == 0
        and tile_rows % (SUBLANES * LANES) == 0
        and tile_cols % (SUBLANES * LANES) == 0
        and rows_n * slab == tile_cols
        and LANES % streams == 0
        and streams * streams % (SUBLANES * LANES) == 0
    )
    if not kernels:
        payload = run_network([[(0, hin)]])[0]
        jac_all = lax.all_gather(payload, ("row", "col"), axis=0, tiled=True)
        return plain_steps(at, jac_all[:, 0:hin], jac_all[:, hin, 0], layer_weight, covariance, slab, cols_n)
    row_size, slab_size = tile_rows // LANES, slab // LANES
    devices = [(r, c) for r in range(rows_n) for c in range(cols_n)]
    plan = [[(r * row_size, row_size), ((c * rows_n + r) * slab_size, slab_size)] for r, c in devices]
    jac = exchange(run_network(plan), ("row", "col"))
    jac = jac.reshape(-1, *jac.shape[2:])
    hi, lo, hi_head, lo_head = stage(covariance, tile_rows // 8 * 3, tile_rows // 4)
    col_part = col_partial(jac, hi_head, lo_head, hi, lo, covariance, slab)
    pieces = exchange(col_part, "row")
    head = read_head(covariance, col_part)
    col_own, with_term, errors = slab_sum(pieces, jac, row_size)
    to_row = [(r * cols_n + c, c * rows_n + r) for r, c in devices]
    row_own = lax.ppermute(col_own, ("row", "col"), to_row)
    col_slabs = lax.all_gather(with_term, "row", axis=0, tiled=False)
    row_slabs = exchange(with_terms(row_own, col_slabs, cols_n), "col")
    new_weight, new_cov = update(row_slabs, col_slabs, errors, layer_weight, head, covariance)
    return new_weight.reshape(-1), new_cov


def solution(mesh):
    in_specs = (
        P(("row", "col"), None),
        P(("row", "col"), None, None),
        P(("row", "col"), None, None),
        P(("row", "col"), None, None),
        P(("row", "col"), None),
        P(("row", "col")),
        P(),
        P(),
        P(),
        P("row", "col"),
    )
    out_specs = (P(("row", "col")), P("row", "col"))
    return jax.shard_map(
        on_device, mesh=mesh, in_specs=in_specs, out_specs=out_specs, check_vma=False
    )
```

```python
import functools
import math

import jax
import jax.numpy as jnp
from jax import lax
from jax.experimental import pallas as pl
from jax.experimental.pallas import tpu as pltpu
from jax.sharding import PartitionSpec as P

NEWTON = 4
LANES = 128
SUBLANES = 8


forget = 0.98
highest = lax.Precision.HIGHEST
f32 = jnp.float32
bf16 = jnp.bfloat16


def dot(left, right, contract, precision=None):
    return lax.dot_general(
        left, right, (contract, ((), ())), precision=precision, preferred_element_type=f32
    )


def split3(x):
    hi = x.astype(bf16)
    rest = x - hi.astype(f32)
    mid = rest.astype(bf16)
    lo = (rest - mid.astype(f32)).astype(bf16)
    return hi, mid, lo


def split2(x):
    hi = x.astype(bf16)
    return hi, (x - hi.astype(f32)).astype(bf16)


def limit(mib):
    return pltpu.CompilerParams(vmem_limit_bytes=mib << 20)


def five_products(parts, hi, lo, contract):
    streams = parts.shape[0] // 3
    by_hi = dot(parts, hi, contract)
    by_lo = dot(parts[0 : 2 * streams], lo, contract)
    return by_hi[0:streams] + (
        by_hi[streams : 2 * streams] + by_lo[0:streams] + (by_hi[2 * streams :] + by_lo[streams:])
    )


def network_kernel(
    types_ref,
    ids_ref,
    switch_ref,
    env_ref,
    force_ref,
    target_ref,
    embed_ref,
    weight_ref,
    out_weight_ref,
    payload_ref,
    mix_ref,
    *,
    plan,
):
    neighbours, atoms = ids_ref.shape
    n_types = embed_ref.shape[0]
    height = min(64, atoms)
    for start in range(0, atoms, height):
        atom_at = lax.broadcasted_iota(jnp.int32, (height, atoms), 0) + start
        total = jnp.zeros((height, atoms), f32)
        for k in range(neighbours):
            total = total + jnp.where(ids_ref[k : k + 1, :] == atom_at, switch_ref[k : k + 1, :], 0.0)
        mix_ref[start : start + height, :] = total
    mix = mix_ref[...]
    type_at = lax.broadcasted_iota(jnp.int32, (n_types, atoms), 0)
    onehot = (types_ref[...] == type_at).astype(f32)
    mixed = env_ref[...] + dot(embed_ref[...], onehot, ((0,), (0,)), highest)
    parts = jnp.concatenate(split3(mixed), axis=0)
    descriptor = five_products(parts, *split2(mix), ((1,), (0,))) * (1.0 / math.sqrt(neighbours))
    hidden = jnp.tanh(descriptor)
    activity = jnp.tanh(dot(hidden, weight_ref[...], ((0,), (0,)), highest))
    out_weight = out_weight_ref[...]
    scale = 1.0 / math.sqrt(atoms)
    force = force_ref[...]
    weighted = dot(force, activity, ((1,), (0,)), highest)
    predicted = jnp.sum(weighted * out_weight, axis=1, keepdims=True) * scale
    slopes = out_weight * (1.0 - activity * activity)
    parts = jnp.concatenate(split3(hidden * force), axis=0)
    jacobian = five_products(parts, *split2(slopes), ((1,), (0,))) * scale
    error = target_ref[...] - predicted
    for block, pieces in enumerate(plan):
        at = 0
        for start, size in pieces:
            payload_ref[block, at : at + size, :] = jacobian[start : start + size, :]
            at += size
        rest = payload_ref.shape[1] - at
        payload_ref[block, at:, :] = jnp.broadcast_to(error, (rest, jacobian.shape[1]))


def network(
    plan, atom_types, neighbor_ids, switching, environment, force_weights, targets, type_embed, layer_weight, out_weight
):
    per_dev, neighbours, atoms = neighbor_ids.shape
    hin, width = layer_weight.shape
    blocks = len(plan)
    rows = pl.cdiv(sum(size for _, size in plan[0]) + 1, SUBLANES) * SUBLANES

    def per_stream(*shape):
        return pl.BlockSpec((None,) + shape, lambda s: (s,) + (0,) * len(shape))

    def shared(shape):
        return pl.BlockSpec(shape, lambda s: (0,) * len(shape))

    return pl.pallas_call(
        functools.partial(network_kernel, plan=plan),
        grid=(per_dev,),
        in_specs=[
            per_stream(1, atoms),
            per_stream(neighbours, atoms),
            per_stream(neighbours, atoms),
            per_stream(hin, atoms),
            per_stream(1, atoms),
            per_stream(1, 1),
            shared(type_embed.shape),
            shared(layer_weight.shape),
            shared((1, width)),
        ],
        out_specs=pl.BlockSpec((blocks, None, rows, width), lambda s: (0, s, 0, 0)),
        out_shape=jax.ShapeDtypeStruct((blocks, per_dev, rows, width), f32),
        scratch_shapes=[pltpu.VMEM((atoms, atoms), f32)],
        name="network",
    )(
        atom_types.reshape(per_dev, 1, atoms),
        neighbor_ids,
        switching,
        environment.swapaxes(1, 2),
        force_weights.reshape(per_dev, 1, atoms),
        targets.reshape(per_dev, 1, 1),
        type_embed,
        layer_weight,
        out_weight.reshape(1, width),
    )


def in_hbm(x):
    return pltpu.with_memory_space_constraint(x, pltpu.HBM)


def in_vmem(x):
    return pltpu.with_memory_space_constraint(x, pltpu.VMEM)


def stage_kernel(cov_ref, hi_ref, lo_ref, hi_head_ref, lo_head_ref, *, head_steps):
    hi, lo = split2(cov_ref[...])
    hi_ref[...] = hi
    lo_ref[...] = lo

    @pl.when(pl.program_id(0) < head_steps)
    def _():
        hi_head_ref[...] = hi
        lo_head_ref[...] = lo


def stage(covariance, head, tail):
    rows, cols = covariance.shape
    height = min(rows // 8, head)
    head_steps = head // height
    block = pl.BlockSpec((height, cols), lambda n: (n, 0))
    rest_block = pl.BlockSpec((height, cols), lambda n: (jnp.maximum(n - head_steps, 0), 0))
    head_block = pl.BlockSpec((height, cols), lambda n: (jnp.minimum(n, head_steps - 1), 0))
    return pl.pallas_call(
        functools.partial(stage_kernel, head_steps=head_steps),
        grid=((rows - tail) // height,),
        in_specs=[block],
        out_specs=[rest_block, rest_block, head_block, head_block],
        out_shape=[pltpu.HBM((rows - head - tail, cols), bf16)] * 2 + [pltpu.VMEM((head, cols), bf16)] * 2,
        compiler_params=limit(12),
        name="stage",
    )(in_hbm(covariance))


def stacked_parts(flat, first, count, streams, stride, into_ref):
    lanes = flat.shape[1]
    for i in range(count):
        parts = split3(flat[pl.ds(first + i, streams, stride=stride), :])
        for n, part in enumerate(parts):
            into_ref[n * streams : (n + 1) * streams, i * lanes : (i + 1) * lanes] = part


def col_kernel(
    jac_ref,
    hi_head_ref,
    lo_head_ref,
    hi_ref,
    lo_ref,
    cov_ref,
    out_ref,
    parts_ref,
    hi_rest_ref,
    lo_rest_ref,
    tail_ref,
    sums_ref,
    sems,
    tail_sem,
):
    streams, rows, lanes = jac_ref.shape
    head, tile_cols = hi_head_ref.shape
    slabs, _, slab = out_ref.shape
    chunks = sems.shape[0]
    copies = []
    for n in range(chunks):
        here = pl.ds(n * head, head)
        copies.append(
            (
                pltpu.make_async_copy(hi_ref.at[here], hi_rest_ref.at[here], sems.at[n, 0]),
                pltpu.make_async_copy(lo_ref.at[here], lo_rest_ref.at[here], sems.at[n, 1]),
            )
        )
        for copy in copies[-1]:
            copy.start()
    tail = tail_ref.shape[0]
    last = pltpu.make_async_copy(cov_ref.at[pl.ds(cov_ref.shape[0] - tail, tail)], tail_ref, tail_sem)
    last.start()
    flat = jac_ref.reshape(streams * rows, lanes)
    stacked_parts(flat, 0, parts_ref.shape[1] // lanes, streams, rows, parts_ref)
    sums_ref[...] = five_products(parts_ref[:, 0:head], hi_head_ref[...], lo_head_ref[...], ((1,), (0,)))
    for n in range(chunks):
        for copy in copies[n]:
            copy.wait()
        here = slice(n * head, (n + 1) * head)
        sums_ref[...] += five_products(
            parts_ref[:, (n + 1) * head : (n + 2) * head], hi_rest_ref[here, :], lo_rest_ref[here, :], ((1,), (0,))
        )
    last.wait()
    sums_ref[...] += five_products(
        parts_ref[:, parts_ref.shape[1] - tail :], *split2(tail_ref[...]), ((1,), (0,))
    )
    for n in range(slabs):
        out_ref[n] = sums_ref[:, n * slab : (n + 1) * slab]


def col_partial(jac, hi_head, lo_head, hi, lo, covariance, slab):
    streams = jac.shape[0]
    rest, tile_cols = hi.shape
    head = hi_head.shape[0]
    tail = covariance.shape[0] - head - rest
    whole = pl.BlockSpec(memory_space=pltpu.VMEM)
    beyond = pl.BlockSpec(memory_space=pl.ANY)
    return pl.pallas_call(
        col_kernel,
        in_specs=[whole] * 3 + [beyond] * 3,
        out_specs=whole,
        out_shape=jax.ShapeDtypeStruct((tile_cols // slab, streams, slab), f32),
        scratch_shapes=[
            pltpu.VMEM((3 * streams, covariance.shape[0]), bf16),
            pltpu.VMEM((rest, tile_cols), bf16),
            pltpu.VMEM((rest, tile_cols), bf16),
            pltpu.VMEM((tail, tile_cols), f32),
            pltpu.VMEM((streams, tile_cols), f32),
            pltpu.SemaphoreType.DMA((rest // head, 2)),
            pltpu.SemaphoreType.DMA,
        ],
        compiler_params=limit(16),
        name="col_cross",
    )(jac, in_vmem(hi_head), in_vmem(lo_head), in_hbm(hi), in_hbm(lo), in_hbm(covariance))


def packed(term):
    streams = term.shape[0]
    groups = LANES // streams
    height = streams // groups
    return jnp.concatenate([term[n * height : (n + 1) * height] for n in range(groups)], axis=1)


def unpacked(rows, streams):
    return jnp.concatenate(
        [rows[:, n * streams : (n + 1) * streams] for n in range(LANES // streams)], axis=0
    )


def slab_kernel(pieces_ref, jac_ref, own_ref, out_ref, error_ref, *, first):
    streams, rows, lanes = jac_ref.shape
    slab = own_ref.shape[1]
    total = pieces_ref[0]
    for n in range(1, pieces_ref.shape[0]):
        total = total + pieces_ref[n]
    own_ref[...] = total
    flat = jac_ref.reshape(streams * rows, lanes)
    term = jnp.zeros((streams, streams), f32)
    for i in range(slab // lanes):
        own = flat[pl.ds(first + i, streams, stride=rows), :]
        here = total[:, i * lanes : (i + 1) * lanes]
        term = term + dot(own, here, ((1,), (1,)), highest)
        out_ref[i * streams : (i + 1) * streams, :] = here
    out_ref[slab // lanes * streams :, :] = packed(term)
    error_ref[...] = flat[pl.ds(first + slab // lanes, streams, stride=rows), :]


def slab_sum(pieces, jac, first):
    _, streams, slab = pieces.shape
    return pl.pallas_call(
        functools.partial(slab_kernel, first=first),
        out_shape=[
            jax.ShapeDtypeStruct((streams, slab), f32),
            jax.ShapeDtypeStruct((streams * (slab + streams) // LANES, LANES), f32),
            jax.ShapeDtypeStruct((streams, LANES), f32),
        ],
        compiler_params=limit(8),
        name="slab",
    )(pieces, jac)


def term_kernel(own_ref, cols_ref, out_ref):
    streams, slab = own_ref.shape
    _, lanes = out_ref.shape[1:]
    under = slab // lanes * streams
    term = cols_ref[0, under:, :]
    for n in range(1, cols_ref.shape[0]):
        term = term + cols_ref[n, under:, :]
    for n in range(out_ref.shape[0]):
        for i in range(slab // lanes):
            out_ref[n, i * streams : (i + 1) * streams, :] = own_ref[:, i * lanes : (i + 1) * lanes]
        out_ref[n, under:, :] = term


def with_terms(own, col_slabs, copies):
    return pl.pallas_call(
        term_kernel,
        out_shape=jax.ShapeDtypeStruct((copies,) + col_slabs.shape[1:], f32),
        compiler_params=limit(8),
        name="term",
    )(own, col_slabs)


def invert(innovation):
    streams = innovation.shape[0]
    row = lax.broadcasted_iota(jnp.int32, (streams, streams), 0)
    col = lax.broadcasted_iota(jnp.int32, (streams, streams), 1)
    identity = (row == col).astype(f32)
    innovation = innovation + forget * identity
    sums = jnp.sum(jnp.abs(innovation), axis=1, keepdims=True)
    bound = jnp.max(sums, axis=0, keepdims=True)
    power = identity - innovation / bound
    inverse = identity + power
    for repeat in range(NEWTON - 1):
        power = dot(power, power, ((1,), (0,)), highest)
        inverse = inverse + dot(inverse, power, ((1,), (0,)), highest)
    return inverse / bound


def head_kernel(cov_ref, _, head_ref, sem):
    copy = pltpu.make_async_copy(cov_ref.at[pl.ds(0, head_ref.shape[0])], head_ref, sem)
    copy.start()
    copy.wait()


def read_head(covariance, after):
    beyond = pl.BlockSpec(memory_space=pl.ANY)
    rows, cols = covariance.shape
    return pl.pallas_call(
        head_kernel,
        in_specs=[beyond, beyond],
        out_specs=pl.BlockSpec(memory_space=pltpu.VMEM),
        out_shape=pltpu.VMEM((rows // 4, cols), f32),
        scratch_shapes=[pltpu.SemaphoreType.DMA],
        compiler_params=limit(2),
        name="head",
    )(in_hbm(covariance), after)


def update_kernel(
    rows_ref, cols_ref, error_ref, weight_ref, head_ref, cov_ref, new_weight_ref, new_cov_ref, left_ref, right_ref, tile_ref, in_sems, out_sems
):
    slabs, _, lanes = rows_ref.shape
    streams = error_ref.shape[0]
    tile_rows = cov_ref.shape[0]
    slab = tile_rows // slabs
    under = slab // lanes * streams
    chunks = in_sems.shape[0]
    height = tile_rows // chunks
    held = head_ref.shape[0] // height
    reads = []
    for n in range(held, chunks):
        here = pl.ds(n * height, height)
        reads.append(pltpu.make_async_copy(cov_ref.at[here], tile_ref.at[here], in_sems.at[n]))
        reads[-1].start()
    term = rows_ref[0, under:, :]
    for n in range(1, slabs):
        term = term + rows_ref[n, under:, :]
    inverse = invert(unpacked(term, streams))
    errors = error_ref[:, 0:1]
    for n in range(cols_ref.shape[0]):
        for i in range(slab // lanes):
            hi, mid, lo = split3(cols_ref[n, i * streams : (i + 1) * streams, :])
            at = n * slab + i * lanes
            for m, part in enumerate((hi, mid, lo, hi, mid, hi)):
                right_ref[m * streams : (m + 1) * streams, at : at + lanes] = part
    cross = jnp.concatenate(
        [rows_ref[n, i : i + streams, :] for n in range(slabs) for i in range(0, under, streams)], axis=1
    )
    gain = dot(inverse, cross, ((0,), (0,)), highest)
    hi, mid, lo = split3(gain)
    for m, part in enumerate((hi, hi, hi, mid, mid, lo)):
        left_ref[m * streams : (m + 1) * streams, :] = part
    writes = []
    for n in range(chunks):
        update = dot(left_ref[:, n * height : (n + 1) * height], right_ref[...], ((0,), (0,)))
        here = pl.ds(n * height, height)
        if n >= held:
            reads[n - held].wait()
        before = head_ref if n < held else tile_ref
        tile_ref[here, :] = (before[here, :] - update) * (1.0 / forget)
        writes.append(pltpu.make_async_copy(tile_ref.at[here], new_cov_ref.at[here], out_sems.at[n]))
        writes[-1].start()
    col_at = lax.axis_index("col")
    own_at = (lax.axis_index("row") * slabs + col_at) * (slab // lanes)
    for n in range(slabs):

        @pl.when(col_at == n)
        def _():
            moved = jnp.sum(gain[:, n * slab : (n + 1) * slab] * errors, axis=0, keepdims=True)
            for i in range(slab // lanes):
                own = weight_ref[pl.ds(own_at + i, 1), :]
                new_weight_ref[i : i + 1, :] = own + moved[:, i * lanes : (i + 1) * lanes]

    for write in writes:
        write.wait()


def update(row_slabs, col_slabs, errors, layer_weight, head, covariance):
    streams = errors.shape[0]
    tile_rows, tile_cols = covariance.shape
    slab = tile_rows // row_slabs.shape[0]
    width = layer_weight.shape[1]
    whole = pl.BlockSpec(memory_space=pltpu.VMEM)
    beyond = pl.BlockSpec(memory_space=pl.ANY)
    return pl.pallas_call(
        update_kernel,
        in_specs=[whole] * 5 + [beyond],
        out_specs=[whole, beyond],
        out_shape=[
            jax.ShapeDtypeStruct((slab // width, width), f32),
            jax.ShapeDtypeStruct((tile_rows, tile_cols), f32),
        ],
        scratch_shapes=[
            pltpu.VMEM((6 * streams, tile_rows), bf16),
            pltpu.VMEM((6 * streams, tile_cols), bf16),
            pltpu.VMEM((tile_rows, tile_cols), f32),
            pltpu.SemaphoreType.DMA((8,)),
            pltpu.SemaphoreType.DMA((8,)),
        ],
        compiler_params=limit(20),
        name="update",
    )(row_slabs, col_slabs, errors, layer_weight, in_vmem(head), in_hbm(covariance))


def plain_steps(at, jac_all, errors, layer_weight, covariance, slab, cols_n):
    streams = jac_all.shape[0]
    hin, width = layer_weight.shape
    tile_rows, tile_cols = covariance.shape
    first = (at[0] * cols_n + at[1]) * slab
    jacobian = jac_all[:, 0:hin, :].reshape(streams, hin * width)
    jac_cols = lax.dynamic_slice_in_dim(jacobian, at[1] * tile_cols, tile_cols, 1)
    partial = dot(jac_cols, covariance, ((1,), (1,)), highest)
    cross_own = lax.psum_scatter(partial, "col", scatter_dimension=1, tiled=True)
    cross = lax.all_gather(cross_own, ("row", "col"), axis=1, tiled=True)
    inverse = invert(dot(jacobian, cross, ((1,), (1,)), highest))
    gain = dot(inverse, lax.dynamic_slice_in_dim(cross, at[0] * tile_rows, tile_rows, 1), ((0,), (0,)), highest)
    across = lax.dynamic_slice_in_dim(cross, at[1] * tile_cols, tile_cols, 1)
    new_cov = (covariance - dot(gain, across, ((0,), (0,)), highest)) / forget
    own_gain = lax.dynamic_slice_in_dim(gain, at[1] * slab, slab, 1)
    own_weight = lax.dynamic_slice_in_dim(layer_weight.reshape(-1), first, slab, 0)
    new_weight = own_weight + dot(errors, own_gain, ((0,), (0,)), highest)
    return new_weight, new_cov


def exchange(x, axes):
    return lax.all_to_all(x, axes, split_axis=0, concat_axis=0, tiled=True)


def on_device(
    atom_types,
    neighbor_ids,
    switching,
    environment,
    force_weights,
    targets,
    type_embed,
    layer_weight,
    out_weight,
    covariance,
):
    rows_n = lax.axis_size("row")
    cols_n = lax.axis_size("col")
    at = jnp.stack([lax.axis_index("row"), lax.axis_index("col")]).astype(jnp.int32)
    tile_rows, tile_cols = covariance.shape
    slab = tile_rows // cols_n
    hin, width = layer_weight.shape
    run_network = functools.partial(
        network,
        atom_types=atom_types,
        neighbor_ids=neighbor_ids,
        switching=switching,
        environment=environment,
        force_weights=force_weights,
        targets=targets,
        type_embed=type_embed,
        layer_weight=layer_weight,
        out_weight=out_weight,
    )
    streams = rows_n * cols_n * atom_types.shape[0]
    kernels = (
        atom_types.shape[0] == 1
        and width == LANES
        and slab % LANES == 0
        and tile_rows % (SUBLANES * LANES) == 0
        and tile_cols % (SUBLANES * LANES) == 0
        and rows_n * slab == tile_cols
        and LANES % streams == 0
        and streams * streams % (SUBLANES * LANES) == 0
    )
    if not kernels:
        payload = run_network([[(0, hin)]])[0]
        jac_all = lax.all_gather(payload, ("row", "col"), axis=0, tiled=True)
        return plain_steps(at, jac_all[:, 0:hin], jac_all[:, hin, 0], layer_weight, covariance, slab, cols_n)
    row_size, slab_size = tile_rows // LANES, slab // LANES
    devices = [(r, c) for r in range(rows_n) for c in range(cols_n)]
    plan = [[(r * row_size, row_size), ((c * rows_n + r) * slab_size, slab_size)] for r, c in devices]
    jac = exchange(run_network(plan), ("row", "col"))
    jac = jac.reshape(-1, *jac.shape[2:])
    hi, lo, hi_head, lo_head = stage(covariance, tile_rows // 4, tile_rows // 4)
    col_part = col_partial(jac, hi_head, lo_head, hi, lo, covariance, slab)
    pieces = exchange(col_part, "row")
    head = read_head(covariance, col_part)
    col_own, with_term, errors = slab_sum(pieces, jac, row_size)
    to_row = [(r * cols_n + c, c * rows_n + r) for r, c in devices]
    row_own = lax.ppermute(col_own, ("row", "col"), to_row)
    col_slabs = lax.all_gather(with_term, "row", axis=0, tiled=False)
    row_slabs = exchange(with_terms(row_own, col_slabs, cols_n), "col")
    new_weight, new_cov = update(row_slabs, col_slabs, errors, layer_weight, head, covariance)
    return new_weight.reshape(-1), new_cov


def solution(mesh):
    in_specs = (
        P(("row", "col"), None),
        P(("row", "col"), None, None),
        P(("row", "col"), None, None),
        P(("row", "col"), None, None),
        P(("row", "col"), None),
        P(("row", "col")),
        P(),
        P(),
        P(),
        P("row", "col"),
    )
    out_specs = (P(("row", "col")), P("row", "col"))
    return jax.shard_map(
        on_device, mesh=mesh, in_specs=in_specs, out_specs=out_specs, check_vma=False
    )
```

```python
import functools
import math

import jax
import jax.numpy as jnp
from jax import lax
from jax.experimental import pallas as pl
from jax.experimental.pallas import tpu as pltpu
from jax.sharding import PartitionSpec as P

NEWTON = 4
LANES = 128
SUBLANES = 8


forget = 0.98
highest = lax.Precision.HIGHEST
f32 = jnp.float32
bf16 = jnp.bfloat16


def dot(left, right, contract, precision=None):
    return lax.dot_general(
        left, right, (contract, ((), ())), precision=precision, preferred_element_type=f32
    )


def split3(x):
    hi = x.astype(bf16)
    rest = x - hi.astype(f32)
    mid = rest.astype(bf16)
    lo = (rest - mid.astype(f32)).astype(bf16)
    return hi, mid, lo


def split2(x):
    hi = x.astype(bf16)
    return hi, (x - hi.astype(f32)).astype(bf16)


def limit(mib):
    return pltpu.CompilerParams(vmem_limit_bytes=mib << 20)


def five_products(parts, hi, lo, contract):
    streams = parts.shape[0] // 3
    by_hi = dot(parts, hi, contract)
    by_lo = dot(parts[0 : 2 * streams], lo, contract)
    return by_hi[0:streams] + (
        by_hi[streams : 2 * streams] + by_lo[0:streams] + (by_hi[2 * streams :] + by_lo[streams:])
    )


def network_kernel(
    types_ref,
    ids_ref,
    switch_ref,
    env_ref,
    force_ref,
    target_ref,
    embed_ref,
    weight_ref,
    out_weight_ref,
    payload_ref,
    mix_ref,
    *,
    plan,
):
    neighbours, atoms = ids_ref.shape
    n_types = embed_ref.shape[0]
    height = min(64, atoms)
    for start in range(0, atoms, height):
        atom_at = lax.broadcasted_iota(jnp.int32, (height, atoms), 0) + start
        total = jnp.zeros((height, atoms), f32)
        for k in range(neighbours):
            total = total + jnp.where(ids_ref[k : k + 1, :] == atom_at, switch_ref[k : k + 1, :], 0.0)
        mix_ref[start : start + height, :] = total
    mix = mix_ref[...]
    type_at = lax.broadcasted_iota(jnp.int32, (n_types, atoms), 0)
    onehot = (types_ref[...] == type_at).astype(f32)
    mixed = env_ref[...] + dot(embed_ref[...], onehot, ((0,), (0,)), highest)
    parts = jnp.concatenate(split3(mixed), axis=0)
    descriptor = five_products(parts, *split2(mix), ((1,), (0,))) * (1.0 / math.sqrt(neighbours))
    hidden = jnp.tanh(descriptor)
    activity = jnp.tanh(dot(hidden, weight_ref[...], ((0,), (0,)), highest))
    out_weight = out_weight_ref[...]
    scale = 1.0 / math.sqrt(atoms)
    force = force_ref[...]
    weighted = dot(force, activity, ((1,), (0,)), highest)
    predicted = jnp.sum(weighted * out_weight, axis=1, keepdims=True) * scale
    slopes = out_weight * (1.0 - activity * activity)
    parts = jnp.concatenate(split3(hidden * force), axis=0)
    jacobian = five_products(parts, *split2(slopes), ((1,), (0,))) * scale
    error = target_ref[...] - predicted
    at = 0
    for pieces in plan:
        for start, size in pieces:
            payload_ref[at : at + size, :] = jacobian[start : start + size, :]
            at += size
        payload_ref[at : at + 1, :] = jnp.broadcast_to(error, (1, jacobian.shape[1]))
        at += 1


def network(
    plan, atom_types, neighbor_ids, switching, environment, force_weights, targets, type_embed, layer_weight, out_weight
):
    per_dev, neighbours, atoms = neighbor_ids.shape
    hin, width = layer_weight.shape
    rows = sum(1 + sum(size for _, size in pieces) for pieces in plan)

    def per_stream(*shape):
        return pl.BlockSpec((None,) + shape, lambda s: (s,) + (0,) * len(shape))

    def shared(shape):
        return pl.BlockSpec(shape, lambda s: (0,) * len(shape))

    return pl.pallas_call(
        functools.partial(network_kernel, plan=plan),
        grid=(per_dev,),
        in_specs=[
            per_stream(1, atoms),
            per_stream(neighbours, atoms),
            per_stream(neighbours, atoms),
            per_stream(hin, atoms),
            per_stream(1, atoms),
            per_stream(1, 1),
            shared(type_embed.shape),
            shared(layer_weight.shape),
            shared((1, width)),
        ],
        out_specs=per_stream(rows, width),
        out_shape=jax.ShapeDtypeStruct((per_dev, rows, width), f32),
        scratch_shapes=[pltpu.VMEM((atoms, atoms), f32)],
        name="network",
    )(
        atom_types.reshape(per_dev, 1, atoms),
        neighbor_ids,
        switching,
        environment.swapaxes(1, 2),
        force_weights.reshape(per_dev, 1, atoms),
        targets.reshape(per_dev, 1, 1),
        type_embed,
        layer_weight,
        out_weight.reshape(1, width),
    )


def in_hbm(x):
    return pltpu.with_memory_space_constraint(x, pltpu.HBM)


def in_vmem(x):
    return pltpu.with_memory_space_constraint(x, pltpu.VMEM)


def stage_kernel(cov_ref, hi_ref, lo_ref, hi_head_ref, lo_head_ref, *, head_steps):
    hi, lo = split2(cov_ref[...])
    hi_ref[...] = hi
    lo_ref[...] = lo

    @pl.when(pl.program_id(0) < head_steps)
    def _():
        hi_head_ref[...] = hi
        lo_head_ref[...] = lo


def stage(covariance, head, tail):
    rows, cols = covariance.shape
    height = min(rows // 8, head)
    head_steps = head // height
    block = pl.BlockSpec((height, cols), lambda n: (n, 0))
    rest_block = pl.BlockSpec((height, cols), lambda n: (jnp.maximum(n - head_steps, 0), 0))
    head_block = pl.BlockSpec((height, cols), lambda n: (jnp.minimum(n, head_steps - 1), 0))
    return pl.pallas_call(
        functools.partial(stage_kernel, head_steps=head_steps),
        grid=((rows - tail) // height,),
        in_specs=[block],
        out_specs=[rest_block, rest_block, head_block, head_block],
        out_shape=[pltpu.HBM((rows - head - tail, cols), bf16)] * 2 + [pltpu.VMEM((head, cols), bf16)] * 2,
        compiler_params=limit(12),
        name="stage",
    )(in_hbm(covariance))


def stacked_parts(flat, first, count, streams, stride, into_ref):
    lanes = flat.shape[1]
    for i in range(count):
        parts = split3(flat[pl.ds(first + i, streams, stride=stride), :])
        for n, part in enumerate(parts):
            into_ref[n * streams : (n + 1) * streams, i * lanes : (i + 1) * lanes] = part


def col_kernel(
    jac_ref,
    hi_head_ref,
    lo_head_ref,
    hi_ref,
    lo_ref,
    cov_ref,
    out_ref,
    parts_ref,
    hi_rest_ref,
    lo_rest_ref,
    tail_ref,
    sums_ref,
    sems,
    tail_sem,
):
    head, tile_cols = hi_head_ref.shape
    slabs, streams, slab = out_ref.shape
    rows, lanes = jac_ref.shape[0] // streams, jac_ref.shape[1]
    chunks = sems.shape[0]
    copies = []
    for n in range(chunks):
        here = pl.ds(n * head, head)
        copies.append(
            (
                pltpu.make_async_copy(hi_ref.at[here], hi_rest_ref.at[here], sems.at[n, 0]),
                pltpu.make_async_copy(lo_ref.at[here], lo_rest_ref.at[here], sems.at[n, 1]),
            )
        )
        for copy in copies[-1]:
            copy.start()
    tail = tail_ref.shape[0]
    last = pltpu.make_async_copy(cov_ref.at[pl.ds(cov_ref.shape[0] - tail, tail)], tail_ref, tail_sem)
    last.start()
    stacked_parts(jac_ref, 0, parts_ref.shape[1] // lanes, streams, rows, parts_ref)
    sums_ref[...] = five_products(parts_ref[:, 0:head], hi_head_ref[...], lo_head_ref[...], ((1,), (0,)))
    for n in range(chunks):
        for copy in copies[n]:
            copy.wait()
        here = slice(n * head, (n + 1) * head)
        sums_ref[...] += five_products(
            parts_ref[:, (n + 1) * head : (n + 2) * head], hi_rest_ref[here, :], lo_rest_ref[here, :], ((1,), (0,))
        )
    last.wait()
    sums_ref[...] += five_products(
        parts_ref[:, parts_ref.shape[1] - tail :], *split2(tail_ref[...]), ((1,), (0,))
    )
    for n in range(slabs):
        out_ref[n] = sums_ref[:, n * slab : (n + 1) * slab]


def col_partial(jac, streams, hi_head, lo_head, hi, lo, covariance, slab):
    rest, tile_cols = hi.shape
    head = hi_head.shape[0]
    tail = covariance.shape[0] - head - rest
    whole = pl.BlockSpec(memory_space=pltpu.VMEM)
    beyond = pl.BlockSpec(memory_space=pl.ANY)
    return pl.pallas_call(
        col_kernel,
        in_specs=[whole] * 3 + [beyond] * 3,
        out_specs=whole,
        out_shape=jax.ShapeDtypeStruct((tile_cols // slab, streams, slab), f32),
        scratch_shapes=[
            pltpu.VMEM((3 * streams, covariance.shape[0]), bf16),
            pltpu.VMEM((rest, tile_cols), bf16),
            pltpu.VMEM((rest, tile_cols), bf16),
            pltpu.VMEM((tail, tile_cols), f32),
            pltpu.VMEM((streams, tile_cols), f32),
            pltpu.SemaphoreType.DMA((rest // head, 2)),
            pltpu.SemaphoreType.DMA,
        ],
        compiler_params=limit(16),
        name="col_cross",
    )(jac, in_vmem(hi_head), in_vmem(lo_head), in_hbm(hi), in_hbm(lo), in_hbm(covariance))


def packed(term):
    streams = term.shape[0]
    groups = LANES // streams
    height = streams // groups
    return jnp.concatenate([term[n * height : (n + 1) * height] for n in range(groups)], axis=1)


def unpacked(rows, streams):
    return jnp.concatenate(
        [rows[:, n * streams : (n + 1) * streams] for n in range(LANES // streams)], axis=0
    )


def slab_kernel(pieces_ref, jac_ref, own_ref, out_ref, error_ref, *, first):
    streams, slab = own_ref.shape
    rows, lanes = jac_ref.shape[0] // streams, jac_ref.shape[1]
    total = pieces_ref[0]
    for n in range(1, pieces_ref.shape[0]):
        total = total + pieces_ref[n]
    own_ref[...] = total
    term = jnp.zeros((streams, streams), f32)
    for i in range(slab // lanes):
        own = jac_ref[pl.ds(first + i, streams, stride=rows), :]
        here = total[:, i * lanes : (i + 1) * lanes]
        term = term + dot(own, here, ((1,), (1,)), highest)
        out_ref[i * streams : (i + 1) * streams, :] = here
    out_ref[slab // lanes * streams :, :] = packed(term)
    error_ref[...] = jac_ref[pl.ds(first + slab // lanes, streams, stride=rows), :]


def slab_sum(pieces, jac, first):
    _, streams, slab = pieces.shape
    return pl.pallas_call(
        functools.partial(slab_kernel, first=first),
        out_shape=[
            jax.ShapeDtypeStruct((streams, slab), f32),
            jax.ShapeDtypeStruct((streams * (slab + streams) // LANES, LANES), f32),
            jax.ShapeDtypeStruct((streams, LANES), f32),
        ],
        compiler_params=limit(8),
        name="slab",
    )(pieces, jac)


def term_kernel(own_ref, cols_ref, out_ref):
    streams, slab = own_ref.shape
    _, lanes = out_ref.shape[1:]
    under = slab // lanes * streams
    term = cols_ref[0, under:, :]
    for n in range(1, cols_ref.shape[0]):
        term = term + cols_ref[n, under:, :]
    for n in range(out_ref.shape[0]):
        for i in range(slab // lanes):
            out_ref[n, i * streams : (i + 1) * streams, :] = own_ref[:, i * lanes : (i + 1) * lanes]
        out_ref[n, under:, :] = term


def with_terms(own, col_slabs, copies):
    return pl.pallas_call(
        term_kernel,
        out_shape=jax.ShapeDtypeStruct((copies,) + col_slabs.shape[1:], f32),
        compiler_params=limit(8),
        name="term",
    )(own, col_slabs)


def invert(innovation):
    streams = innovation.shape[0]
    row = lax.broadcasted_iota(jnp.int32, (streams, streams), 0)
    col = lax.broadcasted_iota(jnp.int32, (streams, streams), 1)
    identity = (row == col).astype(f32)
    innovation = innovation + forget * identity
    sums = jnp.sum(jnp.abs(innovation), axis=1, keepdims=True)
    bound = jnp.max(sums, axis=0, keepdims=True)
    power = identity - innovation / bound
    inverse = identity + power
    for repeat in range(NEWTON - 1):
        power = dot(power, power, ((1,), (0,)), highest)
        inverse = inverse + dot(inverse, power, ((1,), (0,)), highest)
    return inverse / bound


def head_kernel(cov_ref, _, head_ref, sem):
    copy = pltpu.make_async_copy(cov_ref.at[pl.ds(0, head_ref.shape[0])], head_ref, sem)
    copy.start()
    copy.wait()


def read_head(covariance, after):
    beyond = pl.BlockSpec(memory_space=pl.ANY)
    rows, cols = covariance.shape
    return pl.pallas_call(
        head_kernel,
        in_specs=[beyond, beyond],
        out_specs=pl.BlockSpec(memory_space=pltpu.VMEM),
        out_shape=pltpu.VMEM((rows // 4, cols), f32),
        scratch_shapes=[pltpu.SemaphoreType.DMA],
        compiler_params=limit(2),
        name="head",
    )(in_hbm(covariance), after)


def update_kernel(
    rows_ref, cols_ref, error_ref, weight_ref, head_ref, cov_ref, new_weight_ref, new_cov_ref, left_ref, right_ref, tile_ref, in_sems, out_sems
):
    slabs, _, lanes = rows_ref.shape
    streams = error_ref.shape[0]
    tile_rows = cov_ref.shape[0]
    slab = tile_rows // slabs
    under = slab // lanes * streams
    chunks = in_sems.shape[0]
    height = tile_rows // chunks
    held = head_ref.shape[0] // height
    reads = []
    for n in range(held, chunks):
        here = pl.ds(n * height, height)
        reads.append(pltpu.make_async_copy(cov_ref.at[here], tile_ref.at[here], in_sems.at[n]))
        reads[-1].start()
    term = rows_ref[0, under:, :]
    for n in range(1, slabs):
        term = term + rows_ref[n, under:, :]
    inverse = invert(unpacked(term, streams))
    errors = error_ref[:, 0:1]
    for n in range(cols_ref.shape[0]):
        for i in range(slab // lanes):
            hi, mid, lo = split3(cols_ref[n, i * streams : (i + 1) * streams, :])
            at = n * slab + i * lanes
            for m, part in enumerate((hi, mid, lo, hi, mid, hi)):
                right_ref[m * streams : (m + 1) * streams, at : at + lanes] = part
    cross = jnp.concatenate(
        [rows_ref[n, i : i + streams, :] for n in range(slabs) for i in range(0, under, streams)], axis=1
    )
    gain = dot(inverse, cross, ((0,), (0,)), highest)
    hi, mid, lo = split3(gain)
    for m, part in enumerate((hi, hi, hi, mid, mid, lo)):
        left_ref[m * streams : (m + 1) * streams, :] = part
    writes = []
    for n in range(chunks):
        update = dot(left_ref[:, n * height : (n + 1) * height], right_ref[...], ((0,), (0,)))
        here = pl.ds(n * height, height)
        if n >= held:
            reads[n - held].wait()
        before = head_ref if n < held else tile_ref
        tile_ref[here, :] = (before[here, :] - update) * (1.0 / forget)
        writes.append(pltpu.make_async_copy(tile_ref.at[here], new_cov_ref.at[here], out_sems.at[n]))
        writes[-1].start()
    col_at = lax.axis_index("col")
    own_at = (lax.axis_index("row") * slabs + col_at) * (slab // lanes)
    for n in range(slabs):

        @pl.when(col_at == n)
        def _():
            moved = jnp.sum(gain[:, n * slab : (n + 1) * slab] * errors, axis=0, keepdims=True)
            for i in range(slab // lanes):
                own = weight_ref[pl.ds(own_at + i, 1), :]
                new_weight_ref[i : i + 1, :] = own + moved[:, i * lanes : (i + 1) * lanes]

    for write in writes:
        write.wait()


def update(row_slabs, col_slabs, errors, layer_weight, head, covariance):
    streams = errors.shape[0]
    tile_rows, tile_cols = covariance.shape
    slab = tile_rows // row_slabs.shape[0]
    width = layer_weight.shape[1]
    whole = pl.BlockSpec(memory_space=pltpu.VMEM)
    beyond = pl.BlockSpec(memory_space=pl.ANY)
    return pl.pallas_call(
        update_kernel,
        in_specs=[whole] * 5 + [beyond],
        out_specs=[whole, beyond],
        out_shape=[
            jax.ShapeDtypeStruct((slab // width, width), f32),
            jax.ShapeDtypeStruct((tile_rows, tile_cols), f32),
        ],
        scratch_shapes=[
            pltpu.VMEM((6 * streams, tile_rows), bf16),
            pltpu.VMEM((6 * streams, tile_cols), bf16),
            pltpu.VMEM((tile_rows, tile_cols), f32),
            pltpu.SemaphoreType.DMA((8,)),
            pltpu.SemaphoreType.DMA((8,)),
        ],
        compiler_params=limit(20),
        name="update",
    )(row_slabs, col_slabs, errors, layer_weight, in_vmem(head), in_hbm(covariance))


def plain_steps(at, jac_all, errors, layer_weight, covariance, slab, cols_n):
    streams = jac_all.shape[0]
    hin, width = layer_weight.shape
    tile_rows, tile_cols = covariance.shape
    first = (at[0] * cols_n + at[1]) * slab
    jacobian = jac_all[:, 0:hin, :].reshape(streams, hin * width)
    jac_cols = lax.dynamic_slice_in_dim(jacobian, at[1] * tile_cols, tile_cols, 1)
    partial = dot(jac_cols, covariance, ((1,), (1,)), highest)
    cross_own = lax.psum_scatter(partial, "col", scatter_dimension=1, tiled=True)
    cross = lax.all_gather(cross_own, ("row", "col"), axis=1, tiled=True)
    inverse = invert(dot(jacobian, cross, ((1,), (1,)), highest))
    gain = dot(inverse, lax.dynamic_slice_in_dim(cross, at[0] * tile_rows, tile_rows, 1), ((0,), (0,)), highest)
    across = lax.dynamic_slice_in_dim(cross, at[1] * tile_cols, tile_cols, 1)
    new_cov = (covariance - dot(gain, across, ((0,), (0,)), highest)) / forget
    own_gain = lax.dynamic_slice_in_dim(gain, at[1] * slab, slab, 1)
    own_weight = lax.dynamic_slice_in_dim(layer_weight.reshape(-1), first, slab, 0)
    new_weight = own_weight + dot(errors, own_gain, ((0,), (0,)), highest)
    return new_weight, new_cov


def exchange(x, axes):
    return lax.all_to_all(x, axes, split_axis=0, concat_axis=0, tiled=True)


def on_device(
    atom_types,
    neighbor_ids,
    switching,
    environment,
    force_weights,
    targets,
    type_embed,
    layer_weight,
    out_weight,
    covariance,
):
    rows_n = lax.axis_size("row")
    cols_n = lax.axis_size("col")
    at = jnp.stack([lax.axis_index("row"), lax.axis_index("col")]).astype(jnp.int32)
    tile_rows, tile_cols = covariance.shape
    slab = tile_rows // cols_n
    hin, width = layer_weight.shape
    run_network = functools.partial(
        network,
        atom_types=atom_types,
        neighbor_ids=neighbor_ids,
        switching=switching,
        environment=environment,
        force_weights=force_weights,
        targets=targets,
        type_embed=type_embed,
        layer_weight=layer_weight,
        out_weight=out_weight,
    )
    streams = rows_n * cols_n * atom_types.shape[0]
    kernels = (
        atom_types.shape[0] == 1
        and width == LANES
        and slab % LANES == 0
        and tile_rows % (SUBLANES * LANES) == 0
        and tile_cols % (SUBLANES * LANES) == 0
        and rows_n * slab == tile_cols
        and LANES % streams == 0
        and streams * streams % (SUBLANES * LANES) == 0
    )
    if not kernels:
        payload = run_network([[(0, hin)]])
        jac_all = lax.all_gather(payload, ("row", "col"), axis=0, tiled=True)
        return plain_steps(at, jac_all[:, 0:hin], jac_all[:, hin, 0], layer_weight, covariance, slab, cols_n)
    row_size, slab_size = tile_rows // LANES, slab // LANES
    devices = [(r, c) for r in range(rows_n) for c in range(cols_n)]
    plan = [[(r * row_size, row_size), ((c * rows_n + r) * slab_size, slab_size)] for r, c in devices]
    payload = run_network(plan).reshape(streams, 1, -1)
    jac = exchange(payload, ("row", "col")).reshape(-1, width)
    hi, lo, hi_head, lo_head = stage(covariance, tile_rows // 4, tile_rows // 4)
    col_part = col_partial(jac, streams, hi_head, lo_head, hi, lo, covariance, slab)
    pieces = exchange(col_part, "row")
    head = read_head(covariance, col_part)
    col_own, with_term, errors = slab_sum(pieces, jac, row_size)
    to_row = [(r * cols_n + c, c * rows_n + r) for r, c in devices]
    row_own = lax.ppermute(col_own, ("row", "col"), to_row)
    col_slabs = lax.all_gather(with_term, "row", axis=0, tiled=False)
    row_slabs = exchange(with_terms(row_own, col_slabs, cols_n), "col")
    new_weight, new_cov = update(row_slabs, col_slabs, errors, layer_weight, head, covariance)
    return new_weight.reshape(-1), new_cov


def solution(mesh):
    in_specs = (
        P(("row", "col"), None),
        P(("row", "col"), None, None),
        P(("row", "col"), None, None),
        P(("row", "col"), None, None),
        P(("row", "col"), None),
        P(("row", "col")),
        P(),
        P(),
        P(),
        P("row", "col"),
    )
    out_specs = (P(("row", "col")), P("row", "col"))
    return jax.shard_map(
        on_device, mesh=mesh, in_specs=in_specs, out_specs=out_specs, check_vma=False
    )
```

```python
import functools
import math

import jax
import jax.numpy as jnp
from jax import lax
from jax.experimental import pallas as pl
from jax.experimental.pallas import tpu as pltpu
from jax.sharding import PartitionSpec as P

NEWTON = 4
LANES = 128
SUBLANES = 8


forget = 0.98
highest = lax.Precision.HIGHEST
f32 = jnp.float32
bf16 = jnp.bfloat16


def dot(left, right, contract, precision=None):
    return lax.dot_general(
        left, right, (contract, ((), ())), precision=precision, preferred_element_type=f32
    )


def split3(x):
    hi = x.astype(bf16)
    rest = x - hi.astype(f32)
    mid = rest.astype(bf16)
    lo = (rest - mid.astype(f32)).astype(bf16)
    return hi, mid, lo


def split2(x):
    hi = x.astype(bf16)
    return hi, (x - hi.astype(f32)).astype(bf16)


def limit(mib):
    return pltpu.CompilerParams(vmem_limit_bytes=mib << 20)


def five_products(parts, hi, lo, contract):
    streams = parts.shape[0] // 3
    by_hi = dot(parts, hi, contract)
    by_lo = dot(parts[0 : 2 * streams], lo, contract)
    return by_hi[0:streams] + (
        by_hi[streams : 2 * streams] + by_lo[0:streams] + (by_hi[2 * streams :] + by_lo[streams:])
    )


def network_kernel(
    types_ref,
    ids_ref,
    switch_ref,
    env_ref,
    force_ref,
    target_ref,
    embed_ref,
    weight_ref,
    out_weight_ref,
    payload_ref,
    mix_ref,
    *,
    plan,
):
    neighbours, atoms = ids_ref.shape
    n_types = embed_ref.shape[0]
    height = min(64, atoms)
    for start in range(0, atoms, height):
        atom_at = lax.broadcasted_iota(jnp.int32, (height, atoms), 0) + start
        total = jnp.zeros((height, atoms), f32)
        for k in range(neighbours):
            total = total + jnp.where(ids_ref[k : k + 1, :] == atom_at, switch_ref[k : k + 1, :], 0.0)
        mix_ref[start : start + height, :] = total
    mix = mix_ref[...]
    type_at = lax.broadcasted_iota(jnp.int32, (n_types, atoms), 0)
    onehot = (types_ref[...] == type_at).astype(f32)
    mixed = env_ref[...] + dot(embed_ref[...], onehot, ((0,), (0,)), highest)
    parts = jnp.concatenate(split3(mixed), axis=0)
    descriptor = five_products(parts, *split2(mix), ((1,), (0,))) * (1.0 / math.sqrt(neighbours))
    hidden = jnp.tanh(descriptor)
    activity = jnp.tanh(dot(hidden, weight_ref[...], ((0,), (0,)), highest))
    out_weight = out_weight_ref[...]
    scale = 1.0 / math.sqrt(atoms)
    force = force_ref[...]
    weighted = dot(force, activity, ((1,), (0,)), highest)
    predicted = jnp.sum(weighted * out_weight, axis=1, keepdims=True) * scale
    slopes = out_weight * (1.0 - activity * activity)
    parts = jnp.concatenate(split3(hidden * force), axis=0)
    jacobian = five_products(parts, *split2(slopes), ((1,), (0,))) * scale
    error = target_ref[...] - predicted
    at = 0
    for pieces in plan:
        for start, size in pieces:
            payload_ref[at : at + size, :] = jacobian[start : start + size, :]
            at += size
        payload_ref[at : at + 1, :] = jnp.broadcast_to(error, (1, jacobian.shape[1]))
        at += 1


def network(
    plan, atom_types, neighbor_ids, switching, environment, force_weights, targets, type_embed, layer_weight, out_weight
):
    per_dev, neighbours, atoms = neighbor_ids.shape
    hin, width = layer_weight.shape
    rows = sum(1 + sum(size for _, size in pieces) for pieces in plan)

    def per_stream(*shape):
        return pl.BlockSpec((None,) + shape, lambda s: (s,) + (0,) * len(shape))

    def shared(shape):
        return pl.BlockSpec(shape, lambda s: (0,) * len(shape))

    return pl.pallas_call(
        functools.partial(network_kernel, plan=plan),
        grid=(per_dev,),
        in_specs=[
            per_stream(1, atoms),
            per_stream(neighbours, atoms),
            per_stream(neighbours, atoms),
            per_stream(hin, atoms),
            per_stream(1, atoms),
            per_stream(1, 1),
            shared(type_embed.shape),
            shared(layer_weight.shape),
            shared((1, width)),
        ],
        out_specs=per_stream(rows, width),
        out_shape=jax.ShapeDtypeStruct((per_dev, rows, width), f32),
        scratch_shapes=[pltpu.VMEM((atoms, atoms), f32)],
        name="network",
    )(
        atom_types.reshape(per_dev, 1, atoms),
        neighbor_ids,
        switching,
        environment.swapaxes(1, 2),
        force_weights.reshape(per_dev, 1, atoms),
        targets.reshape(per_dev, 1, 1),
        type_embed,
        layer_weight,
        out_weight.reshape(1, width),
    )


def in_hbm(x):
    return pltpu.with_memory_space_constraint(x, pltpu.HBM)


def in_vmem(x):
    return pltpu.with_memory_space_constraint(x, pltpu.VMEM)


def stage_kernel(cov_ref, hi_ref, lo_ref, hi_head_ref, lo_head_ref, *, head_steps):
    hi, lo = split2(cov_ref[...])
    hi_ref[...] = hi
    lo_ref[...] = lo

    @pl.when(pl.program_id(0) < head_steps)
    def _():
        hi_head_ref[...] = hi
        lo_head_ref[...] = lo


def stage(covariance, head, tail):
    rows, cols = covariance.shape
    height = min(rows // 8, head)
    head_steps = head // height
    block = pl.BlockSpec((height, cols), lambda n: (n, 0))
    rest_block = pl.BlockSpec((height, cols), lambda n: (jnp.maximum(n - head_steps, 0), 0))
    head_block = pl.BlockSpec((height, cols), lambda n: (jnp.minimum(n, head_steps - 1), 0))
    return pl.pallas_call(
        functools.partial(stage_kernel, head_steps=head_steps),
        grid=((rows - tail) // height,),
        in_specs=[block],
        out_specs=[rest_block, rest_block, head_block, head_block],
        out_shape=[pltpu.HBM((rows - head - tail, cols), bf16)] * 2 + [pltpu.VMEM((head, cols), bf16)] * 2,
        compiler_params=limit(12),
        name="stage",
    )(in_hbm(covariance))


def stacked_parts(flat, first, count, streams, stride, into_ref):
    lanes = flat.shape[1]
    for i in range(count):
        parts = split3(flat[pl.ds(first + i, streams, stride=stride), :])
        for n, part in enumerate(parts):
            into_ref[n * streams : (n + 1) * streams, i * lanes : (i + 1) * lanes] = part


def col_kernel(
    jac_ref,
    hi_head_ref,
    lo_head_ref,
    hi_ref,
    lo_ref,
    cov_ref,
    out_ref,
    parts_ref,
    hi_rest_ref,
    lo_rest_ref,
    tail_ref,
    sums_ref,
    sems,
    tail_sems,
):
    head, tile_cols = hi_head_ref.shape
    slabs, streams, slab = out_ref.shape
    rows, lanes = jac_ref.shape[0] // streams, jac_ref.shape[1]
    chunks = sems.shape[0]
    copies = []
    for n in range(chunks):
        here = pl.ds(n * head, head)
        copies.append(
            (
                pltpu.make_async_copy(hi_ref.at[here], hi_rest_ref.at[here], sems.at[n, 0]),
                pltpu.make_async_copy(lo_ref.at[here], lo_rest_ref.at[here], sems.at[n, 1]),
            )
        )
        for copy in copies[-1]:
            copy.start()
    tail = tail_ref.shape[0]
    first = cov_ref.shape[0] - tail
    last = []
    for n in range(tail // head):
        source, target = pl.ds(first + n * head, head), pl.ds(n * head, head)
        last.append(pltpu.make_async_copy(cov_ref.at[source], tail_ref.at[target], tail_sems.at[n]))
        last[-1].start()
    stacked_parts(jac_ref, 0, parts_ref.shape[1] // lanes, streams, rows, parts_ref)
    sums_ref[...] = five_products(parts_ref[:, 0:head], hi_head_ref[...], lo_head_ref[...], ((1,), (0,)))
    for n in range(chunks):
        for copy in copies[n]:
            copy.wait()
        here = slice(n * head, (n + 1) * head)
        sums_ref[...] += five_products(
            parts_ref[:, (n + 1) * head : (n + 2) * head], hi_rest_ref[here, :], lo_rest_ref[here, :], ((1,), (0,))
        )
    for n in range(tail // head):
        last[n].wait()
        hi, lo = split2(tail_ref[n * head : (n + 1) * head, :])
        parts = parts_ref[:, first + n * head : first + (n + 1) * head]
        sums_ref[...] += five_products(parts, hi, lo, ((1,), (0,)))
    for n in range(slabs):
        out_ref[n] = sums_ref[:, n * slab : (n + 1) * slab]


def col_partial(jac, streams, hi_head, lo_head, hi, lo, covariance, slab):
    rest, tile_cols = hi.shape
    head = hi_head.shape[0]
    tail = covariance.shape[0] - head - rest
    whole = pl.BlockSpec(memory_space=pltpu.VMEM)
    beyond = pl.BlockSpec(memory_space=pl.ANY)
    return pl.pallas_call(
        col_kernel,
        in_specs=[whole] * 3 + [beyond] * 3,
        out_specs=whole,
        out_shape=jax.ShapeDtypeStruct((tile_cols // slab, streams, slab), f32),
        scratch_shapes=[
            pltpu.VMEM((3 * streams, covariance.shape[0]), bf16),
            pltpu.VMEM((rest, tile_cols), bf16),
            pltpu.VMEM((rest, tile_cols), bf16),
            pltpu.VMEM((tail, tile_cols), f32),
            pltpu.VMEM((streams, tile_cols), f32),
            pltpu.SemaphoreType.DMA((rest // head, 2)),
            pltpu.SemaphoreType.DMA((tail // head,)),
        ],
        compiler_params=limit(20),
        name="col_cross",
    )(jac, in_vmem(hi_head), in_vmem(lo_head), in_hbm(hi), in_hbm(lo), in_hbm(covariance))


def packed(term):
    streams = term.shape[0]
    groups = LANES // streams
    height = streams // groups
    return jnp.concatenate([term[n * height : (n + 1) * height] for n in range(groups)], axis=1)


def unpacked(rows, streams):
    return jnp.concatenate(
        [rows[:, n * streams : (n + 1) * streams] for n in range(LANES // streams)], axis=0
    )


def slab_kernel(pieces_ref, jac_ref, own_ref, out_ref, error_ref, *, first):
    streams, slab = own_ref.shape
    rows, lanes = jac_ref.shape[0] // streams, jac_ref.shape[1]
    total = pieces_ref[0]
    for n in range(1, pieces_ref.shape[0]):
        total = total + pieces_ref[n]
    own_ref[...] = total
    term = jnp.zeros((streams, streams), f32)
    for i in range(slab // lanes):
        own = jac_ref[pl.ds(first + i, streams, stride=rows), :]
        here = total[:, i * lanes : (i + 1) * lanes]
        term = term + dot(own, here, ((1,), (1,)), highest)
        out_ref[i * streams : (i + 1) * streams, :] = here
    out_ref[slab // lanes * streams :, :] = packed(term)
    error_ref[...] = jac_ref[pl.ds(first + slab // lanes, streams, stride=rows), :]


def slab_sum(pieces, jac, first):
    _, streams, slab = pieces.shape
    return pl.pallas_call(
        functools.partial(slab_kernel, first=first),
        out_shape=[
            jax.ShapeDtypeStruct((streams, slab), f32),
            jax.ShapeDtypeStruct((streams * (slab + streams) // LANES, LANES), f32),
            jax.ShapeDtypeStruct((streams, LANES), f32),
        ],
        compiler_params=limit(8),
        name="slab",
    )(pieces, jac)


def term_kernel(own_ref, cols_ref, out_ref):
    streams, slab = own_ref.shape
    _, lanes = out_ref.shape[1:]
    under = slab // lanes * streams
    term = cols_ref[0, under:, :]
    for n in range(1, cols_ref.shape[0]):
        term = term + cols_ref[n, under:, :]
    for n in range(out_ref.shape[0]):
        for i in range(slab // lanes):
            out_ref[n, i * streams : (i + 1) * streams, :] = own_ref[:, i * lanes : (i + 1) * lanes]
        out_ref[n, under:, :] = term


def with_terms(own, col_slabs, copies):
    return pl.pallas_call(
        term_kernel,
        out_shape=jax.ShapeDtypeStruct((copies,) + col_slabs.shape[1:], f32),
        compiler_params=limit(8),
        name="term",
    )(own, col_slabs)


def invert(innovation):
    streams = innovation.shape[0]
    row = lax.broadcasted_iota(jnp.int32, (streams, streams), 0)
    col = lax.broadcasted_iota(jnp.int32, (streams, streams), 1)
    identity = (row == col).astype(f32)
    innovation = innovation + forget * identity
    sums = jnp.sum(jnp.abs(innovation), axis=1, keepdims=True)
    bound = jnp.max(sums, axis=0, keepdims=True)
    power = identity - innovation / bound
    inverse = identity + power
    for repeat in range(NEWTON - 1):
        power = dot(power, power, ((1,), (0,)), highest)
        inverse = inverse + dot(inverse, power, ((1,), (0,)), highest)
    return inverse / bound


def head_kernel(cov_ref, _, head_ref, sem):
    copy = pltpu.make_async_copy(cov_ref.at[pl.ds(0, head_ref.shape[0])], head_ref, sem)
    copy.start()
    copy.wait()


def read_head(covariance, after):
    beyond = pl.BlockSpec(memory_space=pl.ANY)
    rows, cols = covariance.shape
    return pl.pallas_call(
        head_kernel,
        in_specs=[beyond, beyond],
        out_specs=pl.BlockSpec(memory_space=pltpu.VMEM),
        out_shape=pltpu.VMEM((rows // 4, cols), f32),
        scratch_shapes=[pltpu.SemaphoreType.DMA],
        compiler_params=limit(2),
        name="head",
    )(in_hbm(covariance), after)


def update_kernel(
    rows_ref, cols_ref, error_ref, weight_ref, head_ref, cov_ref, new_weight_ref, new_cov_ref, left_ref, right_ref, tile_ref, in_sems, out_sems
):
    slabs, _, lanes = rows_ref.shape
    streams = error_ref.shape[0]
    tile_rows = cov_ref.shape[0]
    slab = tile_rows // slabs
    under = slab // lanes * streams
    chunks = in_sems.shape[0]
    height = tile_rows // chunks
    held = head_ref.shape[0] // height
    reads = []
    for n in range(held, chunks):
        here = pl.ds(n * height, height)
        reads.append(pltpu.make_async_copy(cov_ref.at[here], tile_ref.at[here], in_sems.at[n]))
        reads[-1].start()
    term = rows_ref[0, under:, :]
    for n in range(1, slabs):
        term = term + rows_ref[n, under:, :]
    inverse = invert(unpacked(term, streams))
    errors = error_ref[:, 0:1]
    for n in range(cols_ref.shape[0]):
        for i in range(slab // lanes):
            hi, mid, lo = split3(cols_ref[n, i * streams : (i + 1) * streams, :])
            at = n * slab + i * lanes
            for m, part in enumerate((hi, mid, lo, hi, mid, hi)):
                right_ref[m * streams : (m + 1) * streams, at : at + lanes] = part
    cross = jnp.concatenate(
        [rows_ref[n, i : i + streams, :] for n in range(slabs) for i in range(0, under, streams)], axis=1
    )
    gain = dot(inverse, cross, ((0,), (0,)), highest)
    hi, mid, lo = split3(gain)
    for m, part in enumerate((hi, hi, hi, mid, mid, lo)):
        left_ref[m * streams : (m + 1) * streams, :] = part
    writes = []
    for n in range(chunks):
        update = dot(left_ref[:, n * height : (n + 1) * height], right_ref[...], ((0,), (0,)))
        here = pl.ds(n * height, height)
        if n >= held:
            reads[n - held].wait()
        before = head_ref if n < held else tile_ref
        tile_ref[here, :] = (before[here, :] - update) * (1.0 / forget)
        writes.append(pltpu.make_async_copy(tile_ref.at[here], new_cov_ref.at[here], out_sems.at[n]))
        writes[-1].start()
    col_at = lax.axis_index("col")
    own_at = (lax.axis_index("row") * slabs + col_at) * (slab // lanes)
    for n in range(slabs):

        @pl.when(col_at == n)
        def _():
            moved = jnp.sum(gain[:, n * slab : (n + 1) * slab] * errors, axis=0, keepdims=True)
            for i in range(slab // lanes):
                own = weight_ref[pl.ds(own_at + i, 1), :]
                new_weight_ref[i : i + 1, :] = own + moved[:, i * lanes : (i + 1) * lanes]

    for write in writes:
        write.wait()


def update(row_slabs, col_slabs, errors, layer_weight, head, covariance):
    streams = errors.shape[0]
    tile_rows, tile_cols = covariance.shape
    slab = tile_rows // row_slabs.shape[0]
    width = layer_weight.shape[1]
    whole = pl.BlockSpec(memory_space=pltpu.VMEM)
    beyond = pl.BlockSpec(memory_space=pl.ANY)
    return pl.pallas_call(
        update_kernel,
        in_specs=[whole] * 5 + [beyond],
        out_specs=[whole, beyond],
        out_shape=[
            jax.ShapeDtypeStruct((slab // width, width), f32),
            jax.ShapeDtypeStruct((tile_rows, tile_cols), f32),
        ],
        scratch_shapes=[
            pltpu.VMEM((6 * streams, tile_rows), bf16),
            pltpu.VMEM((6 * streams, tile_cols), bf16),
            pltpu.VMEM((tile_rows, tile_cols), f32),
            pltpu.SemaphoreType.DMA((8,)),
            pltpu.SemaphoreType.DMA((8,)),
        ],
        compiler_params=limit(20),
        name="update",
    )(row_slabs, col_slabs, errors, layer_weight, in_vmem(head), in_hbm(covariance))


def plain_steps(at, jac_all, errors, layer_weight, covariance, slab, cols_n):
    streams = jac_all.shape[0]
    hin, width = layer_weight.shape
    tile_rows, tile_cols = covariance.shape
    first = (at[0] * cols_n + at[1]) * slab
    jacobian = jac_all[:, 0:hin, :].reshape(streams, hin * width)
    jac_cols = lax.dynamic_slice_in_dim(jacobian, at[1] * tile_cols, tile_cols, 1)
    partial = dot(jac_cols, covariance, ((1,), (1,)), highest)
    cross_own = lax.psum_scatter(partial, "col", scatter_dimension=1, tiled=True)
    cross = lax.all_gather(cross_own, ("row", "col"), axis=1, tiled=True)
    inverse = invert(dot(jacobian, cross, ((1,), (1,)), highest))
    gain = dot(inverse, lax.dynamic_slice_in_dim(cross, at[0] * tile_rows, tile_rows, 1), ((0,), (0,)), highest)
    across = lax.dynamic_slice_in_dim(cross, at[1] * tile_cols, tile_cols, 1)
    new_cov = (covariance - dot(gain, across, ((0,), (0,)), highest)) / forget
    own_gain = lax.dynamic_slice_in_dim(gain, at[1] * slab, slab, 1)
    own_weight = lax.dynamic_slice_in_dim(layer_weight.reshape(-1), first, slab, 0)
    new_weight = own_weight + dot(errors, own_gain, ((0,), (0,)), highest)
    return new_weight, new_cov


def exchange(x, axes):
    return lax.all_to_all(x, axes, split_axis=0, concat_axis=0, tiled=True)


def on_device(
    atom_types,
    neighbor_ids,
    switching,
    environment,
    force_weights,
    targets,
    type_embed,
    layer_weight,
    out_weight,
    covariance,
):
    rows_n = lax.axis_size("row")
    cols_n = lax.axis_size("col")
    at = jnp.stack([lax.axis_index("row"), lax.axis_index("col")]).astype(jnp.int32)
    tile_rows, tile_cols = covariance.shape
    slab = tile_rows // cols_n
    hin, width = layer_weight.shape
    run_network = functools.partial(
        network,
        atom_types=atom_types,
        neighbor_ids=neighbor_ids,
        switching=switching,
        environment=environment,
        force_weights=force_weights,
        targets=targets,
        type_embed=type_embed,
        layer_weight=layer_weight,
        out_weight=out_weight,
    )
    streams = rows_n * cols_n * atom_types.shape[0]
    kernels = (
        atom_types.shape[0] == 1
        and width == LANES
        and slab % LANES == 0
        and tile_rows % (SUBLANES * LANES) == 0
        and tile_cols % (SUBLANES * LANES) == 0
        and rows_n * slab == tile_cols
        and LANES % streams == 0
        and streams * streams % (SUBLANES * LANES) == 0
    )
    if not kernels:
        payload = run_network([[(0, hin)]])
        jac_all = lax.all_gather(payload, ("row", "col"), axis=0, tiled=True)
        return plain_steps(at, jac_all[:, 0:hin], jac_all[:, hin, 0], layer_weight, covariance, slab, cols_n)
    row_size, slab_size = tile_rows // LANES, slab // LANES
    devices = [(r, c) for r in range(rows_n) for c in range(cols_n)]
    plan = [[(r * row_size, row_size), ((c * rows_n + r) * slab_size, slab_size)] for r, c in devices]
    payload = run_network(plan).reshape(streams, 1, -1)
    jac = exchange(payload, ("row", "col")).reshape(-1, width)
    hi, lo, hi_head, lo_head = stage(covariance, tile_rows // 4, tile_rows // 2)
    col_part = col_partial(jac, streams, hi_head, lo_head, hi, lo, covariance, slab)
    pieces = exchange(col_part, "row")
    head = read_head(covariance, col_part)
    col_own, with_term, errors = slab_sum(pieces, jac, row_size)
    to_row = [(r * cols_n + c, c * rows_n + r) for r, c in devices]
    row_own = lax.ppermute(col_own, ("row", "col"), to_row)
    col_slabs = lax.all_gather(with_term, "row", axis=0, tiled=False)
    row_slabs = exchange(with_terms(row_own, col_slabs, cols_n), "col")
    new_weight, new_cov = update(row_slabs, col_slabs, errors, layer_weight, head, covariance)
    return new_weight.reshape(-1), new_cov


def solution(mesh):
    in_specs = (
        P(("row", "col"), None),
        P(("row", "col"), None, None),
        P(("row", "col"), None, None),
        P(("row", "col"), None, None),
        P(("row", "col"), None),
        P(("row", "col")),
        P(),
        P(),
        P(),
        P("row", "col"),
    )
    out_specs = (P(("row", "col")), P("row", "col"))
    return jax.shard_map(
        on_device, mesh=mesh, in_specs=in_specs, out_specs=out_specs, check_vma=False
    )
```

```python
import functools
import math

import jax
import jax.numpy as jnp
from jax import lax
from jax.experimental import pallas as pl
from jax.experimental.pallas import tpu as pltpu
from jax.sharding import PartitionSpec as P

NEWTON = 4
LANES = 128
SUBLANES = 8


forget = 0.98
highest = lax.Precision.HIGHEST
f32 = jnp.float32
bf16 = jnp.bfloat16


def dot(left, right, contract, precision=None):
    return lax.dot_general(
        left, right, (contract, ((), ())), precision=precision, preferred_element_type=f32
    )


def split3(x):
    hi = x.astype(bf16)
    rest = x - hi.astype(f32)
    mid = rest.astype(bf16)
    lo = (rest - mid.astype(f32)).astype(bf16)
    return hi, mid, lo


def split2(x):
    hi = x.astype(bf16)
    return hi, (x - hi.astype(f32)).astype(bf16)


def limit(mib):
    return pltpu.CompilerParams(vmem_limit_bytes=mib << 20)


def five_products(parts, hi, lo, contract):
    streams = parts.shape[0] // 3
    by_hi = dot(parts, hi, contract)
    by_lo = dot(parts[0 : 2 * streams], lo, contract)
    return by_hi[0:streams] + (
        by_hi[streams : 2 * streams] + by_lo[0:streams] + (by_hi[2 * streams :] + by_lo[streams:])
    )


def network_kernel(
    types_ref,
    ids_ref,
    switch_ref,
    env_ref,
    force_ref,
    target_ref,
    embed_ref,
    weight_ref,
    out_weight_ref,
    payload_ref,
    mix_ref,
    *,
    plan,
):
    neighbours, atoms = ids_ref.shape
    n_types = embed_ref.shape[0]
    height = min(64, atoms)
    for start in range(0, atoms, height):
        atom_at = lax.broadcasted_iota(jnp.int32, (height, atoms), 0) + start
        total = jnp.zeros((height, atoms), f32)
        for k in range(neighbours):
            total = total + jnp.where(ids_ref[k : k + 1, :] == atom_at, switch_ref[k : k + 1, :], 0.0)
        mix_ref[start : start + height, :] = total
    mix = mix_ref[...]
    type_at = lax.broadcasted_iota(jnp.int32, (n_types, atoms), 0)
    onehot = (types_ref[...] == type_at).astype(f32)
    mixed = env_ref[...] + dot(embed_ref[...], onehot, ((0,), (0,)), highest)
    parts = jnp.concatenate(split3(mixed), axis=0)
    descriptor = five_products(parts, *split2(mix), ((1,), (0,))) * (1.0 / math.sqrt(neighbours))
    hidden = jnp.tanh(descriptor)
    hidden_hi, hidden_lo = split2(hidden)
    weight_hi, weight_lo = split2(weight_ref[...])
    left = jnp.concatenate([hidden_hi, hidden_hi, hidden_lo, hidden_lo], axis=0)
    right = jnp.concatenate([weight_hi, weight_lo, weight_hi, weight_lo], axis=0)
    activity = jnp.tanh(dot(left, right, ((0,), (0,))))
    out_weight = out_weight_ref[...]
    scale = 1.0 / math.sqrt(atoms)
    force = force_ref[...]
    weighted = dot(force, activity, ((1,), (0,)), highest)
    predicted = jnp.sum(weighted * out_weight, axis=1, keepdims=True) * scale
    slopes = out_weight * (1.0 - activity * activity)
    parts = jnp.concatenate(split3(hidden * force), axis=0)
    jacobian = five_products(parts, *split2(slopes), ((1,), (0,))) * scale
    error = target_ref[...] - predicted
    at = 0
    for pieces in plan:
        for start, size in pieces:
            payload_ref[at : at + size, :] = jacobian[start : start + size, :]
            at += size
        payload_ref[at : at + 1, :] = jnp.broadcast_to(error, (1, jacobian.shape[1]))
        at += 1


def network(
    plan, atom_types, neighbor_ids, switching, environment, force_weights, targets, type_embed, layer_weight, out_weight
):
    per_dev, neighbours, atoms = neighbor_ids.shape
    hin, width = layer_weight.shape
    rows = sum(1 + sum(size for _, size in pieces) for pieces in plan)

    def per_stream(*shape):
        return pl.BlockSpec((None,) + shape, lambda s: (s,) + (0,) * len(shape))

    def shared(shape):
        return pl.BlockSpec(shape, lambda s: (0,) * len(shape))

    return pl.pallas_call(
        functools.partial(network_kernel, plan=plan),
        grid=(per_dev,),
        in_specs=[
            per_stream(1, atoms),
            per_stream(neighbours, atoms),
            per_stream(neighbours, atoms),
            per_stream(hin, atoms),
            per_stream(1, atoms),
            per_stream(1, 1),
            shared(type_embed.shape),
            shared(layer_weight.shape),
            shared((1, width)),
        ],
        out_specs=per_stream(rows, width),
        out_shape=jax.ShapeDtypeStruct((per_dev, rows, width), f32),
        scratch_shapes=[pltpu.VMEM((atoms, atoms), f32)],
        name="network",
    )(
        atom_types.reshape(per_dev, 1, atoms),
        neighbor_ids,
        switching,
        environment.swapaxes(1, 2),
        force_weights.reshape(per_dev, 1, atoms),
        targets.reshape(per_dev, 1, 1),
        type_embed,
        layer_weight,
        out_weight.reshape(1, width),
    )


def in_hbm(x):
    return pltpu.with_memory_space_constraint(x, pltpu.HBM)


def in_vmem(x):
    return pltpu.with_memory_space_constraint(x, pltpu.VMEM)


def stage_kernel(cov_ref, hi_ref, lo_ref, hi_head_ref, lo_head_ref, *, head_steps):
    hi, lo = split2(cov_ref[...])
    hi_ref[...] = hi
    lo_ref[...] = lo

    @pl.when(pl.program_id(0) < head_steps)
    def _():
        hi_head_ref[...] = hi
        lo_head_ref[...] = lo


def stage(covariance, head, tail):
    rows, cols = covariance.shape
    height = min(rows // 8, head)
    head_steps = head // height
    block = pl.BlockSpec((height, cols), lambda n: (n, 0))
    rest_block = pl.BlockSpec((height, cols), lambda n: (jnp.maximum(n - head_steps, 0), 0))
    head_block = pl.BlockSpec((height, cols), lambda n: (jnp.minimum(n, head_steps - 1), 0))
    return pl.pallas_call(
        functools.partial(stage_kernel, head_steps=head_steps),
        grid=((rows - tail) // height,),
        in_specs=[block],
        out_specs=[rest_block, rest_block, head_block, head_block],
        out_shape=[pltpu.HBM((rows - head - tail, cols), bf16)] * 2 + [pltpu.VMEM((head, cols), bf16)] * 2,
        compiler_params=limit(12),
        name="stage",
    )(in_hbm(covariance))


def stacked_parts(flat, first, count, streams, stride, into_ref):
    lanes = flat.shape[1]
    for i in range(count):
        parts = split3(flat[pl.ds(first + i, streams, stride=stride), :])
        for n, part in enumerate(parts):
            into_ref[n * streams : (n + 1) * streams, i * lanes : (i + 1) * lanes] = part


def col_kernel(
    jac_ref,
    hi_head_ref,
    lo_head_ref,
    hi_ref,
    lo_ref,
    cov_ref,
    out_ref,
    parts_ref,
    hi_rest_ref,
    lo_rest_ref,
    tail_ref,
    sums_ref,
    sems,
    tail_sems,
):
    head, tile_cols = hi_head_ref.shape
    slabs, streams, slab = out_ref.shape
    rows, lanes = jac_ref.shape[0] // streams, jac_ref.shape[1]
    chunks = sems.shape[0]
    copies = []
    for n in range(chunks):
        here = pl.ds(n * head, head)
        copies.append(
            (
                pltpu.make_async_copy(hi_ref.at[here], hi_rest_ref.at[here], sems.at[n, 0]),
                pltpu.make_async_copy(lo_ref.at[here], lo_rest_ref.at[here], sems.at[n, 1]),
            )
        )
        for copy in copies[-1]:
            copy.start()
    tail = tail_ref.shape[0]
    first = cov_ref.shape[0] - tail
    last = []
    for n in range(tail // head):
        source, target = pl.ds(first + n * head, head), pl.ds(n * head, head)
        last.append(pltpu.make_async_copy(cov_ref.at[source], tail_ref.at[target], tail_sems.at[n]))
        last[-1].start()
    stacked_parts(jac_ref, 0, parts_ref.shape[1] // lanes, streams, rows, parts_ref)
    sums_ref[...] = five_products(parts_ref[:, 0:head], hi_head_ref[...], lo_head_ref[...], ((1,), (0,)))
    for n in range(chunks):
        for copy in copies[n]:
            copy.wait()
        here = slice(n * head, (n + 1) * head)
        sums_ref[...] += five_products(
            parts_ref[:, (n + 1) * head : (n + 2) * head], hi_rest_ref[here, :], lo_rest_ref[here, :], ((1,), (0,))
        )
    for n in range(tail // head):
        last[n].wait()
        hi, lo = split2(tail_ref[n * head : (n + 1) * head, :])
        parts = parts_ref[:, first + n * head : first + (n + 1) * head]
        sums_ref[...] += five_products(parts, hi, lo, ((1,), (0,)))
    for n in range(slabs):
        out_ref[n] = sums_ref[:, n * slab : (n + 1) * slab]


def col_partial(jac, streams, hi_head, lo_head, hi, lo, covariance, slab):
    rest, tile_cols = hi.shape
    head = hi_head.shape[0]
    tail = covariance.shape[0] - head - rest
    whole = pl.BlockSpec(memory_space=pltpu.VMEM)
    beyond = pl.BlockSpec(memory_space=pl.ANY)
    return pl.pallas_call(
        col_kernel,
        in_specs=[whole] * 3 + [beyond] * 3,
        out_specs=whole,
        out_shape=jax.ShapeDtypeStruct((tile_cols // slab, streams, slab), f32),
        scratch_shapes=[
            pltpu.VMEM((3 * streams, covariance.shape[0]), bf16),
            pltpu.VMEM((rest, tile_cols), bf16),
            pltpu.VMEM((rest, tile_cols), bf16),
            pltpu.VMEM((tail, tile_cols), f32),
            pltpu.VMEM((streams, tile_cols), f32),
            pltpu.SemaphoreType.DMA((rest // head, 2)),
            pltpu.SemaphoreType.DMA((tail // head,)),
        ],
        compiler_params=limit(20),
        name="col_cross",
    )(jac, in_vmem(hi_head), in_vmem(lo_head), in_hbm(hi), in_hbm(lo), in_hbm(covariance))


def packed(term):
    streams = term.shape[0]
    groups = LANES // streams
    height = streams // groups
    return jnp.concatenate([term[n * height : (n + 1) * height] for n in range(groups)], axis=1)


def unpacked(rows, streams):
    return jnp.concatenate(
        [rows[:, n * streams : (n + 1) * streams] for n in range(LANES // streams)], axis=0
    )


def slab_kernel(pieces_ref, jac_ref, _, own_ref, out_ref, error_ref, *, first):
    streams, slab = own_ref.shape
    rows, lanes = jac_ref.shape[0] // streams, jac_ref.shape[1]
    total = pieces_ref[0]
    for n in range(1, pieces_ref.shape[0]):
        total = total + pieces_ref[n]
    own_ref[...] = total
    term = jnp.zeros((streams, streams), f32)
    for i in range(slab // lanes):
        own = jac_ref[pl.ds(first + i, streams, stride=rows), :]
        here = total[:, i * lanes : (i + 1) * lanes]
        term = term + dot(own, here, ((1,), (1,)), highest)
        out_ref[i * streams : (i + 1) * streams, :] = here
    out_ref[slab // lanes * streams :, :] = packed(term)
    error_ref[...] = jac_ref[pl.ds(first + slab // lanes, streams, stride=rows), :]


def slab_sum(pieces, jac, after, first):
    _, streams, slab = pieces.shape
    return pl.pallas_call(
        functools.partial(slab_kernel, first=first),
        in_specs=[pl.BlockSpec(memory_space=pltpu.VMEM)] * 2 + [pl.BlockSpec(memory_space=pl.ANY)],
        out_shape=[
            jax.ShapeDtypeStruct((streams, slab), f32),
            jax.ShapeDtypeStruct((streams * (slab + streams) // LANES, LANES), f32),
            jax.ShapeDtypeStruct((streams, LANES), f32),
        ],
        compiler_params=limit(8),
        name="slab",
    )(pieces, jac, in_vmem(after))


def term_kernel(own_ref, cols_ref, out_ref):
    streams, slab = own_ref.shape
    _, lanes = out_ref.shape[1:]
    under = slab // lanes * streams
    term = cols_ref[0, under:, :]
    for n in range(1, cols_ref.shape[0]):
        term = term + cols_ref[n, under:, :]
    for n in range(out_ref.shape[0]):
        for i in range(slab // lanes):
            out_ref[n, i * streams : (i + 1) * streams, :] = own_ref[:, i * lanes : (i + 1) * lanes]
        out_ref[n, under:, :] = term


def with_terms(own, col_slabs, copies):
    return pl.pallas_call(
        term_kernel,
        out_shape=jax.ShapeDtypeStruct((copies,) + col_slabs.shape[1:], f32),
        compiler_params=limit(8),
        name="term",
    )(own, col_slabs)


def invert(innovation):
    streams = innovation.shape[0]
    row = lax.broadcasted_iota(jnp.int32, (streams, streams), 0)
    col = lax.broadcasted_iota(jnp.int32, (streams, streams), 1)
    identity = (row == col).astype(f32)
    innovation = innovation + forget * identity
    sums = jnp.sum(jnp.abs(innovation), axis=1, keepdims=True)
    bound = jnp.max(sums, axis=0, keepdims=True)
    power = identity - innovation / bound
    inverse = identity + power
    for repeat in range(NEWTON - 1):
        power = dot(power, power, ((1,), (0,)), highest)
        inverse = inverse + dot(inverse, power, ((1,), (0,)), highest)
    return inverse / bound


def head_kernel(cov_ref, _, head_ref, sem):
    copy = pltpu.make_async_copy(cov_ref.at[pl.ds(0, head_ref.shape[0])], head_ref, sem)
    copy.start()
    copy.wait()


def read_head(covariance, after):
    beyond = pl.BlockSpec(memory_space=pl.ANY)
    rows, cols = covariance.shape
    return pl.pallas_call(
        head_kernel,
        in_specs=[beyond, beyond],
        out_specs=pl.BlockSpec(memory_space=pltpu.VMEM),
        out_shape=pltpu.VMEM((rows // 4, cols), f32),
        scratch_shapes=[pltpu.SemaphoreType.DMA],
        compiler_params=limit(2),
        name="head",
    )(in_hbm(covariance), after)


def update_kernel(
    rows_ref, cols_ref, error_ref, weight_ref, head_ref, cov_ref, new_weight_ref, new_cov_ref, left_ref, right_ref, tile_ref, in_sems, out_sems
):
    slabs, _, lanes = rows_ref.shape
    streams = error_ref.shape[0]
    tile_rows = cov_ref.shape[0]
    slab = tile_rows // slabs
    under = slab // lanes * streams
    chunks = in_sems.shape[0]
    height = tile_rows // chunks
    held = head_ref.shape[0] // height
    reads = []
    for n in range(held, chunks):
        here = pl.ds(n * height, height)
        reads.append(pltpu.make_async_copy(cov_ref.at[here], tile_ref.at[here], in_sems.at[n]))
        reads[-1].start()
    term = rows_ref[0, under:, :]
    for n in range(1, slabs):
        term = term + rows_ref[n, under:, :]
    inverse = invert(unpacked(term, streams))
    errors = error_ref[:, 0:1]
    for n in range(cols_ref.shape[0]):
        for i in range(slab // lanes):
            hi, mid, lo = split3(cols_ref[n, i * streams : (i + 1) * streams, :])
            at = n * slab + i * lanes
            for m, part in enumerate((hi, mid, lo, hi, mid, hi)):
                right_ref[m * streams : (m + 1) * streams, at : at + lanes] = part
    cross = jnp.concatenate(
        [rows_ref[n, i : i + streams, :] for n in range(slabs) for i in range(0, under, streams)], axis=1
    )
    gain = dot(inverse, cross, ((0,), (0,)), highest)
    hi, mid, lo = split3(gain)
    for m, part in enumerate((hi, hi, hi, mid, mid, lo)):
        left_ref[m * streams : (m + 1) * streams, :] = part
    writes = []
    for n in range(chunks):
        update = dot(left_ref[:, n * height : (n + 1) * height], right_ref[...], ((0,), (0,)))
        here = pl.ds(n * height, height)
        if n >= held:
            reads[n - held].wait()
        before = head_ref if n < held else tile_ref
        tile_ref[here, :] = (before[here, :] - update) * (1.0 / forget)
        writes.append(pltpu.make_async_copy(tile_ref.at[here], new_cov_ref.at[here], out_sems.at[n]))
        writes[-1].start()
    col_at = lax.axis_index("col")
    own_at = (lax.axis_index("row") * slabs + col_at) * (slab // lanes)
    for n in range(slabs):

        @pl.when(col_at == n)
        def _():
            moved = jnp.sum(gain[:, n * slab : (n + 1) * slab] * errors, axis=0, keepdims=True)
            for i in range(slab // lanes):
                own = weight_ref[pl.ds(own_at + i, 1), :]
                new_weight_ref[i : i + 1, :] = own + moved[:, i * lanes : (i + 1) * lanes]

    for write in writes:
        write.wait()


def update(row_slabs, col_slabs, errors, layer_weight, head, covariance):
    streams = errors.shape[0]
    tile_rows, tile_cols = covariance.shape
    slab = tile_rows // row_slabs.shape[0]
    width = layer_weight.shape[1]
    whole = pl.BlockSpec(memory_space=pltpu.VMEM)
    beyond = pl.BlockSpec(memory_space=pl.ANY)
    return pl.pallas_call(
        update_kernel,
        in_specs=[whole] * 5 + [beyond],
        out_specs=[whole, beyond],
        out_shape=[
            jax.ShapeDtypeStruct((slab // width, width), f32),
            jax.ShapeDtypeStruct((tile_rows, tile_cols), f32),
        ],
        scratch_shapes=[
            pltpu.VMEM((6 * streams, tile_rows), bf16),
            pltpu.VMEM((6 * streams, tile_cols), bf16),
            pltpu.VMEM((tile_rows, tile_cols), f32),
            pltpu.SemaphoreType.DMA((8,)),
            pltpu.SemaphoreType.DMA((8,)),
        ],
        compiler_params=limit(20),
        name="update",
    )(row_slabs, col_slabs, errors, layer_weight, in_vmem(head), in_hbm(covariance))


def plain_steps(at, jac_all, errors, layer_weight, covariance, slab, cols_n):
    streams = jac_all.shape[0]
    hin, width = layer_weight.shape
    tile_rows, tile_cols = covariance.shape
    first = (at[0] * cols_n + at[1]) * slab
    jacobian = jac_all[:, 0:hin, :].reshape(streams, hin * width)
    jac_cols = lax.dynamic_slice_in_dim(jacobian, at[1] * tile_cols, tile_cols, 1)
    partial = dot(jac_cols, covariance, ((1,), (1,)), highest)
    cross_own = lax.psum_scatter(partial, "col", scatter_dimension=1, tiled=True)
    cross = lax.all_gather(cross_own, ("row", "col"), axis=1, tiled=True)
    inverse = invert(dot(jacobian, cross, ((1,), (1,)), highest))
    gain = dot(inverse, lax.dynamic_slice_in_dim(cross, at[0] * tile_rows, tile_rows, 1), ((0,), (0,)), highest)
    across = lax.dynamic_slice_in_dim(cross, at[1] * tile_cols, tile_cols, 1)
    new_cov = (covariance - dot(gain, across, ((0,), (0,)), highest)) / forget
    own_gain = lax.dynamic_slice_in_dim(gain, at[1] * slab, slab, 1)
    own_weight = lax.dynamic_slice_in_dim(layer_weight.reshape(-1), first, slab, 0)
    new_weight = own_weight + dot(errors, own_gain, ((0,), (0,)), highest)
    return new_weight, new_cov


def exchange(x, axes):
    return lax.all_to_all(x, axes, split_axis=0, concat_axis=0, tiled=True)


def on_device(
    atom_types,
    neighbor_ids,
    switching,
    environment,
    force_weights,
    targets,
    type_embed,
    layer_weight,
    out_weight,
    covariance,
):
    rows_n = lax.axis_size("row")
    cols_n = lax.axis_size("col")
    at = jnp.stack([lax.axis_index("row"), lax.axis_index("col")]).astype(jnp.int32)
    tile_rows, tile_cols = covariance.shape
    slab = tile_rows // cols_n
    hin, width = layer_weight.shape
    run_network = functools.partial(
        network,
        atom_types=atom_types,
        neighbor_ids=neighbor_ids,
        switching=switching,
        environment=environment,
        force_weights=force_weights,
        targets=targets,
        type_embed=type_embed,
        layer_weight=layer_weight,
        out_weight=out_weight,
    )
    streams = rows_n * cols_n * atom_types.shape[0]
    kernels = (
        atom_types.shape[0] == 1
        and width == LANES
        and slab % LANES == 0
        and tile_rows % (SUBLANES * LANES) == 0
        and tile_cols % (SUBLANES * LANES) == 0
        and rows_n * slab == tile_cols
        and LANES % streams == 0
        and streams * streams % (SUBLANES * LANES) == 0
    )
    if not kernels:
        payload = run_network([[(0, hin)]])
        jac_all = lax.all_gather(payload, ("row", "col"), axis=0, tiled=True)
        return plain_steps(at, jac_all[:, 0:hin], jac_all[:, hin, 0], layer_weight, covariance, slab, cols_n)
    row_size, slab_size = tile_rows // LANES, slab // LANES
    devices = [(r, c) for r in range(rows_n) for c in range(cols_n)]
    plan = [[(r * row_size, row_size), ((c * rows_n + r) * slab_size, slab_size)] for r, c in devices]
    payload = run_network(plan).reshape(streams, 1, -1)
    jac = exchange(payload, ("row", "col")).reshape(-1, width)
    hi, lo, hi_head, lo_head = stage(covariance, tile_rows // 4, tile_rows // 2)
    col_part = col_partial(jac, streams, hi_head, lo_head, hi, lo, covariance, slab)
    pieces = exchange(col_part, "row")
    head = read_head(covariance, col_part)
    col_own, with_term, errors = slab_sum(pieces, jac, head, row_size)
    to_row = [(r * cols_n + c, c * rows_n + r) for r, c in devices]
    row_own = lax.ppermute(col_own, ("row", "col"), to_row)
    col_slabs = lax.all_gather(with_term, "row", axis=0, tiled=False)
    row_slabs = exchange(with_terms(row_own, col_slabs, cols_n), "col")
    new_weight, new_cov = update(row_slabs, col_slabs, errors, layer_weight, head, covariance)
    return new_weight.reshape(-1), new_cov


def solution(mesh):
    in_specs = (
        P(("row", "col"), None),
        P(("row", "col"), None, None),
        P(("row", "col"), None, None),
        P(("row", "col"), None, None),
        P(("row", "col"), None),
        P(("row", "col")),
        P(),
        P(),
        P(),
        P("row", "col"),
    )
    out_specs = (P(("row", "col")), P("row", "col"))
    return jax.shard_map(
        on_device, mesh=mesh, in_specs=in_specs, out_specs=out_specs, check_vma=False
    )
```

```python
import functools
import math

import jax
import jax.numpy as jnp
from jax import lax
from jax.experimental import pallas as pl
from jax.experimental.pallas import tpu as pltpu
from jax.sharding import PartitionSpec as P

NEWTON = 4
LANES = 128
SUBLANES = 8


forget = 0.98
highest = lax.Precision.HIGHEST
f32 = jnp.float32
bf16 = jnp.bfloat16


def dot(left, right, contract, precision=None):
    return lax.dot_general(
        left, right, (contract, ((), ())), precision=precision, preferred_element_type=f32
    )


def split3(x):
    hi = x.astype(bf16)
    rest = x - hi.astype(f32)
    mid = rest.astype(bf16)
    lo = (rest - mid.astype(f32)).astype(bf16)
    return hi, mid, lo


def split2(x):
    hi = x.astype(bf16)
    return hi, (x - hi.astype(f32)).astype(bf16)


def limit(mib):
    return pltpu.CompilerParams(vmem_limit_bytes=mib << 20)


def five_products(parts, hi, lo, contract):
    streams = parts.shape[0] // 3
    by_hi = dot(parts, hi, contract)
    by_lo = dot(parts[0 : 2 * streams], lo, contract)
    return by_hi[0:streams] + (
        by_hi[streams : 2 * streams] + by_lo[0:streams] + (by_hi[2 * streams :] + by_lo[streams:])
    )


def network_kernel(
    types_ref,
    ids_ref,
    switch_ref,
    env_ref,
    force_ref,
    target_ref,
    embed_ref,
    weight_ref,
    out_weight_ref,
    payload_ref,
    mix_ref,
    *,
    plan,
):
    neighbours, atoms = ids_ref.shape
    n_types = embed_ref.shape[0]
    height = min(64, atoms)
    for start in range(0, atoms, height):
        atom_at = lax.broadcasted_iota(jnp.int32, (height, atoms), 0) + start
        total = jnp.zeros((height, atoms), f32)
        for k in range(neighbours):
            total = total + jnp.where(ids_ref[k : k + 1, :] == atom_at, switch_ref[k : k + 1, :], 0.0)
        mix_ref[start : start + height, :] = total
    mix = mix_ref[...]
    type_at = lax.broadcasted_iota(jnp.int32, (n_types, atoms), 0)
    onehot = (types_ref[...] == type_at).astype(f32)
    mixed = env_ref[...] + dot(embed_ref[...], onehot, ((0,), (0,)), highest)
    parts = jnp.concatenate(split3(mixed), axis=0)
    descriptor = five_products(parts, *split2(mix), ((1,), (0,))) * (1.0 / math.sqrt(neighbours))
    hidden = jnp.tanh(descriptor)
    hidden_hi, hidden_lo = split2(hidden)
    weight_hi, weight_lo = split2(weight_ref[...])
    left = jnp.concatenate([hidden_hi, hidden_hi, hidden_lo, hidden_lo], axis=0)
    right = jnp.concatenate([weight_hi, weight_lo, weight_hi, weight_lo], axis=0)
    activity = jnp.tanh(dot(left, right, ((0,), (0,))))
    out_weight = out_weight_ref[...]
    scale = 1.0 / math.sqrt(atoms)
    force = force_ref[...]
    weighted = dot(force, activity, ((1,), (0,)), highest)
    predicted = jnp.sum(weighted * out_weight, axis=1, keepdims=True) * scale
    slopes = out_weight * (1.0 - activity * activity)
    parts = jnp.concatenate(split3(hidden * force), axis=0)
    jacobian = five_products(parts, *split2(slopes), ((1,), (0,))) * scale
    error = target_ref[...] - predicted
    at = 0
    for pieces in plan:
        for start, size in pieces:
            payload_ref[at : at + size, :] = jacobian[start : start + size, :]
            at += size
        payload_ref[at : at + 1, :] = jnp.broadcast_to(error, (1, jacobian.shape[1]))
        at += 1


def network(
    plan, atom_types, neighbor_ids, switching, environment, force_weights, targets, type_embed, layer_weight, out_weight
):
    per_dev, neighbours, atoms = neighbor_ids.shape
    hin, width = layer_weight.shape
    rows = sum(1 + sum(size for _, size in pieces) for pieces in plan)

    def per_stream(*shape):
        return pl.BlockSpec((None,) + shape, lambda s: (s,) + (0,) * len(shape))

    def shared(shape):
        return pl.BlockSpec(shape, lambda s: (0,) * len(shape))

    return pl.pallas_call(
        functools.partial(network_kernel, plan=plan),
        grid=(per_dev,),
        in_specs=[
            per_stream(1, atoms),
            per_stream(neighbours, atoms),
            per_stream(neighbours, atoms),
            per_stream(hin, atoms),
            per_stream(1, atoms),
            per_stream(1, 1),
            shared(type_embed.shape),
            shared(layer_weight.shape),
            shared((1, width)),
        ],
        out_specs=per_stream(rows, width),
        out_shape=jax.ShapeDtypeStruct((per_dev, rows, width), f32),
        scratch_shapes=[pltpu.VMEM((atoms, atoms), f32)],
        name="network",
    )(
        atom_types.reshape(per_dev, 1, atoms),
        neighbor_ids,
        switching,
        environment.swapaxes(1, 2),
        force_weights.reshape(per_dev, 1, atoms),
        targets.reshape(per_dev, 1, 1),
        type_embed,
        layer_weight,
        out_weight.reshape(1, width),
    )


def in_hbm(x):
    return pltpu.with_memory_space_constraint(x, pltpu.HBM)


def in_vmem(x):
    return pltpu.with_memory_space_constraint(x, pltpu.VMEM)


def stage_kernel(cov_ref, hi_ref, lo_ref, hi_head_ref, lo_head_ref, *, head_steps):
    hi, lo = split2(cov_ref[...])
    hi_ref[...] = hi
    lo_ref[...] = lo

    @pl.when(pl.program_id(0) < head_steps)
    def _():
        hi_head_ref[...] = hi
        lo_head_ref[...] = lo


def stage(covariance, head, tail):
    rows, cols = covariance.shape
    height = min(rows // 8, head)
    head_steps = head // height
    block = pl.BlockSpec((height, cols), lambda n: (n, 0))
    rest_block = pl.BlockSpec((height, cols), lambda n: (jnp.maximum(n - head_steps, 0), 0))
    head_block = pl.BlockSpec((height, cols), lambda n: (jnp.minimum(n, head_steps - 1), 0))
    return pl.pallas_call(
        functools.partial(stage_kernel, head_steps=head_steps),
        grid=((rows - tail) // height,),
        in_specs=[block],
        out_specs=[rest_block, rest_block, head_block, head_block],
        out_shape=[pltpu.HBM((rows - head - tail, cols), bf16)] * 2 + [pltpu.VMEM((head, cols), bf16)] * 2,
        compiler_params=limit(12),
        name="stage",
    )(in_hbm(covariance))


def stacked_parts(flat, first, count, streams, stride, into_ref):
    lanes = flat.shape[1]
    for i in range(count):
        parts = split3(flat[pl.ds(first + i, streams, stride=stride), :])
        for n, part in enumerate(parts):
            into_ref[n * streams : (n + 1) * streams, i * lanes : (i + 1) * lanes] = part


def col_kernel(
    jac_ref,
    hi_head_ref,
    lo_head_ref,
    hi_ref,
    lo_ref,
    cov_ref,
    out_ref,
    parts_ref,
    hi_rest_ref,
    lo_rest_ref,
    tail_ref,
    sums_ref,
    sems,
    tail_sems,
):
    head, tile_cols = hi_head_ref.shape
    slabs, streams, slab = out_ref.shape
    rows, lanes = jac_ref.shape[0] // streams, jac_ref.shape[1]
    chunks = sems.shape[0]
    copies = []
    for n in range(chunks):
        here = pl.ds(n * head, head)
        copies.append(
            (
                pltpu.make_async_copy(hi_ref.at[here], hi_rest_ref.at[here], sems.at[n, 0]),
                pltpu.make_async_copy(lo_ref.at[here], lo_rest_ref.at[here], sems.at[n, 1]),
            )
        )
        for copy in copies[-1]:
            copy.start()
    tail = tail_ref.shape[0]
    first = cov_ref.shape[0] - tail
    last = []
    for n in range(tail // head):
        source, target = pl.ds(first + n * head, head), pl.ds(n * head, head)
        last.append(pltpu.make_async_copy(cov_ref.at[source], tail_ref.at[target], tail_sems.at[n]))
        last[-1].start()
    stacked_parts(jac_ref, 0, parts_ref.shape[1] // lanes, streams, rows, parts_ref)
    sums_ref[...] = five_products(parts_ref[:, 0:head], hi_head_ref[...], lo_head_ref[...], ((1,), (0,)))
    for n in range(chunks):
        for copy in copies[n]:
            copy.wait()
        here = slice(n * head, (n + 1) * head)
        sums_ref[...] += five_products(
            parts_ref[:, (n + 1) * head : (n + 2) * head], hi_rest_ref[here, :], lo_rest_ref[here, :], ((1,), (0,))
        )
    for n in range(tail // head):
        last[n].wait()
        hi, lo = split2(tail_ref[n * head : (n + 1) * head, :])
        parts = parts_ref[:, first + n * head : first + (n + 1) * head]
        sums_ref[...] += five_products(parts, hi, lo, ((1,), (0,)))
    for n in range(slabs):
        out_ref[n] = sums_ref[:, n * slab : (n + 1) * slab]


def col_partial(jac, streams, hi_head, lo_head, hi, lo, covariance, slab):
    rest, tile_cols = hi.shape
    head = hi_head.shape[0]
    tail = covariance.shape[0] - head - rest
    whole = pl.BlockSpec(memory_space=pltpu.VMEM)
    beyond = pl.BlockSpec(memory_space=pl.ANY)
    return pl.pallas_call(
        col_kernel,
        in_specs=[whole] * 3 + [beyond] * 3,
        out_specs=whole,
        out_shape=jax.ShapeDtypeStruct((tile_cols // slab, streams, slab), f32),
        scratch_shapes=[
            pltpu.VMEM((3 * streams, covariance.shape[0]), bf16),
            pltpu.VMEM((rest, tile_cols), bf16),
            pltpu.VMEM((rest, tile_cols), bf16),
            pltpu.VMEM((tail, tile_cols), f32),
            pltpu.VMEM((streams, tile_cols), f32),
            pltpu.SemaphoreType.DMA((rest // head, 2)),
            pltpu.SemaphoreType.DMA((tail // head,)),
        ],
        compiler_params=limit(20),
        name="col_cross",
    )(jac, in_vmem(hi_head), in_vmem(lo_head), in_hbm(hi), in_hbm(lo), in_hbm(covariance))


def packed(term):
    streams = term.shape[0]
    groups = LANES // streams
    height = streams // groups
    return jnp.concatenate([term[n * height : (n + 1) * height] for n in range(groups)], axis=1)


def unpacked(rows, streams):
    return jnp.concatenate(
        [rows[:, n * streams : (n + 1) * streams] for n in range(LANES // streams)], axis=0
    )


def slab_kernel(pieces_ref, jac_ref, own_ref, out_ref, error_ref, *, first):
    streams, slab = own_ref.shape
    rows, lanes = jac_ref.shape[0] // streams, jac_ref.shape[1]
    total = pieces_ref[0]
    for n in range(1, pieces_ref.shape[0]):
        total = total + pieces_ref[n]
    own_ref[...] = total
    term = jnp.zeros((streams, streams), f32)
    for i in range(slab // lanes):
        own = jac_ref[pl.ds(first + i, streams, stride=rows), :]
        here = total[:, i * lanes : (i + 1) * lanes]
        term = term + dot(own, here, ((1,), (1,)), highest)
        out_ref[i * streams : (i + 1) * streams, :] = here
    out_ref[slab // lanes * streams :, :] = packed(term)
    error_ref[...] = jac_ref[pl.ds(first + slab // lanes, streams, stride=rows), :]


def slab_sum(pieces, jac, first):
    _, streams, slab = pieces.shape
    return pl.pallas_call(
        functools.partial(slab_kernel, first=first),
        out_shape=[
            jax.ShapeDtypeStruct((streams, slab), f32),
            jax.ShapeDtypeStruct((streams * (slab + streams) // LANES, LANES), f32),
            jax.ShapeDtypeStruct((streams, LANES), f32),
        ],
        compiler_params=limit(8),
        name="slab",
    )(pieces, jac)


def term_kernel(own_ref, cols_ref, out_ref):
    streams, slab = own_ref.shape
    _, lanes = out_ref.shape[1:]
    under = slab // lanes * streams
    term = cols_ref[0, under:, :]
    for n in range(1, cols_ref.shape[0]):
        term = term + cols_ref[n, under:, :]
    for n in range(out_ref.shape[0]):
        for i in range(slab // lanes):
            out_ref[n, i * streams : (i + 1) * streams, :] = own_ref[:, i * lanes : (i + 1) * lanes]
        out_ref[n, under:, :] = term


def with_terms(own, col_slabs, copies):
    return pl.pallas_call(
        term_kernel,
        out_shape=jax.ShapeDtypeStruct((copies,) + col_slabs.shape[1:], f32),
        compiler_params=limit(8),
        name="term",
    )(own, col_slabs)


def invert(innovation):
    streams = innovation.shape[0]
    row = lax.broadcasted_iota(jnp.int32, (streams, streams), 0)
    col = lax.broadcasted_iota(jnp.int32, (streams, streams), 1)
    identity = (row == col).astype(f32)
    innovation = innovation + forget * identity
    sums = jnp.sum(jnp.abs(innovation), axis=1, keepdims=True)
    bound = jnp.max(sums, axis=0, keepdims=True)
    power = identity - innovation / bound
    inverse = identity + power
    for repeat in range(NEWTON - 1):
        power = dot(power, power, ((1,), (0,)), highest)
        inverse = inverse + dot(inverse, power, ((1,), (0,)), highest)
    return inverse / bound


def head_kernel(cov_ref, _, head_ref, sem):
    copy = pltpu.make_async_copy(cov_ref.at[pl.ds(0, head_ref.shape[0])], head_ref, sem)
    copy.start()
    copy.wait()


def read_head(covariance, after):
    beyond = pl.BlockSpec(memory_space=pl.ANY)
    rows, cols = covariance.shape
    return pl.pallas_call(
        head_kernel,
        in_specs=[beyond, beyond],
        out_specs=pl.BlockSpec(memory_space=pltpu.VMEM),
        out_shape=pltpu.VMEM((rows // 4, cols), f32),
        scratch_shapes=[pltpu.SemaphoreType.DMA],
        compiler_params=limit(2),
        name="head",
    )(in_hbm(covariance), after)


def update_kernel(
    rows_ref, cols_ref, error_ref, weight_ref, head_ref, cov_ref, new_weight_ref, new_cov_ref, left_ref, right_ref, tile_ref, in_sems, out_sems
):
    slabs, _, lanes = rows_ref.shape
    streams = error_ref.shape[0]
    tile_rows = cov_ref.shape[0]
    slab = tile_rows // slabs
    under = slab // lanes * streams
    chunks = in_sems.shape[0]
    height = tile_rows // chunks
    held = head_ref.shape[0] // height
    reads = []
    for n in range(held, chunks):
        here = pl.ds(n * height, height)
        reads.append(pltpu.make_async_copy(cov_ref.at[here], tile_ref.at[here], in_sems.at[n]))
        reads[-1].start()
    term = rows_ref[0, under:, :]
    for n in range(1, slabs):
        term = term + rows_ref[n, under:, :]
    inverse = invert(unpacked(term, streams))
    errors = error_ref[:, 0:1]
    for n in range(cols_ref.shape[0]):
        for i in range(slab // lanes):
            hi, mid, lo = split3(cols_ref[n, i * streams : (i + 1) * streams, :])
            at = n * slab + i * lanes
            for m, part in enumerate((hi, mid, lo, hi, mid, hi)):
                right_ref[m * streams : (m + 1) * streams, at : at + lanes] = part
    cross = jnp.concatenate(
        [rows_ref[n, i : i + streams, :] for n in range(slabs) for i in range(0, under, streams)], axis=1
    )
    gain = dot(inverse, cross, ((0,), (0,)), highest)
    hi, mid, lo = split3(gain)
    for m, part in enumerate((hi, hi, hi, mid, mid, lo)):
        left_ref[m * streams : (m + 1) * streams, :] = part
    writes = []
    for n in range(chunks):
        update = dot(left_ref[:, n * height : (n + 1) * height], right_ref[...], ((0,), (0,)))
        here = pl.ds(n * height, height)
        if n >= held:
            reads[n - held].wait()
        before = head_ref if n < held else tile_ref
        tile_ref[here, :] = (before[here, :] - update) * (1.0 / forget)
        writes.append(pltpu.make_async_copy(tile_ref.at[here], new_cov_ref.at[here], out_sems.at[n]))
        writes[-1].start()
    col_at = lax.axis_index("col")
    own_at = (lax.axis_index("row") * slabs + col_at) * (slab // lanes)
    for n in range(slabs):

        @pl.when(col_at == n)
        def _():
            moved = jnp.sum(gain[:, n * slab : (n + 1) * slab] * errors, axis=0, keepdims=True)
            for i in range(slab // lanes):
                own = weight_ref[pl.ds(own_at + i, 1), :]
                new_weight_ref[i : i + 1, :] = own + moved[:, i * lanes : (i + 1) * lanes]

    for write in writes:
        write.wait()


def update(row_slabs, col_slabs, errors, layer_weight, head, covariance):
    streams = errors.shape[0]
    tile_rows, tile_cols = covariance.shape
    slab = tile_rows // row_slabs.shape[0]
    width = layer_weight.shape[1]
    whole = pl.BlockSpec(memory_space=pltpu.VMEM)
    beyond = pl.BlockSpec(memory_space=pl.ANY)
    return pl.pallas_call(
        update_kernel,
        in_specs=[whole] * 5 + [beyond],
        out_specs=[whole, beyond],
        out_shape=[
            jax.ShapeDtypeStruct((slab // width, width), f32),
            jax.ShapeDtypeStruct((tile_rows, tile_cols), f32),
        ],
        scratch_shapes=[
            pltpu.VMEM((6 * streams, tile_rows), bf16),
            pltpu.VMEM((6 * streams, tile_cols), bf16),
            pltpu.VMEM((tile_rows, tile_cols), f32),
            pltpu.SemaphoreType.DMA((8,)),
            pltpu.SemaphoreType.DMA((8,)),
        ],
        compiler_params=limit(20),
        name="update",
    )(row_slabs, col_slabs, errors, layer_weight, in_vmem(head), in_hbm(covariance))


def plain_steps(at, jac_all, errors, layer_weight, covariance, slab, cols_n):
    streams = jac_all.shape[0]
    hin, width = layer_weight.shape
    tile_rows, tile_cols = covariance.shape
    first = (at[0] * cols_n + at[1]) * slab
    jacobian = jac_all[:, 0:hin, :].reshape(streams, hin * width)
    jac_cols = lax.dynamic_slice_in_dim(jacobian, at[1] * tile_cols, tile_cols, 1)
    partial = dot(jac_cols, covariance, ((1,), (1,)), highest)
    cross_own = lax.psum_scatter(partial, "col", scatter_dimension=1, tiled=True)
    cross = lax.all_gather(cross_own, ("row", "col"), axis=1, tiled=True)
    inverse = invert(dot(jacobian, cross, ((1,), (1,)), highest))
    gain = dot(inverse, lax.dynamic_slice_in_dim(cross, at[0] * tile_rows, tile_rows, 1), ((0,), (0,)), highest)
    across = lax.dynamic_slice_in_dim(cross, at[1] * tile_cols, tile_cols, 1)
    new_cov = (covariance - dot(gain, across, ((0,), (0,)), highest)) / forget
    own_gain = lax.dynamic_slice_in_dim(gain, at[1] * slab, slab, 1)
    own_weight = lax.dynamic_slice_in_dim(layer_weight.reshape(-1), first, slab, 0)
    new_weight = own_weight + dot(errors, own_gain, ((0,), (0,)), highest)
    return new_weight, new_cov


def exchange(x, axes):
    return lax.all_to_all(x, axes, split_axis=0, concat_axis=0, tiled=True)


def on_device(
    atom_types,
    neighbor_ids,
    switching,
    environment,
    force_weights,
    targets,
    type_embed,
    layer_weight,
    out_weight,
    covariance,
):
    rows_n = lax.axis_size("row")
    cols_n = lax.axis_size("col")
    at = jnp.stack([lax.axis_index("row"), lax.axis_index("col")]).astype(jnp.int32)
    tile_rows, tile_cols = covariance.shape
    slab = tile_rows // cols_n
    hin, width = layer_weight.shape
    run_network = functools.partial(
        network,
        atom_types=atom_types,
        neighbor_ids=neighbor_ids,
        switching=switching,
        environment=environment,
        force_weights=force_weights,
        targets=targets,
        type_embed=type_embed,
        layer_weight=layer_weight,
        out_weight=out_weight,
    )
    streams = rows_n * cols_n * atom_types.shape[0]
    kernels = (
        atom_types.shape[0] == 1
        and width == LANES
        and slab % LANES == 0
        and tile_rows % (SUBLANES * LANES) == 0
        and tile_cols % (SUBLANES * LANES) == 0
        and rows_n * slab == tile_cols
        and LANES % streams == 0
        and streams * streams % (SUBLANES * LANES) == 0
    )
    if not kernels:
        payload = run_network([[(0, hin)]])
        jac_all = lax.all_gather(payload, ("row", "col"), axis=0, tiled=True)
        return plain_steps(at, jac_all[:, 0:hin], jac_all[:, hin, 0], layer_weight, covariance, slab, cols_n)
    row_size, slab_size = tile_rows // LANES, slab // LANES
    devices = [(r, c) for r in range(rows_n) for c in range(cols_n)]
    plan = [[(r * row_size, row_size), ((c * rows_n + r) * slab_size, slab_size)] for r, c in devices]
    payload = run_network(plan).reshape(streams, 1, -1)
    jac = exchange(payload, ("row", "col")).reshape(-1, width)
    hi, lo, hi_head, lo_head = stage(covariance, tile_rows // 4, tile_rows // 2)
    col_part = col_partial(jac, streams, hi_head, lo_head, hi, lo, covariance, slab)
    pieces = exchange(col_part, "row")
    head = read_head(covariance, col_part)
    col_own, with_term, errors = slab_sum(pieces, jac, row_size)
    to_row = [(r * cols_n + c, c * rows_n + r) for r, c in devices]
    row_own = lax.ppermute(col_own, ("row", "col"), to_row)
    col_slabs = lax.all_gather(with_term, "row", axis=0, tiled=False)
    row_slabs = exchange(with_terms(row_own, col_slabs, cols_n), "col")
    new_weight, new_cov = update(row_slabs, col_slabs, errors, layer_weight, head, covariance)
    return new_weight.reshape(-1), new_cov


def solution(mesh):
    in_specs = (
        P(("row", "col"), None),
        P(("row", "col"), None, None),
        P(("row", "col"), None, None),
        P(("row", "col"), None, None),
        P(("row", "col"), None),
        P(("row", "col")),
        P(),
        P(),
        P(),
        P("row", "col"),
    )
    out_specs = (P(("row", "col")), P("row", "col"))
    return jax.shard_map(
        on_device, mesh=mesh, in_specs=in_specs, out_specs=out_specs, check_vma=False
    )
```
